32 devices in a mesh: ca: 16 (over z, y, x), tp: 2 (over core).
Axes of the slice: x: 2, y: 2, z: 4, core: 2. Of those that a mesh axis runs over, the one named last changes fastest.
Arguments:
- tokens: bfloat16 [8192, 4096], P('ca'), may hold values from -7 to 7
- lengths: int32 [8], replicated, may hold values from 1 to 1536, 8192 in all
- w_query: bfloat16 [4096, 4096], P('ca', 'tp'), may hold values from -0.09375 to 0.09375
- w_key: bfloat16 [4096, 1024], P('ca', 'tp'), may hold values from -0.09375 to 0.09375
- w_value: bfloat16 [4096, 1024], P('ca', 'tp'), may hold values from -0.09375 to 0.09375
Outputs:
- attended: bfloat16 [8192, 4096], P('ca', 'tp')
The draws below stay inside these ranges and needn't reach their ends.
Inputs may be any that keep to these rules, and one draw needn't show every extreme that they name: `lengths`: the 8 documents lie end to end in this order and fill all 8192 tokens; the longest has exactly 1536 tokens.
All inputs are finite; a program needn't handle non-finite values.
Results may differ from the reference program's by a relative error of at most 0.007.
Values may be sent and summed in bfloat16 or wider, within the bound.
No kernel may reach another device: no remote copies, remote signals or barrier semaphores. Data moves between devices by JAX's collectives and lax.ppermute only.
A program may use at most 64 MiB of HBM per device.

```python
import math
import jax
import jax.numpy as jnp
import numpy as np
from jax import lax

D = 4096
HEADS = 32
KV_HEADS = 8
HEAD_DIM = 128
TOK_DEV = 512
REACH = 3
TOKENS = 8192
MAX_DOC = 1536
DOCS = 8
N_CA = 16


def levels(rng, extent, pieces, least, largest):
    level = 1.0
    for position, parts in pieces:
        heights = jax.random.uniform(jax.random.fold_in(jax.random.fold_in(rng, 6), position), (parts,), jnp.float32, least / len(pieces), largest / len(pieces))
        level = level * jnp.repeat(jnp.exp(heights), extent[position] // parts).reshape((-1,) + (1,) * (len(extent) - 1 - position))
    return level


def length_profile(amount, total, limit, slope):
    portions = [(1 << 20) // math.isqrt(rank ** slope) + 1 for rank in range(2, amount + 1)]
    rest, given = total - limit - (amount - 1), [1] * (amount - 1)
    while rest > 0:
        movable = [i for i in range(amount - 1) if given[i] < limit]
        whole, remaining = sum([portions[i] for i in movable]), rest
        for i in movable:
            more = min(limit - given[i], max(1, remaining * portions[i] // whole), rest)
            given[i] = given[i] + more
            rest = rest - more
    return np.array([limit] + given)


def ragged_sizes(key, number_of, total, limit, slope):
    if number_of == 2:
        one = jax.random.randint(key, (), max(1, total - limit), min(limit, total - 1) + 1)
        return jnp.stack([one, total - one])
    sizes = jnp.asarray(length_profile(number_of, total, limit, slope), jnp.int32)
    couples = (number_of - 1) // 2
    donor, sink = sizes[1:1 + 2 * couples:2], sizes[2:2 + 2 * couples:2]
    room = jnp.minimum(donor - 1, limit - sink)
    passed = jax.random.randint(jax.random.fold_in(key, 1), (couples,), 0, 1 << 20) % (room + 1)
    sizes = sizes.at[1:1 + 2 * couples:2].set(donor - passed).at[2:2 + 2 * couples:2].set(sink + passed)
    return sizes[jax.random.permutation(jax.random.fold_in(key, 2), number_of)]


def centred(key, shape, deviation, limit, shards=(), held_as=jnp.bfloat16):
    entries = jax.random.normal(key, shape, jnp.float32) * deviation
    if len(shards) > 0:
        entries = levels(key, shape, shards, -0.22, 0.18) * entries
    return jnp.clip(entries, min=-limit, max=limit).astype(held_as)


def setup_inputs(seed: int = 0) -> dict:
    key_list = jax.random.split(jax.random.key(seed), 6)
    tokens = centred(key_list[0], (TOKENS, D), 1.2, 7.0, ((0, 16),))
    lengths = ragged_sizes(key_list[1], DOCS, TOKENS, MAX_DOC, 2).astype(jnp.int32)
    w_query = centred(key_list[2], (D, HEADS * HEAD_DIM), D ** -0.5, 0.09375, ((0, 16), (1, 2)))
    w_key = centred(key_list[3], (D, KV_HEADS * HEAD_DIM), D ** -0.5, 0.09375, ((0, 16), (1, 2)))
    w_value = centred(key_list[4], (D, KV_HEADS * HEAD_DIM), D ** -0.5, 0.09375, ((0, 16), (1, 2)))
    return {"tokens": tokens, "lengths": lengths, "w_query": w_query, "w_key": w_key, "w_value": w_value}


rope_theta = 500000.0
logit_cap = 5.0

def doc_starts(lengths, positions):
    doc_ends = jnp.cumsum(lengths).astype(jnp.int32)
    before = doc_ends[None, :] <= positions[:, None]
    return lax.optimization_barrier(jnp.max(jnp.where(before, doc_ends[None, :], jnp.zeros_like(doc_ends)[None, :]), axis=1)).astype(jnp.int32)

def rotate(values, offsets):
    half_dim = values.shape[-1] // 2
    frequency = rope_theta ** (-(jnp.arange(half_dim, dtype=jnp.float32) * 2.0) / values.shape[-1])
    angles = offsets.astype(jnp.float32)[:, None] * frequency[None, :]
    cosine = jnp.cos(angles)[:, None, :]
    sine_part = jnp.sin(angles)[:, None, :]
    first_half = values[..., :half_dim]
    second_half = values[..., half_dim:]
    return jnp.concatenate([first_half * cosine - second_half * sine_part, second_half * cosine + first_half * sine_part], axis=-1)

def reference(tokens, lengths, w_query, w_key, w_value):
    token_count = tokens.shape[0]
    row_ids = jnp.arange(token_count, dtype=jnp.int32)
    starts = doc_starts(lengths, row_ids)
    offsets = row_ids - starts
    query = jnp.dot(tokens, w_query, preferred_element_type=jnp.float32).reshape(token_count, HEADS, HEAD_DIM)
    query = rotate(query, offsets).astype(jnp.bfloat16)
    key_all = jnp.dot(tokens, w_key, preferred_element_type=jnp.float32).reshape(token_count, KV_HEADS, HEAD_DIM)
    key_all = rotate(key_all, offsets).astype(jnp.bfloat16)
    value_all = jnp.dot(tokens, w_value, preferred_element_type=jnp.float32).astype(jnp.bfloat16)
    value_all = value_all.reshape(token_count, KV_HEADS, HEAD_DIM)
    margin = REACH * TOK_DEV
    window = (REACH + 1) * TOK_DEV
    key_pad = jnp.concatenate([jnp.zeros((margin, KV_HEADS, HEAD_DIM), jnp.bfloat16), key_all], axis=0)
    value_pad = jnp.concatenate([jnp.zeros((margin, KV_HEADS, HEAD_DIM), jnp.bfloat16), value_all], axis=0)
    group_size = HEADS // KV_HEADS

    def one_block(block_index):
        first_row = (block_index * TOK_DEV).astype(jnp.int32)
        q_block = lax.dynamic_slice_in_dim(query, first_row, TOK_DEV, 0).astype(jnp.float32)
        q_block = q_block.reshape(TOK_DEV, KV_HEADS, group_size, HEAD_DIM)
        k_block = lax.dynamic_slice_in_dim(key_pad, first_row, window, 0).astype(jnp.float32)
        v_block = lax.dynamic_slice_in_dim(value_pad, first_row, window, 0).astype(jnp.float32)
        q_rows = first_row + jnp.arange(TOK_DEV, dtype=jnp.int32)
        k_rows = first_row - margin + jnp.arange(window, dtype=jnp.int32)
        q_starts = lax.dynamic_slice_in_dim(starts, first_row, TOK_DEV, 0)
        raw = jnp.einsum('tkgd,skd->kgts', q_block, k_block)
        scores = logit_cap * jnp.tanh(raw / (math.sqrt(HEAD_DIM) * logit_cap))
        allowed = (k_rows[None, :] <= q_rows[:, None]) & (k_rows[None, :] >= q_starts[:, None])
        weights = jnp.where(allowed[None, None], jnp.exp(scores), jnp.zeros_like(scores))
        totals = lax.optimization_barrier(jnp.sum(weights, axis=-1))
        rounded = lax.optimization_barrier(weights.astype(jnp.bfloat16)).astype(jnp.float32)
        mixed_out = jnp.einsum('kgts,skd->kgtd', rounded, v_block) / totals[..., None]
        mixed_out = jnp.transpose(mixed_out, (2, 0, 1, 3)).reshape(TOK_DEV, HEADS * HEAD_DIM)
        return mixed_out.astype(jnp.bfloat16)
    blocks = lax.map(one_block, jnp.arange(N_CA, dtype=jnp.int32))
    return blocks.reshape(token_count, HEADS * HEAD_DIM)
```

```python
import functools
import math

import jax
import jax.numpy as jnp
from jax import lax
from jax.experimental import pallas as pl
from jax.experimental.pallas import tpu as pltpu
from jax.sharding import PartitionSpec as P

HEADS = 32
KV_HEADS = 8
HEAD_DIM = 128
REACH = 3
ROPE_THETA = 500000.0
LOGIT_CAP = 5.0
TILE = 256
VMEM_BYTES = 48 * 1024 * 1024


def doc_starts(lengths, positions):
    doc_ends = jnp.cumsum(lengths).astype(jnp.int32)
    before = doc_ends[None, :] <= positions[:, None]
    return jnp.max(jnp.where(before, doc_ends[None, :], 0), axis=1).astype(jnp.int32)


def rope_tables(offsets):
    half_dim = HEAD_DIM // 2
    frequency = ROPE_THETA ** (-(jnp.arange(half_dim, dtype=jnp.float32) * 2.0) / HEAD_DIM)
    angles = offsets.astype(jnp.float32)[:, None] * frequency[None, :]
    cosine, sine = jnp.cos(angles), jnp.sin(angles)
    return jnp.concatenate([cosine, cosine], axis=1), jnp.concatenate([-sine, sine], axis=1)


def rotated(values, cosine, sine):
    return values * cosine + pltpu.roll(values, HEAD_DIM // 2, 1) * sine


def project_kernel(rope_heads, group, slice_rows, place, x_ref, own_ref, rest_ref, cos_ref, sin_ref, out_ref, w_ref):
    @pl.when(pl.program_id(0) == 0)
    def _():
        lines = own_ref.shape[0] // slice_rows
        mine = place[0]
        for line in range(lines):
            at = pl.multiple_of((line * group + mine) * slice_rows, slice_rows)
            w_ref[pl.ds(at, slice_rows), :] = own_ref[line * slice_rows : (line + 1) * slice_rows, :]
            for step in range(1, group):
                at = pl.multiple_of((line * group + (mine ^ step)) * slice_rows, slice_rows)
                first = (line * (group - 1) + step - 1) * slice_rows
                w_ref[pl.ds(at, slice_rows), :] = rest_ref[first : first + slice_rows, :]

    total = jnp.dot(x_ref[...], w_ref[...], preferred_element_type=jnp.float32)
    cosine, sine = cos_ref[...], sin_ref[...]
    for head in range(out_ref.shape[1] // HEAD_DIM):
        columns = slice(head * HEAD_DIM, (head + 1) * HEAD_DIM)
        part = total[:, columns]
        if head < rope_heads:
            part = rotated(part, cosine, sine)
        out_ref[:, columns] = part.astype(out_ref.dtype)


def project(place, tokens, own, rest, column_block, width, cosine, sine, rope_heads, group, slice_rows):
    rows, depth = tokens.shape
    tile = min(512, rows)
    if rest is None:
        rest = jnp.zeros((16, width), own.dtype)
    kernel = functools.partial(project_kernel, rope_heads, group, slice_rows)
    return pl.pallas_call(
        kernel,
        out_shape=jax.ShapeDtypeStruct((rows, width), jnp.bfloat16),
        grid_spec=pltpu.PrefetchScalarGridSpec(
            num_scalar_prefetch=1,
            grid=(rows // tile,),
            in_specs=[
                pl.BlockSpec((tile, depth), lambda i, s: (i, 0)),
                pl.BlockSpec((own.shape[0], width), lambda i, s: (0, column_block)),
                pl.BlockSpec(rest.shape, lambda i, s: (0, 0)),
                pl.BlockSpec((tile, HEAD_DIM), lambda i, s: (i, 0)),
                pl.BlockSpec((tile, HEAD_DIM), lambda i, s: (i, 0)),
            ],
            out_specs=pl.BlockSpec((tile, width), lambda i, s: (i, 0)),
            scratch_shapes=[pltpu.VMEM((depth, width), own.dtype)],
        ),
        compiler_params=pltpu.CompilerParams(vmem_limit_bytes=VMEM_BYTES),
        cost_estimate=pl.CostEstimate(
            flops=2 * rows * depth * width, bytes_accessed=2 * depth * (rows + width), transcendentals=0
        ),
    )(place, tokens, own, rest, cosine, sine)


def attend_kernel(kv_heads, share, halo_rows, bounds, q_ref, start_ref, halo_ref, kv_ref, out_ref, kv_all, sums, totals):
    tile_index = pl.program_id(0)

    @pl.when(tile_index == 0)
    def _():
        kv_all[:halo_rows, :] = halo_ref[...]
        kv_all[halo_rows:, :] = kv_ref[...]

    tile = q_ref.shape[0]
    place = bounds[0, tile_index]
    first_start = bounds[1, tile_index]
    last_start = bounds[2, tile_index]
    q_first = halo_rows + place
    first_block = first_start // TILE
    last_block = (q_first + tile - 1) // TILE
    sums[...] = jnp.zeros_like(sums)
    totals[...] = jnp.zeros_like(totals)
    inner = 1.0 / (math.sqrt(HEAD_DIM) * LOGIT_CAP)
    outer = LOGIT_CAP * math.log2(math.e)

    def block_step(block, masked):
        rows = pl.ds(pl.multiple_of(block * TILE, TILE), TILE)
        if masked:
            k_ids = block * TILE + lax.broadcasted_iota(jnp.int32, (tile, TILE), 1)
            q_ids = q_first + lax.broadcasted_iota(jnp.int32, (tile, TILE), 0)
            allowed = (k_ids <= q_ids) & (k_ids >= start_ref[...])
        for kv_head in range(kv_heads):
            keys = kv_all[rows, kv_head * HEAD_DIM : (kv_head + 1) * HEAD_DIM]
            at = (kv_heads + kv_head) * HEAD_DIM
            values = kv_all[rows, at : at + HEAD_DIM]
            for member in range(share):
                head = kv_head * share + member
                query = q_ref[:, head * HEAD_DIM : (head + 1) * HEAD_DIM]
                raw = lax.dot_general(query, keys, (((1,), (1,)), ((), ())), preferred_element_type=jnp.float32)
                weights = jnp.exp2(outer * jnp.tanh(raw * inner))
                if masked:
                    weights = jnp.where(allowed, weights, 0.0)
                partial = weights[:, :HEAD_DIM]
                for part in range(1, TILE // HEAD_DIM):
                    partial = partial + weights[:, part * HEAD_DIM : (part + 1) * HEAD_DIM]
                totals[head] += partial
                sums[head] += jnp.dot(weights.astype(jnp.bfloat16), values, preferred_element_type=jnp.float32)

    def either(block, carry):
        begin = block * TILE
        whole = (begin >= last_start) & (begin + TILE - 1 <= q_first)

        @pl.when(whole)
        def _():
            block_step(block, False)

        @pl.when(jnp.logical_not(whole))
        def _():
            block_step(block, True)

        return carry

    lax.fori_loop(first_block, last_block + 1, either, 0)
    for head in range(kv_heads * share):
        denominator = jnp.sum(totals[head], axis=1, keepdims=True)
        out_ref[:, head * HEAD_DIM : (head + 1) * HEAD_DIM] = (sums[head] / denominator).astype(out_ref.dtype)


def attend(chunk, chunk_rows, query, starts, halo, kv, kv_heads):
    width = query.shape[1]
    heads = width // HEAD_DIM
    halo_rows = halo.shape[0]
    tiles = chunk_rows // TILE
    places = chunk * chunk_rows + jnp.arange(tiles, dtype=jnp.int32) * TILE
    bounds = jnp.stack([places, starts[places], starts[places + TILE - 1]])
    kernel = functools.partial(attend_kernel, kv_heads, heads // kv_heads, halo_rows)
    return pl.pallas_call(
        kernel,
        out_shape=jax.ShapeDtypeStruct((chunk_rows, width), jnp.bfloat16),
        grid_spec=pltpu.PrefetchScalarGridSpec(
            num_scalar_prefetch=1,
            grid=(tiles,),
            in_specs=[
                pl.BlockSpec((TILE, width), lambda i, s: (s[0, i] // TILE, 0)),
                pl.BlockSpec((TILE, 1), lambda i, s: (s[0, i] // TILE, 0)),
                pl.BlockSpec(halo.shape, lambda i, s: (0, 0)),
                pl.BlockSpec(kv.shape, lambda i, s: (0, 0)),
            ],
            out_specs=pl.BlockSpec((TILE, width), lambda i, s: (i, 0)),
            scratch_shapes=[
                pltpu.VMEM((halo_rows + kv.shape[0], kv.shape[1]), jnp.bfloat16),
                pltpu.VMEM((heads, TILE, HEAD_DIM), jnp.float32),
                pltpu.VMEM((heads, TILE, HEAD_DIM), jnp.float32),
            ],
        ),
        compiler_params=pltpu.CompilerParams(vmem_limit_bytes=VMEM_BYTES),
        cost_estimate=pl.CostEstimate(
            flops=4 * chunk_rows * width * (halo_rows + chunk_rows) // 2,
            bytes_accessed=4 * chunk_rows * width,
            transcendentals=chunk_rows * heads * (halo_rows + chunk_rows),
        ),
    )(bounds, query, starts[:, None], halo, kv)


def per_device(group, lines, cores, tokens, lengths, w_query, w_key, w_value):
    row_count, depth = tokens.shape
    slice_rows = w_query.shape[0]
    index = lax.axis_index("ca")
    mine, line = index % group, index // group
    core = lax.axis_index("tp")
    q_width = w_query.shape[1] // group
    one_width = w_key.shape[1] // group
    kv_width = 2 * one_width
    kv_heads = one_width // HEAD_DIM
    group_rows = group * row_count
    devices = range(group * lines)

    def slice_for(target):
        return jnp.concatenate(
            [
                lax.dynamic_slice_in_dim(w_query, target * q_width, q_width, 1),
                lax.dynamic_slice_in_dim(w_key, target * one_width, one_width, 1),
                lax.dynamic_slice_in_dim(w_value, target * one_width, one_width, 1),
            ],
            axis=1,
        )

    def to_partner(block, step):
        return lax.ppermute(block, "ca", [(i, i ^ step) for i in devices])

    def along_lines(block):
        lanes = [[place + group * i for i in range(lines)] for place in range(group)]
        return lax.all_gather(block, "ca", axis=0, tiled=True, axis_index_groups=lanes)

    own_slices = along_lines(slice_for(mine))
    rest_kv = rest_q = None
    all_tokens = tokens
    if group > 1:
        arrived = [to_partner(slice_for(mine ^ step), step) for step in range(1, group)]
        rest_kv = along_lines(jnp.concatenate([a[:, q_width:] for a in arrived]))
        rest_q = along_lines(jnp.concatenate([a[:, :q_width] for a in arrived]))

        half = row_count // cores
        both = ("ca", "tp")

        def cross(block, steps):
            pairs = [(i * 2 + c, (i ^ steps[c]) * 2 + c) for i in devices for c in range(2)]
            return lax.ppermute(block, both, pairs)

        def swap(block):
            return lax.ppermute(block, both, [(i * 2 + c, i * 2 + 1 - c) for i in devices for c in range(2)])

        own_half = lax.dynamic_slice_in_dim(tokens, core * half, half, 0)
        near = cross(own_half, (1, 2))
        other = cross(own_half, (2, 1))
        far = cross(near, (2, 1))
        all_tokens = jnp.zeros((group_rows, depth), tokens.dtype)
        all_tokens = lax.dynamic_update_slice_in_dim(all_tokens, tokens, mine * row_count, 0)
        for block, steps in ((near, (1, 2)), (other, (2, 1)), (far, (3, 3))):
            mate = swap(block)
            step_here = jnp.where(core == 0, steps[0], steps[1])
            step_mate = jnp.where(core == 0, steps[1], steps[0])
            all_tokens = lax.dynamic_update_slice_in_dim(
                all_tokens, block, (mine ^ step_here) * row_count + core * half, 0
            )
            all_tokens = lax.dynamic_update_slice_in_dim(
                all_tokens, mate, (mine ^ step_mate) * row_count + (1 - core) * half, 0
            )

    row_ids = line * group_rows + jnp.arange(group_rows, dtype=jnp.int32)
    starts = doc_starts(lengths, row_ids)
    cosine, sine = rope_tables(row_ids - starts)
    place = mine.reshape(1).astype(jnp.int32)
    kv = project(
        place, all_tokens, own_slices, rest_kv, q_width // kv_width, kv_width, cosine, sine, kv_heads, group, slice_rows
    )
    query = project(
        place, all_tokens, own_slices, rest_q, 0, q_width, cosine, sine, q_width // HEAD_DIM, group, slice_rows
    )

    halo_rows = REACH * row_count
    hops = -(-halo_rows // group_rows)
    pieces, moving = [], kv
    for hop in range(hops):
        keep = min(halo_rows - hop * group_rows, group_rows)
        moving = moving[moving.shape[0] - keep :]
        moving = lax.ppermute(moving, "ca", [(i, i + group) for i in devices if i + group in devices])
        pieces.insert(0, moving)
    halo = pieces[0] if len(pieces) == 1 else jnp.concatenate(pieces)

    window_starts = starts - (line * group_rows - halo_rows)
    result = jnp.zeros((row_count, w_query.shape[1]), jnp.bfloat16)
    for step in reversed(range(group)):
        part = attend(mine ^ step, row_count, query, window_starts, halo, kv, kv_heads)
        if step > 0:
            part = to_partner(part, step)
        elif group == 1:
            return part
        result = lax.dynamic_update_slice_in_dim(result, part, (mine ^ step) * q_width, 1)
    return result


def solution(mesh):
    size, cores = mesh.shape["ca"], mesh.shape["tp"]
    local_kv = KV_HEADS // cores
    group = 4 if cores == 2 and local_kv % 4 == 0 and size % 4 == 0 else 1
    placed = (P("ca", None), P(), P("ca", "tp"), P("ca", "tp"), P("ca", "tp"))
    body = functools.partial(per_device, group, size // group, cores)
    return jax.shard_map(body, mesh=mesh, in_specs=placed, out_specs=P("ca", "tp"), check_vma=False)
```

```python
import functools
import math

import jax
import jax.numpy as jnp
from jax import lax
from jax.experimental import pallas as pl
from jax.experimental.pallas import tpu as pltpu
from jax.sharding import PartitionSpec as P

HEADS = 32
KV_HEADS = 8
HEAD_DIM = 128
REACH = 3
ROPE_THETA = 500000.0
LOGIT_CAP = 5.0
TILE = 256
VMEM_BYTES = 48 * 1024 * 1024


def doc_starts(lengths, positions):
    doc_ends = jnp.cumsum(lengths).astype(jnp.int32)
    before = doc_ends[None, :] <= positions[:, None]
    return jnp.max(jnp.where(before, doc_ends[None, :], 0), axis=1).astype(jnp.int32)


def rope_tables(offsets):
    half_dim = HEAD_DIM // 2
    frequency = ROPE_THETA ** (-(jnp.arange(half_dim, dtype=jnp.float32) * 2.0) / HEAD_DIM)
    angles = offsets.astype(jnp.float32)[:, None] * frequency[None, :]
    cosine, sine = jnp.cos(angles), jnp.sin(angles)
    return jnp.concatenate([cosine, cosine], axis=1), jnp.concatenate([-sine, sine], axis=1)


def rotated(values, cosine, sine):
    return values * cosine + pltpu.roll(values, HEAD_DIM // 2, 1) * sine


def project_kernel(rope_heads, layout, place, *refs):
    parts, weights = layout
    inputs = len(parts) + len(weights)
    x_refs, w_refs = refs[: len(parts)], refs[len(parts) : inputs]
    cos_ref, sin_ref, out_ref, x_all, w_all, x_sems, w_sem = refs[inputs:]
    slot = 0
    w_copies, x_copies, rows_of = [], [], []
    for ref, (column, pieces) in zip(w_refs, weights):
        for source, rows, target in pieces:
            at = pl.multiple_of(target(place), rows)
            width = w_all.shape[1]
            copy = pltpu.make_async_copy(
                ref.at[pl.ds(source, rows), pl.ds(column, width)], w_all.at[pl.ds(at, rows), :], w_sem.at[slot]
            )
            copy.start()
            w_copies.append(copy)
            slot += 1
    slot = 0
    tile = x_all.shape[0]
    for ref, targets in zip(x_refs, parts):
        step = ref.shape[0] // len(targets)
        for number, target in enumerate(targets):
            copy = pltpu.make_async_copy(
                ref.at[pl.ds(number * step, step), :], x_all.at[pl.ds(slot * step, step), :], x_sems.at[slot]
            )
            copy.start()
            x_copies.append(copy)
            rows_of.append(pl.multiple_of(target(place), step))
            slot += 1
    for copy in w_copies:
        copy.wait()
    count = len(x_copies)
    step = tile // count
    pair = 2 if count % 2 == 0 else 1
    for first in range(0, count, pair):
        for number in range(first, first + pair):
            x_copies[number].wait()
        total = jnp.dot(
            x_all[first * step : (first + pair) * step, :], w_all[...], preferred_element_type=jnp.float32
        )
        for number in range(pair):
            rows = pl.ds(rows_of[first + number], step)
            cosine, sine = cos_ref[rows, :], sin_ref[rows, :]
            for head in range(out_ref.shape[1] // HEAD_DIM):
                columns = slice(head * HEAD_DIM, (head + 1) * HEAD_DIM)
                part = total[number * step : (number + 1) * step, columns]
                if head < rope_heads:
                    part = rotated(part, cosine, sine)
                out_ref[rows, columns] = part.astype(out_ref.dtype)


def project(place, tokens, weights, width, cosine, sine, rope_heads):
    rows = sum(part.shape[0] for part, _ in tokens)
    depth = tokens[0][0].shape[1]
    layout = ([targets for _, targets in tokens], [(column, pieces) for _, column, pieces in weights])
    arrays = [part for part, _ in tokens] + [part for part, _, _ in weights]
    dtype = tokens[0][0].dtype
    return pl.pallas_call(
        functools.partial(project_kernel, rope_heads, layout),
        out_shape=jax.ShapeDtypeStruct((rows, width), jnp.bfloat16),
        in_specs=[pl.BlockSpec(memory_space=pltpu.SMEM)]
        + [pl.BlockSpec(memory_space=pl.ANY)] * len(arrays)
        + [pl.BlockSpec(memory_space=pltpu.VMEM)] * 2,
        out_specs=pl.BlockSpec(memory_space=pltpu.VMEM),
        scratch_shapes=[
            pltpu.VMEM((rows, depth), dtype),
            pltpu.VMEM((depth, width), dtype),
            pltpu.SemaphoreType.DMA((sum(len(targets) for _, targets in tokens),)),
            pltpu.SemaphoreType.DMA((sum(len(pieces) for _, _, pieces in weights),)),
        ],
        compiler_params=pltpu.CompilerParams(vmem_limit_bytes=VMEM_BYTES),
        cost_estimate=pl.CostEstimate(
            flops=2 * rows * depth * width, bytes_accessed=2 * depth * (rows + width), transcendentals=0
        ),
    )(place, *arrays, cosine, sine)


def attend_kernel(kv_heads, share, halo_rows, bounds, q_ref, start_ref, halo_ref, kv_ref, out_ref, kv_all, sums, totals):
    tile_index = pl.program_id(0)

    @pl.when(tile_index == 0)
    def _():
        kv_all[:halo_rows, :] = halo_ref[...]
        kv_all[halo_rows:, :] = kv_ref[...]

    tile = q_ref.shape[0]
    place = bounds[0, tile_index]
    first_start = bounds[1, tile_index]
    last_start = bounds[2, tile_index]
    q_first = halo_rows + place
    first_block = first_start // TILE
    last_block = (q_first + tile - 1) // TILE
    sums[...] = jnp.zeros_like(sums)
    totals[...] = jnp.zeros_like(totals)
    inner = 1.0 / (math.sqrt(HEAD_DIM) * LOGIT_CAP)
    outer = LOGIT_CAP * math.log2(math.e)

    def block_step(block, masked):
        rows = pl.ds(pl.multiple_of(block * TILE, TILE), TILE)
        if masked:
            k_ids = block * TILE + lax.broadcasted_iota(jnp.int32, (tile, TILE), 1)
            q_ids = q_first + lax.broadcasted_iota(jnp.int32, (tile, TILE), 0)
            allowed = (k_ids <= q_ids) & (k_ids >= start_ref[...])
        for kv_head in range(kv_heads):
            keys = kv_all[rows, kv_head * HEAD_DIM : (kv_head + 1) * HEAD_DIM]
            at = (kv_heads + kv_head) * HEAD_DIM
            values = kv_all[rows, at : at + HEAD_DIM]
            for member in range(share):
                head = kv_head * share + member
                query = q_ref[:, head * HEAD_DIM : (head + 1) * HEAD_DIM]
                raw = lax.dot_general(query, keys, (((1,), (1,)), ((), ())), preferred_element_type=jnp.float32)
                weights = jnp.exp2(outer * jnp.tanh(raw * inner))
                if masked:
                    weights = jnp.where(allowed, weights, 0.0)
                partial = weights[:, :HEAD_DIM]
                for part in range(1, TILE // HEAD_DIM):
                    partial = partial + weights[:, part * HEAD_DIM : (part + 1) * HEAD_DIM]
                totals[head] += partial
                sums[head] += jnp.dot(weights.astype(jnp.bfloat16), values, preferred_element_type=jnp.float32)

    def either(block, carry):
        begin = block * TILE
        whole = (begin >= last_start) & (begin + TILE - 1 <= q_first)

        @pl.when(whole)
        def _():
            block_step(block, False)

        @pl.when(jnp.logical_not(whole))
        def _():
            block_step(block, True)

        return carry

    lax.fori_loop(first_block, last_block + 1, either, 0)
    for head in range(kv_heads * share):
        denominator = jnp.sum(totals[head], axis=1, keepdims=True)
        out_ref[:, head * HEAD_DIM : (head + 1) * HEAD_DIM] = (sums[head] / denominator).astype(out_ref.dtype)


def attend(chunk, chunk_rows, query, starts, halo, kv, kv_heads):
    width = query.shape[1]
    heads = width // HEAD_DIM
    halo_rows = halo.shape[0]
    tiles = chunk_rows // TILE
    places = chunk * chunk_rows + jnp.arange(tiles, dtype=jnp.int32) * TILE
    bounds = jnp.stack([places, starts[places], starts[places + TILE - 1]])
    kernel = functools.partial(attend_kernel, kv_heads, heads // kv_heads, halo_rows)
    return pl.pallas_call(
        kernel,
        out_shape=jax.ShapeDtypeStruct((chunk_rows, width), jnp.bfloat16),
        grid_spec=pltpu.PrefetchScalarGridSpec(
            num_scalar_prefetch=1,
            grid=(tiles,),
            in_specs=[
                pl.BlockSpec((TILE, width), lambda i, s: (s[0, i] // TILE, 0)),
                pl.BlockSpec((TILE, 1), lambda i, s: (s[0, i] // TILE, 0)),
                pl.BlockSpec(halo.shape, lambda i, s: (0, 0)),
                pl.BlockSpec(kv.shape, lambda i, s: (0, 0)),
            ],
            out_specs=pl.BlockSpec((TILE, width), lambda i, s: (i, 0)),
            scratch_shapes=[
                pltpu.VMEM((halo_rows + kv.shape[0], kv.shape[1]), jnp.bfloat16),
                pltpu.VMEM((heads, TILE, HEAD_DIM), jnp.float32),
                pltpu.VMEM((heads, TILE, HEAD_DIM), jnp.float32),
            ],
        ),
        compiler_params=pltpu.CompilerParams(vmem_limit_bytes=VMEM_BYTES),
        cost_estimate=pl.CostEstimate(
            flops=4 * chunk_rows * width * (halo_rows + chunk_rows) // 2,
            bytes_accessed=4 * chunk_rows * width,
            transcendentals=chunk_rows * heads * (halo_rows + chunk_rows),
        ),
    )(bounds, query, starts[:, None], halo, kv)


def per_device(group, lines, cores, tokens, lengths, w_query, w_key, w_value):
    row_count, depth = tokens.shape
    slice_rows = w_query.shape[0]
    index = lax.axis_index("ca")
    mine, line = index % group, index // group
    core = lax.axis_index("tp")
    q_width = w_query.shape[1] // group
    one_width = w_key.shape[1] // group
    kv_width = 2 * one_width
    kv_heads = one_width // HEAD_DIM
    group_rows = group * row_count
    devices = range(group * lines)

    def slice_for(target):
        return jnp.concatenate(
            [
                lax.dynamic_slice_in_dim(w_query, target * q_width, q_width, 1),
                lax.dynamic_slice_in_dim(w_key, target * one_width, one_width, 1),
                lax.dynamic_slice_in_dim(w_value, target * one_width, one_width, 1),
            ],
            axis=1,
        )

    def to_partner(block, step):
        return lax.ppermute(block, "ca", [(i, i ^ step) for i in devices])

    def along_lines(block):
        lanes = [[place + group * i for i in range(lines)] for place in range(group)]
        return lax.all_gather(block, "ca", axis=0, tiled=True, axis_index_groups=lanes)

    def ring(block):
        held = [block]
        for hop in range(1, lines):
            held.append(lax.ppermute(held[-1], "ca", [(i, (i + group) % (group * lines)) for i in devices]))
        return held

    def gathered(array, column, members):
        if group == 1:
            return (array, column, [(0, array.shape[0], lambda s: 0)])
        pieces = []
        for at in range(lines):
            for number, step in enumerate(members):
                source = (at * len(members) + number) * slice_rows
                pieces.append((source, slice_rows, lambda s, at=at, step=step: (at * group + (s[0] ^ step)) * slice_rows))
        return (array, column, pieces)

    def from_ring(held, members):
        entries = []
        for back, array in enumerate(held):
            pieces = []
            for number, step in enumerate(members):

                def target(s, back=back, step=step):
                    at = lax.rem(s[1] - back + lines, lines)
                    return (at * group + (s[0] ^ step)) * slice_rows

                pieces.append((number * slice_rows, slice_rows, target))
            entries.append((array, 0, pieces))
        return entries

    own_slices = along_lines(slice_for(mine))
    half = row_count // cores if group > 1 else row_count
    token_parts = [
        (tokens, [lambda s, i=i: s[0] * row_count + i * half for i in range(row_count // half)]),
    ]
    if group > 1:
        others = range(1, group)
        arrived = [to_partner(slice_for(mine ^ step), step) for step in others]
        split = q_width // 2
        rest_kv = ring(jnp.concatenate([a[:, q_width:] for a in arrived]))
        rest_first = along_lines(jnp.concatenate([a[:, :split] for a in arrived]))
        rest_second = ring(jnp.concatenate([a[:, split:q_width] for a in arrived]))
        kv_weights = [gathered(own_slices, q_width, [0])] + from_ring(rest_kv, others)
        q_weights = [
            [gathered(own_slices, 0, [0]), gathered(rest_first, 0, others)],
            [gathered(own_slices, split, [0])] + from_ring(rest_second, others),
        ]

        both = ("ca", "tp")

        def cross(block, steps):
            pairs = [(i * 2 + c, (i ^ steps[c]) * 2 + c) for i in devices for c in range(2)]
            return lax.ppermute(block, both, pairs)

        def swap(block):
            return lax.ppermute(block, both, [(i * 2 + c, i * 2 + 1 - c) for i in devices for c in range(2)])

        own_half = lax.dynamic_slice_in_dim(tokens, core * half, half, 0)
        near = cross(own_half, (1, 2))
        other = cross(own_half, (2, 1))
        far = cross(near, (2, 1))
        for block, steps in ((near, (1, 2)), (other, (2, 1)), (far, (3, 3))):

            def here(s, steps=steps):
                return (s[0] ^ jnp.where(s[2] == 0, steps[0], steps[1])) * row_count + s[2] * half

            def mate(s, steps=steps):
                return (s[0] ^ jnp.where(s[2] == 0, steps[1], steps[0])) * row_count + (1 - s[2]) * half

            token_parts += [(block, [here]), (swap(block), [mate])]
    else:
        split = q_width
        kv_weights = [gathered(own_slices, q_width, [0])]
        q_weights = [[gathered(own_slices, 0, [0])]]

    row_ids = line * group_rows + jnp.arange(group_rows, dtype=jnp.int32)
    starts = doc_starts(lengths, row_ids)
    cosine, sine = rope_tables(row_ids - starts)
    place = jnp.stack([mine, line, core]).astype(jnp.int32)
    kv = project(place, token_parts, kv_weights, kv_width, cosine, sine, kv_heads)

    halo_rows = REACH * row_count
    hops = -(-halo_rows // group_rows)
    pieces, moving = [], kv
    for hop in range(hops):
        keep = min(halo_rows - hop * group_rows, group_rows)
        moving = moving[moving.shape[0] - keep :]
        moving = lax.ppermute(moving, "ca", [(i, i + group) for i in devices if i + group in devices])
        pieces.insert(0, moving)
    halo = pieces[0] if len(pieces) == 1 else jnp.concatenate(pieces)

    window_starts = starts - (line * group_rows - halo_rows)
    result = jnp.zeros((row_count, w_query.shape[1]), jnp.bfloat16)
    for number, weights in enumerate(q_weights):
        query = project(place, token_parts, weights, split, cosine, sine, split // HEAD_DIM)
        for step in reversed(range(group)):
            part = attend(mine ^ step, row_count, query, window_starts, halo, kv, kv_heads)
            if step > 0:
                part = to_partner(part, step)
            elif group == 1:
                return part
            result = lax.dynamic_update_slice_in_dim(result, part, (mine ^ step) * q_width + number * split, 1)
    return result


def solution(mesh):
    size, cores = mesh.shape["ca"], mesh.shape["tp"]
    local_kv = KV_HEADS // cores
    group = 4 if cores == 2 and local_kv == 4 and size % 4 == 0 else 1
    placed = (P("ca", None), P(), P("ca", "tp"), P("ca", "tp"), P("ca", "tp"))
    body = functools.partial(per_device, group, size // group, cores)
    return jax.shard_map(body, mesh=mesh, in_specs=placed, out_specs=P("ca", "tp"), check_vma=False)
```

```python
import functools
import math

import jax
import jax.numpy as jnp
from jax import lax
from jax.experimental import pallas as pl
from jax.experimental.pallas import tpu as pltpu
from jax.sharding import PartitionSpec as P

HEADS = 32
KV_HEADS = 8
HEAD_DIM = 128
REACH = 3
ROPE_THETA = 500000.0
LOGIT_CAP = 5.0
TILE = 256
VMEM_BYTES = 48 * 1024 * 1024


def doc_starts(lengths, positions):
    doc_ends = jnp.cumsum(lengths).astype(jnp.int32)
    before = doc_ends[None, :] <= positions[:, None]
    return jnp.max(jnp.where(before, doc_ends[None, :], 0), axis=1).astype(jnp.int32)


def rope_tables(offsets):
    half_dim = HEAD_DIM // 2
    frequency = ROPE_THETA ** (-(jnp.arange(half_dim, dtype=jnp.float32) * 2.0) / HEAD_DIM)
    angles = offsets.astype(jnp.float32)[:, None] * frequency[None, :]
    cosine, sine = jnp.cos(angles), jnp.sin(angles)
    return jnp.concatenate([cosine, cosine], axis=1), jnp.concatenate([-sine, sine], axis=1)


def rotated(values, cosine, sine):
    return values * cosine + pltpu.roll(values, HEAD_DIM // 2, 1) * sine


def project_kernel(rope_heads, layout, based, place, *refs):
    parts, weights = layout
    x_refs, w_refs = refs[: len(parts)], refs[len(parts) : len(parts) + len(weights)]
    refs = refs[len(parts) + len(weights) :]
    if based:
        base_ref, refs = refs[0], refs[1:]
    cos_ref, sin_ref, out_ref, x_all, w_all, x_sems, w_sem = refs
    width, depth = out_ref.shape[1], x_all.shape[2]
    slot = 0
    w_copies, x_copies = [], []
    for ref, (column, pieces) in zip(w_refs, weights):
        for source, rows, target in pieces:
            at = pl.multiple_of(target(place), rows)
            copy = pltpu.make_async_copy(
                ref.at[pl.ds(source, rows), pl.ds(column, width)], w_all.at[pl.ds(at, rows), :], w_sem.at[slot]
            )
            copy.start()
            w_copies.append(copy)
            slot += 1
    slots, step = x_all.shape[0], x_all.shape[1]
    for ref, targets in zip(x_refs, parts):
        for number, target in enumerate(targets):
            at = len(x_copies) % slots
            copy = pltpu.make_async_copy(ref.at[pl.ds(number * step, step), :], x_all.at[at], x_sems.at[at])
            x_copies.append((copy, pl.multiple_of(target(place), step), at))
    for copy, _, _ in x_copies[: slots - 1]:
        copy.start()
    if based:
        out_ref[...] = base_ref[...]
    for copy in w_copies:
        copy.wait()
    for number, (copy, at, slot) in enumerate(x_copies):
        if number + slots - 1 < len(x_copies):
            x_copies[number + slots - 1][0].start()
        copy.wait()
        total = jnp.dot(x_all[slot], w_all[...], preferred_element_type=jnp.float32)
        rows = pl.ds(at, step)
        cosine, sine = cos_ref[rows, :], sin_ref[rows, :]
        for head in range(width // HEAD_DIM):
            columns = slice(head * HEAD_DIM, (head + 1) * HEAD_DIM)
            part = total[:, columns]
            if head < rope_heads:
                part = rotated(part, cosine, sine)
            out_ref[rows, columns] = part.astype(out_ref.dtype)


def project(place, tokens, weights, width, cosine, sine, rope_heads, base=None):
    rows, depth = cosine.shape[0], tokens[0][0].shape[1]
    step = tokens[0][0].shape[0] // len(tokens[0][1])
    worked = sum(part.shape[0] for part, _ in tokens)
    layout = ([targets for _, targets in tokens], [(column, pieces) for _, column, pieces in weights])
    arrays = [part for part, _ in tokens] + [part for part, _, _ in weights]
    dtype = tokens[0][0].dtype
    bases = [] if base is None else [base]
    return pl.pallas_call(
        functools.partial(project_kernel, rope_heads, layout, base is not None),
        out_shape=jax.ShapeDtypeStruct((rows, width), jnp.bfloat16),
        in_specs=[pl.BlockSpec(memory_space=pltpu.SMEM)]
        + [pl.BlockSpec(memory_space=pl.ANY)] * len(arrays)
        + [pl.BlockSpec(memory_space=pltpu.VMEM)] * (2 + len(bases)),
        out_specs=pl.BlockSpec(memory_space=pltpu.VMEM),
        scratch_shapes=[
            pltpu.VMEM((4, step, depth), dtype),
            pltpu.VMEM((depth, width), dtype),
            pltpu.SemaphoreType.DMA((4,)),
            pltpu.SemaphoreType.DMA((sum(len(pieces) for _, _, pieces in weights),)),
        ],
        compiler_params=pltpu.CompilerParams(vmem_limit_bytes=VMEM_BYTES),
        cost_estimate=pl.CostEstimate(
            flops=worked * width, bytes_accessed=worked * width, transcendentals=0
        ),
    )(place, *arrays, *bases, cosine, sine)


def attend_kernel(kv_heads, share, halo_rows, bounds, q_ref, start_ref, halo_ref, kv_ref, out_ref, kv_all, sums, totals):
    tile_index = pl.program_id(0)

    @pl.when(tile_index == 0)
    def _():
        kv_all[:halo_rows, :] = halo_ref[...]
        kv_all[halo_rows:, :] = kv_ref[...]

    tile = q_ref.shape[0]
    place = bounds[0, tile_index]
    first_start = bounds[1, tile_index]
    last_start = bounds[2, tile_index]
    q_first = halo_rows + place
    first_block = first_start // TILE
    last_block = (q_first + tile - 1) // TILE
    sums[...] = jnp.zeros_like(sums)
    totals[...] = jnp.zeros_like(totals)
    inner = 1.0 / (math.sqrt(HEAD_DIM) * LOGIT_CAP)
    outer = LOGIT_CAP * math.log2(math.e)

    def block_step(block, masked):
        rows = pl.ds(pl.multiple_of(block * TILE, TILE), TILE)
        if masked:
            k_ids = block * TILE + lax.broadcasted_iota(jnp.int32, (tile, TILE), 1)
            q_ids = q_first + lax.broadcasted_iota(jnp.int32, (tile, TILE), 0)
            allowed = (k_ids <= q_ids) & (k_ids >= start_ref[...])
        for kv_head in range(kv_heads):
            keys = kv_all[rows, kv_head * HEAD_DIM : (kv_head + 1) * HEAD_DIM]
            at = (kv_heads + kv_head) * HEAD_DIM
            values = kv_all[rows, at : at + HEAD_DIM]
            for member in range(share):
                head = kv_head * share + member
                query = q_ref[:, head * HEAD_DIM : (head + 1) * HEAD_DIM]
                raw = lax.dot_general(query, keys, (((1,), (1,)), ((), ())), preferred_element_type=jnp.float32)
                weights = jnp.exp2(outer * jnp.tanh(raw * inner))
                if masked:
                    weights = jnp.where(allowed, weights, 0.0)
                partial = weights[:, :HEAD_DIM]
                for part in range(1, TILE // HEAD_DIM):
                    partial = partial + weights[:, part * HEAD_DIM : (part + 1) * HEAD_DIM]
                totals[head] += partial
                sums[head] += jnp.dot(weights.astype(jnp.bfloat16), values, preferred_element_type=jnp.float32)

    def either(block, carry):
        begin = block * TILE
        whole = (begin >= last_start) & (begin + TILE - 1 <= q_first)

        @pl.when(whole)
        def _():
            block_step(block, False)

        @pl.when(jnp.logical_not(whole))
        def _():
            block_step(block, True)

        return carry

    lax.fori_loop(first_block, last_block + 1, either, 0)
    for head in range(kv_heads * share):
        denominator = jnp.sum(totals[head], axis=1, keepdims=True)
        out_ref[:, head * HEAD_DIM : (head + 1) * HEAD_DIM] = (sums[head] / denominator).astype(out_ref.dtype)


def attend(chunk, chunk_rows, query, starts, halo, kv, kv_heads):
    width = query.shape[1]
    heads = width // HEAD_DIM
    halo_rows = halo.shape[0]
    tiles = chunk_rows // TILE
    places = chunk * chunk_rows + jnp.arange(tiles, dtype=jnp.int32) * TILE
    bounds = jnp.stack([places, starts[places], starts[places + TILE - 1]])
    kernel = functools.partial(attend_kernel, kv_heads, heads // kv_heads, halo_rows)
    return pl.pallas_call(
        kernel,
        out_shape=jax.ShapeDtypeStruct((chunk_rows, width), jnp.bfloat16),
        grid_spec=pltpu.PrefetchScalarGridSpec(
            num_scalar_prefetch=1,
            grid=(tiles,),
            in_specs=[
                pl.BlockSpec((TILE, width), lambda i, s: (s[0, i] // TILE, 0)),
                pl.BlockSpec((TILE, 1), lambda i, s: (s[0, i] // TILE, 0)),
                pl.BlockSpec(halo.shape, lambda i, s: (0, 0)),
                pl.BlockSpec(kv.shape, lambda i, s: (0, 0)),
            ],
            out_specs=pl.BlockSpec((TILE, width), lambda i, s: (i, 0)),
            scratch_shapes=[
                pltpu.VMEM((halo_rows + kv.shape[0], kv.shape[1]), jnp.bfloat16),
                pltpu.VMEM((heads, TILE, HEAD_DIM), jnp.float32),
                pltpu.VMEM((heads, TILE, HEAD_DIM), jnp.float32),
            ],
        ),
        compiler_params=pltpu.CompilerParams(vmem_limit_bytes=VMEM_BYTES),
        cost_estimate=pl.CostEstimate(
            flops=4 * chunk_rows * width * (halo_rows + chunk_rows) // 2,
            bytes_accessed=4 * chunk_rows * width,
            transcendentals=chunk_rows * heads * (halo_rows + chunk_rows),
        ),
    )(bounds, query, starts[:, None], halo, kv)


def per_device(group, lines, cores, tokens, lengths, w_query, w_key, w_value):
    row_count, depth = tokens.shape
    slice_rows = w_query.shape[0]
    index = lax.axis_index("ca")
    mine, line = index % group, index // group
    core = lax.axis_index("tp")
    q_width = w_query.shape[1] // group
    one_width = w_key.shape[1] // group
    kv_width = 2 * one_width
    kv_heads = one_width // HEAD_DIM
    group_rows = group * row_count
    devices = range(group * lines)

    def slice_for(target):
        return jnp.concatenate(
            [
                lax.dynamic_slice_in_dim(w_query, target * q_width, q_width, 1),
                lax.dynamic_slice_in_dim(w_key, target * one_width, one_width, 1),
                lax.dynamic_slice_in_dim(w_value, target * one_width, one_width, 1),
            ],
            axis=1,
        )

    def to_partner(block, step):
        return lax.ppermute(block, "ca", [(i, i ^ step) for i in devices])

    def along_lines(block):
        lanes = [[place + group * i for i in range(lines)] for place in range(group)]
        return lax.all_gather(block, "ca", axis=0, tiled=True, axis_index_groups=lanes)

    def directly(block):
        total = group * lines
        shifts = [[(i, (i + group * back) % total) for i in devices] for back in range(1, lines)]
        return [block] + [lax.ppermute(block, "ca", pairs) for pairs in shifts]

    def gathered(array, column, members):
        if group == 1:
            return (array, column, [(0, array.shape[0], lambda s: 0)])
        pieces = []
        for at in range(lines):
            for number, step in enumerate(members):
                source = (at * len(members) + number) * slice_rows
                pieces.append((source, slice_rows, lambda s, at=at, step=step: (at * group + (s[0] ^ step)) * slice_rows))
        return (array, column, pieces)

    def from_lines(held, members):
        entries = []
        for back, array in enumerate(held):
            pieces = []
            for number, step in enumerate(members):

                def target(s, back=back, step=step):
                    at = lax.rem(s[1] - back + lines, lines)
                    return (at * group + (s[0] ^ step)) * slice_rows

                pieces.append((number * slice_rows, slice_rows, target))
            entries.append((array, 0, pieces))
        return entries

    own_slices = along_lines(slice_for(mine))
    half = row_count // cores if group > 1 else row_count
    token_parts = [
        (tokens, [lambda s, i=i: s[0] * row_count + i * half for i in range(row_count // half)]),
    ]
    if group > 1:
        others = range(1, group)
        arrived = [to_partner(slice_for(mine ^ step), step) for step in others]
        split = q_width // 2
        rest_kv = along_lines(jnp.concatenate([a[:, q_width:] for a in arrived]))
        rest_first = directly(jnp.concatenate([a[:, :split] for a in arrived]))
        rest_second = along_lines(jnp.concatenate([a[:, split:q_width] for a in arrived]))
        kv_weights = [gathered(own_slices, q_width, [0]), gathered(rest_kv, 0, others)]
        q_weights = [
            [gathered(own_slices, 0, [0])] + from_lines(rest_first, others),
            [gathered(own_slices, split, [0]), gathered(rest_second, 0, others)],
        ]

        both = ("ca", "tp")

        def cross(block, steps):
            pairs = [(i * 2 + c, (i ^ steps[c]) * 2 + c) for i in devices for c in range(2)]
            return lax.ppermute(block, both, pairs)

        def swap(block):
            return lax.ppermute(block, both, [(i * 2 + c, i * 2 + 1 - c) for i in devices for c in range(2)])

        begin = core * half

        def share_tokens(tokens):
            own_half = lax.dynamic_slice_in_dim(tokens, begin, half, 0)
            near = cross(own_half, (1, 2))
            other = cross(own_half, (2, 1))
            far = cross(near, (2, 1))
            return tuple((block, swap(block)) for block in (near, other, far))

        def no_tokens(tokens):
            return tuple((jnp.zeros((half, depth), tokens.dtype),) * 2 for _ in range(3))

        known = sum(a[0, 0].astype(jnp.float32) for a in arrived)
        blocks = lax.cond(known == known, share_tokens, no_tokens, tokens)
        for (block, other_half), steps in zip(blocks, ((1, 2), (2, 1), (3, 3))):

            def here(s, steps=steps):
                return (s[0] ^ jnp.where(s[2] == 0, steps[0], steps[1])) * row_count + s[2] * half

            def mate(s, steps=steps):
                return (s[0] ^ jnp.where(s[2] == 0, steps[1], steps[0])) * row_count + (1 - s[2]) * half

            token_parts += [(block, [here]), (other_half, [mate])]
    else:
        split = q_width
        kv_weights = [gathered(own_slices, q_width, [0])]
        q_weights = [[gathered(own_slices, 0, [0])]]

    row_ids = line * group_rows + jnp.arange(group_rows, dtype=jnp.int32)
    starts = doc_starts(lengths, row_ids)
    cosine, sine = rope_tables(row_ids - starts)
    place = jnp.stack([mine, line, core]).astype(jnp.int32)
    kv = project(place, token_parts, kv_weights, kv_width, cosine, sine, kv_heads)

    halo_rows = REACH * row_count
    hops = -(-halo_rows // group_rows)
    pieces, moving = [], kv
    for hop in range(hops):
        keep = min(halo_rows - hop * group_rows, group_rows)
        moving = moving[moving.shape[0] - keep :]
        moving = lax.ppermute(moving, "ca", [(i, i + group) for i in devices if i + group in devices])
        pieces.insert(0, moving)
    halo = pieces[0] if len(pieces) == 1 else jnp.concatenate(pieces)

    window_starts = starts - (line * group_rows - halo_rows)
    result = jnp.zeros((row_count, w_query.shape[1]), jnp.bfloat16)
    for number, weights in enumerate(q_weights):
        query = project(place, token_parts, weights, split, cosine, sine, split // HEAD_DIM)
        for step in reversed(range(group)):
            part = attend(mine ^ step, row_count, query, window_starts, halo, kv, kv_heads)
            if step > 0:
                part = to_partner(part, step)
            elif group == 1:
                return part
            result = lax.dynamic_update_slice_in_dim(result, part, (mine ^ step) * q_width + number * split, 1)
    return result


def solution(mesh):
    size, cores = mesh.shape["ca"], mesh.shape["tp"]
    local_kv = KV_HEADS // cores
    group = 4 if cores == 2 and local_kv == 4 and size % 4 == 0 else 1
    placed = (P("ca", None), P(), P("ca", "tp"), P("ca", "tp"), P("ca", "tp"))
    body = functools.partial(per_device, group, size // group, cores)
    return jax.shard_map(body, mesh=mesh, in_specs=placed, out_specs=P("ca", "tp"), check_vma=False)
```

```python
import functools
import math

import jax
import jax.numpy as jnp
from jax import lax
from jax.experimental import pallas as pl
from jax.experimental.pallas import tpu as pltpu
from jax.sharding import PartitionSpec as P

HEADS = 32
KV_HEADS = 8
HEAD_DIM = 128
REACH = 3
ROPE_THETA = 500000.0
LOGIT_CAP = 5.0
TILE = 256
COST = 2
VMEM_BYTES = 48 * 1024 * 1024


def doc_starts(lengths, positions):
    doc_ends = jnp.cumsum(lengths).astype(jnp.int32)
    before = doc_ends[None, :] <= positions[:, None]
    return jnp.max(jnp.where(before, doc_ends[None, :], 0), axis=1).astype(jnp.int32)


def rope_tables(offsets):
    half_dim = HEAD_DIM // 2
    frequency = ROPE_THETA ** (-(jnp.arange(half_dim, dtype=jnp.float32) * 2.0) / HEAD_DIM)
    angles = offsets.astype(jnp.float32)[:, None] * frequency[None, :]
    cosine, sine = jnp.cos(angles), jnp.sin(angles)
    return jnp.concatenate([cosine, cosine], axis=1), jnp.concatenate([-sine, sine], axis=1)


def rotated(values, cosine, sine):
    return values * cosine + pltpu.roll(values, HEAD_DIM // 2, 1) * sine


def project_kernel(rope_heads, layout, based, place, *refs):
    parts, weights = layout
    x_refs, w_refs = refs[: len(parts)], refs[len(parts) : len(parts) + len(weights)]
    refs = refs[len(parts) + len(weights) :]
    if based:
        base_ref, refs = refs[0], refs[1:]
    cos_ref, sin_ref, out_ref, x_all, w_all, x_sems, w_sem = refs
    width, depth = out_ref.shape[1], x_all.shape[2]
    slot = 0
    w_copies, x_copies = [], []
    for ref, (column, pieces) in zip(w_refs, weights):
        for source, rows, target in pieces:
            at = pl.multiple_of(target(place), rows)
            copy = pltpu.make_async_copy(
                ref.at[pl.ds(source, rows), pl.ds(column, width)], w_all.at[pl.ds(at, rows), :], w_sem.at[slot]
            )
            copy.start()
            w_copies.append(copy)
            slot += 1
    slots, step = x_all.shape[0], x_all.shape[1] // 2
    for ref, targets in zip(x_refs, parts):
        for number, target in enumerate(targets):
            at = len(x_copies)
            slot, row = (at // 2) % slots, (at % 2) * step
            copy = pltpu.make_async_copy(
                ref.at[pl.ds(number * step, step), :], x_all.at[slot, pl.ds(row, step), :], x_sems.at[slot, at % 2]
            )
            x_copies.append((copy, pl.multiple_of(target(place), step)))
    for copy, _ in x_copies[: 2 * (slots - 1)]:
        copy.start()
    if based:
        out_ref[...] = base_ref[...]
    for copy in w_copies:
        copy.wait()
    for number in range(0, len(x_copies), 2):
        for copy, _ in x_copies[number + 2 * (slots - 1) : number + 2 * slots]:
            copy.start()
        slot = (number // 2) % slots
        for copy, _ in x_copies[number : number + 2]:
            copy.wait()
        total = jnp.dot(x_all[slot], w_all[...], preferred_element_type=jnp.float32)
        for part, (_, at) in enumerate(x_copies[number : number + 2]):
            rows = pl.ds(at, step)
            cosine, sine = cos_ref[rows, :], sin_ref[rows, :]
            for head in range(width // HEAD_DIM):
                columns = slice(head * HEAD_DIM, (head + 1) * HEAD_DIM)
                values = total[part * step : (part + 1) * step, columns]
                if head < rope_heads:
                    values = rotated(values, cosine, sine)
                out_ref[rows, columns] = values.astype(out_ref.dtype)


def project(place, tokens, weights, width, cosine, sine, rope_heads, base=None):
    rows, depth = cosine.shape[0], tokens[0][0].shape[1]
    step = tokens[0][0].shape[0] // len(tokens[0][1])
    worked = sum(part.shape[0] for part, _ in tokens)
    layout = ([targets for _, targets in tokens], [(column, pieces) for _, column, pieces in weights])
    arrays = [part for part, _ in tokens] + [part for part, _, _ in weights]
    dtype = tokens[0][0].dtype
    bases = [] if base is None else [base]
    return pl.pallas_call(
        functools.partial(project_kernel, rope_heads, layout, base is not None),
        out_shape=jax.ShapeDtypeStruct((rows, width), jnp.bfloat16),
        in_specs=[pl.BlockSpec(memory_space=pltpu.SMEM)]
        + [pl.BlockSpec(memory_space=pl.ANY)] * len(arrays)
        + [pl.BlockSpec(memory_space=pltpu.VMEM)] * (2 + len(bases)),
        out_specs=pl.BlockSpec(memory_space=pltpu.VMEM),
        scratch_shapes=[
            pltpu.VMEM((3, 2 * step, depth), dtype),
            pltpu.VMEM((depth, width), dtype),
            pltpu.SemaphoreType.DMA((3, 2)),
            pltpu.SemaphoreType.DMA((sum(len(pieces) for _, _, pieces in weights),)),
        ],
        compiler_params=pltpu.CompilerParams(vmem_limit_bytes=VMEM_BYTES),
        cost_estimate=pl.CostEstimate(
            flops=COST * worked * depth * width, bytes_accessed=2 * depth * (worked + width), transcendentals=0
        ),
    )(place, *arrays, *bases, cosine, sine)


def attend_kernel(kv_heads, share, halo_rows, first, bounds, q_ref, start_ref, halo_ref, kv_ref, out_ref, kv_all, sums, totals):
    tile_index = pl.program_id(0)

    @pl.when(tile_index == 0)
    def _():
        kv_all[:halo_rows, :] = halo_ref[...]
        kv_all[halo_rows:, :] = kv_ref[...]

    tile = q_ref.shape[0]
    place = bounds[0, first[0] + tile_index]
    first_start = bounds[1, first[0] + tile_index]
    last_start = bounds[2, first[0] + tile_index]
    q_first = halo_rows + place
    first_block = first_start // TILE
    last_block = (q_first + tile - 1) // TILE
    sums[...] = jnp.zeros_like(sums)
    totals[...] = jnp.zeros_like(totals)
    inner = 1.0 / (math.sqrt(HEAD_DIM) * LOGIT_CAP)
    outer = LOGIT_CAP * math.log2(math.e)

    def block_step(block, masked):
        rows = pl.ds(pl.multiple_of(block * TILE, TILE), TILE)
        if masked:
            k_ids = block * TILE + lax.broadcasted_iota(jnp.int32, (tile, TILE), 1)
            q_ids = q_first + lax.broadcasted_iota(jnp.int32, (tile, TILE), 0)
            allowed = (k_ids <= q_ids) & (k_ids >= start_ref[...])
        for kv_head in range(kv_heads):
            keys = kv_all[rows, kv_head * HEAD_DIM : (kv_head + 1) * HEAD_DIM]
            at = (kv_heads + kv_head) * HEAD_DIM
            values = kv_all[rows, at : at + HEAD_DIM]
            for member in range(share):
                head = kv_head * share + member
                query = q_ref[:, head * HEAD_DIM : (head + 1) * HEAD_DIM]
                raw = lax.dot_general(query, keys, (((1,), (1,)), ((), ())), preferred_element_type=jnp.float32)
                weights = jnp.exp2(outer * jnp.tanh(raw * inner))
                if masked:
                    weights = jnp.where(allowed, weights, 0.0)
                partial = weights[:, :HEAD_DIM]
                for part in range(1, TILE // HEAD_DIM):
                    partial = partial + weights[:, part * HEAD_DIM : (part + 1) * HEAD_DIM]
                totals[head] += partial
                sums[head] += jnp.dot(weights.astype(jnp.bfloat16), values, preferred_element_type=jnp.float32)

    def either(block, carry):
        begin = block * TILE
        whole = (begin >= last_start) & (begin + TILE - 1 <= q_first)

        @pl.when(whole)
        def _():
            block_step(block, False)

        @pl.when(jnp.logical_not(whole))
        def _():
            block_step(block, True)

        return carry

    lax.fori_loop(first_block, last_block + 1, either, 0)
    for head in range(kv_heads * share):
        denominator = jnp.sum(totals[head], axis=1, keepdims=True)
        out_ref[:, head * HEAD_DIM : (head + 1) * HEAD_DIM] = (sums[head] / denominator).astype(out_ref.dtype)


def attend(chunk, chunk_rows, query, starts, bounds, halo, kv, kv_heads):
    width = query.shape[1]
    heads = width // HEAD_DIM
    halo_rows = halo.shape[0]
    tiles = chunk_rows // TILE
    first = (chunk * tiles).reshape(1).astype(jnp.int32)
    kernel = functools.partial(attend_kernel, kv_heads, heads // kv_heads, halo_rows)
    return pl.pallas_call(
        kernel,
        out_shape=jax.ShapeDtypeStruct((chunk_rows, width), jnp.bfloat16),
        grid_spec=pltpu.PrefetchScalarGridSpec(
            num_scalar_prefetch=2,
            grid=(tiles,),
            in_specs=[
                pl.BlockSpec((TILE, width), lambda i, c, s: (c[0] + i, 0)),
                pl.BlockSpec((TILE, 1), lambda i, c, s: (c[0] + i, 0)),
                pl.BlockSpec(halo.shape, lambda i, c, s: (0, 0)),
                pl.BlockSpec(kv.shape, lambda i, c, s: (0, 0)),
            ],
            out_specs=pl.BlockSpec((TILE, width), lambda i, c, s: (i, 0)),
            scratch_shapes=[
                pltpu.VMEM((halo_rows + kv.shape[0], kv.shape[1]), jnp.bfloat16),
                pltpu.VMEM((heads, TILE, HEAD_DIM), jnp.float32),
                pltpu.VMEM((heads, TILE, HEAD_DIM), jnp.float32),
            ],
        ),
        compiler_params=pltpu.CompilerParams(vmem_limit_bytes=VMEM_BYTES),
        cost_estimate=pl.CostEstimate(
            flops=4 * chunk_rows * width * (halo_rows + chunk_rows) // 2,
            bytes_accessed=4 * chunk_rows * width,
            transcendentals=chunk_rows * heads * (halo_rows + chunk_rows),
        ),
    )(first, bounds, query, starts, halo, kv)


def after(block, *others):
    space = pl.BlockSpec(memory_space=pl.ANY)
    return pl.pallas_call(
        lambda *refs: None,
        out_shape=jax.ShapeDtypeStruct(block.shape, block.dtype),
        in_specs=[space] * (1 + len(others)),
        out_specs=space,
        input_output_aliases={0: 0},
    )(block, *others)


def per_device(group, lines, cores, tokens, lengths, w_query, w_key, w_value):
    row_count, depth = tokens.shape
    slice_rows = w_query.shape[0]
    index = lax.axis_index("ca")
    mine, line = index % group, index // group
    core = lax.axis_index("tp")
    q_width = w_query.shape[1] // group
    one_width = w_key.shape[1] // group
    kv_width = 2 * one_width
    kv_heads = one_width // HEAD_DIM
    group_rows = group * row_count
    devices = range(group * lines)

    def slice_for(target):
        return jnp.concatenate(
            [
                lax.dynamic_slice_in_dim(w_query, target * q_width, q_width, 1),
                lax.dynamic_slice_in_dim(w_key, target * one_width, one_width, 1),
                lax.dynamic_slice_in_dim(w_value, target * one_width, one_width, 1),
            ],
            axis=1,
        )

    def to_partner(block, step):
        return lax.ppermute(block, "ca", [(i, i ^ step) for i in devices])

    def along_lines(block):
        lanes = [[place + group * i for i in range(lines)] for place in range(group)]
        return lax.all_gather(block, "ca", axis=0, tiled=True, axis_index_groups=lanes)

    def forwarded(block):
        return lax.ppermute(block, "ca", [(i, (i + group) % (group * lines)) for i in devices])

    def gathered(array, column, members):
        if group == 1:
            return (array, column, [(0, array.shape[0], lambda s: 0)])
        pieces = []
        for at in range(lines):
            for number, step in enumerate(members):
                source = (at * len(members) + number) * slice_rows
                pieces.append((source, slice_rows, lambda s, at=at, step=step: (at * group + (s[0] ^ step)) * slice_rows))
        return (array, column, pieces)

    def from_lines(held, members):
        entries = []
        for back, array in enumerate(held):
            pieces = []
            for number, step in enumerate(members):

                def target(s, back=back, step=step):
                    at = lax.rem(s[1] - back + lines, lines)
                    return (at * group + (s[0] ^ step)) * slice_rows

                pieces.append((number * slice_rows, slice_rows, target))
            entries.append((array, 0, pieces))
        return entries

    own_slices = along_lines(slice_for(mine))
    half = row_count // 2
    halo_rows = REACH * row_count
    tiles = row_count // TILE

    def tables():
        row_ids = line * group_rows + jnp.arange(group_rows, dtype=jnp.int32)
        starts = doc_starts(lengths, row_ids)
        window_starts = starts - (line * group_rows - halo_rows)
        places = jnp.arange(group * tiles, dtype=jnp.int32) * TILE
        first = window_starts.reshape(group * tiles, TILE)
        bounds = jnp.stack([places, first[:, 0], first[:, -1]])
        cosine, sine = rope_tables(row_ids - starts)
        return cosine, sine, window_starts[:, None], bounds

    place = jnp.stack([mine, line, core]).astype(jnp.int32)
    token_parts = [
        (tokens, [lambda s, i=i: s[0] * row_count + i * half for i in range(row_count // half)]),
    ]
    if group > 1:
        others = range(1, group)
        arrived = [to_partner(slice_for(mine ^ step), step) for step in others]
        split = q_width // 2
        rest_kv = along_lines(jnp.concatenate([a[:, q_width:] for a in arrived]))
        rest_first = jnp.concatenate([a[:, :split] for a in arrived])
        rest_second = along_lines(jnp.concatenate([a[:, split:q_width] for a in arrived]))
        both = ("ca", "tp")

        def cross(block, steps):
            pairs = [(i * 2 + c, (i ^ steps[c]) * 2 + c) for i in devices for c in range(2)]
            return lax.ppermute(block, both, pairs)

        def swap(block):
            return lax.ppermute(block, both, [(i * 2 + c, i * 2 + 1 - c) for i in devices for c in range(2)])

        begin = core * half

        def share_tokens(tokens, rest_first):
            held = [rest_first]
            for _ in range(1, lines):
                held.append(forwarded(held[-1]))
            own_half = lax.dynamic_slice_in_dim(tokens, begin, half, 0)
            near = cross(own_half, (1, 2))
            other = cross(own_half, (2, 1))
            lists = tables()
            near = after(near, held[-2], *lists)
            far = cross(near, (2, 1))
            near = after(near, held[-1])
            return tuple((block, swap(block)) for block in (near, other, far)), lists, tuple(held[1:])

        def no_tokens(tokens, rest_first):
            nothing = tuple(jnp.zeros(t.shape, t.dtype) for t in jax.eval_shape(tables))
            blank = tuple((jnp.zeros((half, depth), tokens.dtype),) * 2 for _ in range(3))
            return blank, nothing, (jnp.zeros_like(rest_first),) * (lines - 1)

        known = sum(a[0, 0].astype(jnp.float32) for a in arrived)
        blocks, known_tables, held = lax.cond(known == known, share_tokens, no_tokens, tokens, rest_first)
        kv_weights = [gathered(own_slices, q_width, [0]), gathered(rest_kv, 0, others)]
        q_weights = [
            [gathered(own_slices, 0, [0])] + from_lines((rest_first, *held), others),
            [gathered(own_slices, split, [0]), gathered(rest_second, 0, others)],
        ]
        for (block, other_half), steps in zip(blocks, ((1, 2), (2, 1), (3, 3))):

            def here(s, steps=steps):
                return (s[0] ^ jnp.where(s[2] == 0, steps[0], steps[1])) * row_count + s[2] * half

            def mate(s, steps=steps):
                return (s[0] ^ jnp.where(s[2] == 0, steps[1], steps[0])) * row_count + (1 - s[2]) * half

            token_parts += [(block, [here]), (other_half, [mate])]
    else:
        known_tables = tables()
        split = q_width
        kv_weights = [gathered(own_slices, q_width, [0])]
        q_weights = [[gathered(own_slices, 0, [0])]]

    cosine, sine, window_starts, bounds = known_tables
    kv = project(place, token_parts, kv_weights, kv_width, cosine, sine, kv_heads)

    hops = -(-halo_rows // group_rows)
    pieces, moving = [], kv
    for hop in range(hops):
        keep = min(halo_rows - hop * group_rows, group_rows)
        moving = moving[moving.shape[0] - keep :]
        moving = lax.ppermute(moving, "ca", [(i, i + group) for i in devices if i + group in devices])
        pieces.insert(0, moving)
    halo = pieces[0] if len(pieces) == 1 else jnp.concatenate(pieces)

    result = jnp.zeros((row_count, w_query.shape[1]), jnp.bfloat16)
    for number, weights in enumerate(q_weights):
        query = project(place, token_parts, weights, split, cosine, sine, split // HEAD_DIM)
        for step in reversed(range(group)):
            part = attend(mine ^ step, row_count, query, window_starts, bounds, halo, kv, kv_heads)
            if step > 0:
                part = to_partner(part, step)
            elif group == 1:
                return part
            result = lax.dynamic_update_slice_in_dim(result, part, (mine ^ step) * q_width + number * split, 1)
    return result


def solution(mesh):
    size, cores = mesh.shape["ca"], mesh.shape["tp"]
    local_kv = KV_HEADS // cores
    group = 4 if cores == 2 and local_kv == 4 and size % 4 == 0 else 1
    placed = (P("ca", None), P(), P("ca", "tp"), P("ca", "tp"), P("ca", "tp"))
    body = functools.partial(per_device, group, size // group, cores)
    return jax.shard_map(body, mesh=mesh, in_specs=placed, out_specs=P("ca", "tp"), check_vma=False)
```

```python
import functools
import math

import jax
import jax.numpy as jnp
from jax import lax
from jax.experimental import pallas as pl
from jax.experimental.pallas import tpu as pltpu
from jax.sharding import PartitionSpec as P

HEADS = 32
KV_HEADS = 8
HEAD_DIM = 128
REACH = 3
ROPE_THETA = 500000.0
LOGIT_CAP = 5.0
TILE = 256
PROJECT_BYTES = 30 * 1024 * 1024
VMEM_BYTES = 48 * 1024 * 1024


def doc_starts(lengths, positions):
    doc_ends = jnp.cumsum(lengths).astype(jnp.int32)
    before = doc_ends[None, :] <= positions[:, None]
    return jnp.max(jnp.where(before, doc_ends[None, :], 0), axis=1).astype(jnp.int32)


def rope_tables(offsets):
    half_dim = HEAD_DIM // 2
    frequency = ROPE_THETA ** (-(jnp.arange(half_dim, dtype=jnp.float32) * 2.0) / HEAD_DIM)
    angles = offsets.astype(jnp.float32)[:, None] * frequency[None, :]
    cosine, sine = jnp.cos(angles), jnp.sin(angles)
    return jnp.concatenate([cosine, cosine], axis=1), jnp.concatenate([-sine, sine], axis=1)


def rotated(values, cosine, sine):
    return values * cosine + pltpu.roll(values, HEAD_DIM // 2, 1) * sine


def project_kernel(rope_heads, layout, place, x_ref, *refs):
    w_refs = refs[: len(layout)]
    cos_ref, sin_ref, out_ref, w_all = refs[len(layout) :]

    @pl.when(pl.program_id(0) == 0)
    def _():
        for ref, (_, column, pieces) in zip(w_refs, layout):
            columns = slice(column, column + ref.shape[1])
            for source, rows, target in pieces:
                at = pl.multiple_of(target(place), rows)
                w_all[pl.ds(at, rows), columns] = ref[source : source + rows, :]

    total = jnp.dot(x_ref[...], w_all[...], preferred_element_type=jnp.float32)
    cosine, sine = cos_ref[...], sin_ref[...]
    for head in range(out_ref.shape[1] // HEAD_DIM):
        columns = slice(head * HEAD_DIM, (head + 1) * HEAD_DIM)
        part = total[:, columns]
        if head < rope_heads:
            part = rotated(part, cosine, sine)
        out_ref[:, columns] = part.astype(out_ref.dtype)


def project(place, tokens, weights, width, cosine, sine, rope_heads):
    rows, depth = tokens.shape
    tile = min(512, rows)
    arrays, blocks, layout = [], [], []
    for array, (block, columns), column, pieces in weights:
        arrays.append(array)
        blocks.append(pl.BlockSpec((array.shape[0], columns), lambda i, s, block=block: (0, block)))
        layout.append((array, column, pieces))
    layout = [(None, column, pieces) for _, column, pieces in layout]
    return pl.pallas_call(
        functools.partial(project_kernel, rope_heads, layout),
        out_shape=jax.ShapeDtypeStruct((rows, width), jnp.bfloat16),
        grid_spec=pltpu.PrefetchScalarGridSpec(
            num_scalar_prefetch=1,
            grid=(rows // tile,),
            in_specs=[pl.BlockSpec((tile, depth), lambda i, s: (i, 0))]
            + blocks
            + [pl.BlockSpec((tile, HEAD_DIM), lambda i, s: (i, 0))] * 2,
            out_specs=pl.BlockSpec((tile, width), lambda i, s: (i, 0)),
            scratch_shapes=[pltpu.VMEM((depth, width), tokens.dtype)],
        ),
        compiler_params=pltpu.CompilerParams(vmem_limit_bytes=PROJECT_BYTES),
        cost_estimate=pl.CostEstimate(
            flops=2 * rows * depth * width, bytes_accessed=2 * depth * (rows + width), transcendentals=0
        ),
    )(place, tokens, *arrays, cosine, sine)


def put_kernel(targets, place, *refs):
    sems, out_ref = refs[-1], refs[-2]
    copies = []
    for number, (ref, target) in enumerate(zip(refs, targets)):
        rows = ref.shape[0]
        at = pl.multiple_of(target(place), rows)
        copies.append(pltpu.make_async_copy(ref, out_ref.at[pl.ds(at, rows), :], sems.at[number]))
        copies[-1].start()
    for copy in copies:
        copy.wait()


def put(place, rows, blocks, into=None):
    arrays, targets = [block for block, _ in blocks], [target for _, target in blocks]
    space = pl.BlockSpec(memory_space=pl.ANY)
    aliases = {}
    if into is not None:
        aliases = {1 + len(arrays): 0}
        arrays.append(into)
    return pl.pallas_call(
        functools.partial(put_kernel, targets),
        out_shape=jax.ShapeDtypeStruct((rows, arrays[0].shape[1]), arrays[0].dtype),
        in_specs=[pl.BlockSpec(memory_space=pltpu.SMEM)] + [space] * len(arrays),
        out_specs=space,
        scratch_shapes=[pltpu.SemaphoreType.DMA((len(targets),))],
        input_output_aliases=aliases,
    )(place, *arrays)


def attend_kernel(kv_heads, share, halo_rows, first, bounds, q_ref, start_ref, halo_ref, kv_ref, out_ref, kv_all, sums, totals):
    tile_index = pl.program_id(0)

    @pl.when(tile_index == 0)
    def _():
        kv_all[:halo_rows, :] = halo_ref[...]
        kv_all[halo_rows:, :] = kv_ref[...]

    tile = q_ref.shape[0]
    place = bounds[0, first[0] + tile_index]
    first_start = bounds[1, first[0] + tile_index]
    last_start = bounds[2, first[0] + tile_index]
    q_first = halo_rows + place
    first_block = first_start // TILE
    last_block = (q_first + tile - 1) // TILE
    sums[...] = jnp.zeros_like(sums)
    totals[...] = jnp.zeros_like(totals)
    inner = 1.0 / (math.sqrt(HEAD_DIM) * LOGIT_CAP)
    outer = LOGIT_CAP * math.log2(math.e)

    def block_step(block, masked):
        rows = pl.ds(pl.multiple_of(block * TILE, TILE), TILE)
        if masked:
            k_ids = block * TILE + lax.broadcasted_iota(jnp.int32, (tile, TILE), 1)
            q_ids = q_first + lax.broadcasted_iota(jnp.int32, (tile, TILE), 0)
            allowed = (k_ids <= q_ids) & (k_ids >= start_ref[...])
        for kv_head in range(kv_heads):
            keys = kv_all[rows, kv_head * HEAD_DIM : (kv_head + 1) * HEAD_DIM]
            at = (kv_heads + kv_head) * HEAD_DIM
            values = kv_all[rows, at : at + HEAD_DIM]
            for member in range(share):
                head = kv_head * share + member
                query = q_ref[:, head * HEAD_DIM : (head + 1) * HEAD_DIM]
                raw = lax.dot_general(query, keys, (((1,), (1,)), ((), ())), preferred_element_type=jnp.float32)
                weights = jnp.exp2(outer * jnp.tanh(raw * inner))
                if masked:
                    weights = jnp.where(allowed, weights, 0.0)
                partial = weights[:, :HEAD_DIM]
                for part in range(1, TILE // HEAD_DIM):
                    partial = partial + weights[:, part * HEAD_DIM : (part + 1) * HEAD_DIM]
                totals[head] += partial
                sums[head] += jnp.dot(weights.astype(jnp.bfloat16), values, preferred_element_type=jnp.float32)

    def either(block, carry):
        begin = block * TILE
        whole = (begin >= last_start) & (begin + TILE - 1 <= q_first)

        @pl.when(whole)
        def _():
            block_step(block, False)

        @pl.when(jnp.logical_not(whole))
        def _():
            block_step(block, True)

        return carry

    lax.fori_loop(first_block, last_block + 1, either, 0)
    for head in range(kv_heads * share):
        denominator = jnp.sum(totals[head], axis=1, keepdims=True)
        out_ref[:, head * HEAD_DIM : (head + 1) * HEAD_DIM] = (sums[head] / denominator).astype(out_ref.dtype)


def attend(chunk, chunk_rows, query, starts, bounds, halo, kv, kv_heads):
    width = query.shape[1]
    heads = width // HEAD_DIM
    halo_rows = halo.shape[0]
    tiles = chunk_rows // TILE
    first = (chunk * tiles).reshape(1).astype(jnp.int32)
    kernel = functools.partial(attend_kernel, kv_heads, heads // kv_heads, halo_rows)
    return pl.pallas_call(
        kernel,
        out_shape=jax.ShapeDtypeStruct((chunk_rows, width), jnp.bfloat16),
        grid_spec=pltpu.PrefetchScalarGridSpec(
            num_scalar_prefetch=2,
            grid=(tiles,),
            in_specs=[
                pl.BlockSpec((TILE, width), lambda i, c, s: (c[0] + i, 0)),
                pl.BlockSpec((TILE, 1), lambda i, c, s: (c[0] + i, 0)),
                pl.BlockSpec(halo.shape, lambda i, c, s: (0, 0)),
                pl.BlockSpec(kv.shape, lambda i, c, s: (0, 0)),
            ],
            out_specs=pl.BlockSpec((TILE, width), lambda i, c, s: (i, 0)),
            scratch_shapes=[
                pltpu.VMEM((halo_rows + kv.shape[0], kv.shape[1]), jnp.bfloat16),
                pltpu.VMEM((heads, TILE, HEAD_DIM), jnp.float32),
                pltpu.VMEM((heads, TILE, HEAD_DIM), jnp.float32),
            ],
        ),
        compiler_params=pltpu.CompilerParams(vmem_limit_bytes=VMEM_BYTES),
        cost_estimate=pl.CostEstimate(
            flops=4 * chunk_rows * width * (halo_rows + chunk_rows) // 2,
            bytes_accessed=4 * chunk_rows * width,
            transcendentals=chunk_rows * heads * (halo_rows + chunk_rows),
        ),
    )(first, bounds, query, starts, halo, kv)


def after(block, *others):
    space = pl.BlockSpec(memory_space=pl.ANY)
    return pl.pallas_call(
        lambda *refs: None,
        out_shape=jax.ShapeDtypeStruct(block.shape, block.dtype),
        in_specs=[space] * (1 + len(others)),
        out_specs=space,
        input_output_aliases={0: 0},
    )(block, *others)


def per_device(group, lines, cores, tokens, lengths, w_query, w_key, w_value):
    row_count, depth = tokens.shape
    slice_rows = w_query.shape[0]
    index = lax.axis_index("ca")
    mine, line = index % group, index // group
    core = lax.axis_index("tp")
    q_width = w_query.shape[1] // group
    one_width = w_key.shape[1] // group
    kv_width = 2 * one_width
    kv_heads = one_width // HEAD_DIM
    group_rows = group * row_count
    devices = range(group * lines)

    def slice_for(target):
        return jnp.concatenate(
            [
                lax.dynamic_slice_in_dim(w_query, target * q_width, q_width, 1),
                lax.dynamic_slice_in_dim(w_key, target * one_width, one_width, 1),
                lax.dynamic_slice_in_dim(w_value, target * one_width, one_width, 1),
            ],
            axis=1,
        )

    def to_partner(block, step):
        return lax.ppermute(block, "ca", [(i, i ^ step) for i in devices])

    def along_lines(block):
        lanes = [[place + group * i for i in range(lines)] for place in range(group)]
        return lax.all_gather(block, "ca", axis=0, tiled=True, axis_index_groups=lanes)

    def forwarded(block):
        return lax.ppermute(block, "ca", [(i, (i + group) % (group * lines)) for i in devices])

    def gathered(array, block, column, members):
        if group == 1:
            return (array, block, column, [(0, array.shape[0], lambda s: 0)])
        pieces = []
        for at in range(lines):
            for number, step in enumerate(members):
                source = (at * len(members) + number) * slice_rows
                pieces.append((source, slice_rows, lambda s, at=at, step=step: (at * group + (s[0] ^ step)) * slice_rows))
        return (array, block, column, pieces)

    def from_lines(held, column, members):
        entries = []
        for back, array in enumerate(held):
            pieces = []
            for number, step in enumerate(members):

                def target(s, back=back, step=step):
                    at = lax.rem(s[1] - back + lines, lines)
                    return (at * group + (s[0] ^ step)) * slice_rows

                pieces.append((number * slice_rows, slice_rows, target))
            entries.append((array, (0, array.shape[1]), column, pieces))
        return entries

    own_slices = along_lines(slice_for(mine))
    half = row_count // 2
    halo_rows = REACH * row_count
    tiles = row_count // TILE

    def tables():
        row_ids = line * group_rows + jnp.arange(group_rows, dtype=jnp.int32)
        starts = doc_starts(lengths, row_ids)
        window_starts = starts - (line * group_rows - halo_rows)
        places = jnp.arange(group * tiles, dtype=jnp.int32) * TILE
        first = window_starts.reshape(group * tiles, TILE)
        bounds = jnp.stack([places, first[:, 0], first[:, -1]])
        cosine, sine = rope_tables(row_ids - starts)
        return cosine, sine, window_starts[:, None], bounds

    place = jnp.stack([mine, line, core]).astype(jnp.int32)
    if group > 1:
        others = range(1, group)
        arrived = [to_partner(slice_for(mine ^ step), step) for step in others]
        split = q_width // 2
        rest_kv = along_lines(jnp.concatenate([a[:, q_width:] for a in arrived]))
        rest_first = jnp.concatenate([a[:, :split] for a in arrived])
        rest_second = along_lines(jnp.concatenate([a[:, split:q_width] for a in arrived]))
        both = ("ca", "tp")

        def cross(block, steps):
            pairs = [(i * 2 + c, (i ^ steps[c]) * 2 + c) for i in devices for c in range(2)]
            return lax.ppermute(block, both, pairs)

        def swap(block):
            return lax.ppermute(block, both, [(i * 2 + c, i * 2 + 1 - c) for i in devices for c in range(2)])

        begin = core * half

        own_half = lax.dynamic_slice_in_dim(tokens, begin, half, 0)

        def home(step_even, step_odd, mate):
            def target(s):
                step = jnp.where(s[2] == mate, step_even, step_odd)
                return (s[0] ^ step) * row_count + jnp.where(mate == 0, s[2], 1 - s[2]) * half

            return target

        def share_tokens(tokens, own_half, rest_first):
            held = [rest_first]
            for _ in range(1, lines):
                held.append(forwarded(held[-1]))
            near = cross(own_half, (1, 2))
            other = cross(own_half, (2, 1))
            lists = tables()
            everything = put(place, group_rows, [(tokens, lambda s: s[0] * row_count)])
            near = after(near, held[-2], *lists, everything)
            far = cross(near, (2, 1))
            near = after(near, held[-1])
            mates = [swap(block) for block in (near, other, far)]
            first = [(near, home(1, 2, 0)), (mates[0], home(1, 2, 1)), (other, home(2, 1, 0)), (mates[1], home(2, 1, 1))]
            everything = put(place, group_rows, first, everything)
            last = [(far, home(3, 3, 0)), (mates[2], home(3, 3, 1))]
            everything = put(place, group_rows, last, everything)
            return everything, lists, tuple(held[1:])

        def no_tokens(tokens, own_half, rest_first):
            nothing = tuple(jnp.zeros(t.shape, t.dtype) for t in jax.eval_shape(tables))
            blank = jnp.zeros((group_rows, depth), tokens.dtype)
            return blank, nothing, (jnp.zeros_like(rest_first),) * (lines - 1)

        known = sum(a[0, 0].astype(jnp.float32) for a in arrived)
        all_tokens, known_tables, held = lax.cond(
            known == known, share_tokens, no_tokens, tokens, own_half, rest_first
        )
        kv_block = (q_width // kv_width, kv_width)
        kv_weights = [gathered(own_slices, kv_block, 0, [0]), gathered(rest_kv, (0, kv_width), 0, others)]
        q_weights = [gathered(own_slices, (0, q_width), 0, [0])] + from_lines((rest_first, *held), 0, others)
        q_weights.append(gathered(rest_second, (0, q_width - split), split, others))
    else:
        all_tokens, known_tables = tokens, tables()
        kv_weights = [gathered(own_slices, (q_width // kv_width, kv_width), 0, [0])]
        q_weights = [gathered(own_slices, (0, q_width), 0, [0])]

    cosine, sine, window_starts, bounds = known_tables
    kv = project(place, all_tokens, kv_weights, kv_width, cosine, sine, kv_heads)

    hops = -(-halo_rows // group_rows)
    pieces, moving = [], kv
    for hop in range(hops):
        keep = min(halo_rows - hop * group_rows, group_rows)
        moving = moving[moving.shape[0] - keep :]
        moving = lax.ppermute(moving, "ca", [(i, i + group) for i in devices if i + group in devices])
        pieces.insert(0, moving)
    halo = pieces[0] if len(pieces) == 1 else jnp.concatenate(pieces)

    query = project(place, all_tokens, q_weights, q_width, cosine, sine, q_width // HEAD_DIM)
    result = jnp.zeros((row_count, w_query.shape[1]), jnp.bfloat16)
    for step in reversed(range(group)):
        part = attend(mine ^ step, row_count, query, window_starts, bounds, halo, kv, kv_heads)
        if step > 0:
            part = to_partner(part, step)
        elif group == 1:
            return part
        result = lax.dynamic_update_slice_in_dim(result, part, (mine ^ step) * q_width, 1)
    return result


def solution(mesh):
    size, cores = mesh.shape["ca"], mesh.shape["tp"]
    local_kv = KV_HEADS // cores
    group = 4 if cores == 2 and local_kv == 4 and size % 4 == 0 else 1
    placed = (P("ca", None), P(), P("ca", "tp"), P("ca", "tp"), P("ca", "tp"))
    body = functools.partial(per_device, group, size // group, cores)
    return jax.shard_map(body, mesh=mesh, in_specs=placed, out_specs=P("ca", "tp"), check_vma=False)
```

```python
import functools
import math

import jax
import jax.numpy as jnp
from jax import lax
from jax.experimental import pallas as pl
from jax.experimental.pallas import tpu as pltpu
from jax.sharding import PartitionSpec as P

HEADS = 32
KV_HEADS = 8
HEAD_DIM = 128
REACH = 3
ROPE_THETA = 500000.0
LOGIT_CAP = 5.0
TILE = 256
PUT_BYTES = 20 * 1024 * 1024
PROJECT_BYTES = 30 * 1024 * 1024
VMEM_BYTES = 48 * 1024 * 1024


def doc_starts(lengths, positions):
    doc_ends = jnp.cumsum(lengths).astype(jnp.int32)
    before = doc_ends[None, :] <= positions[:, None]
    return jnp.max(jnp.where(before, doc_ends[None, :], 0), axis=1).astype(jnp.int32)


def rope_tables(offsets):
    half_dim = HEAD_DIM // 2
    frequency = ROPE_THETA ** (-(jnp.arange(half_dim, dtype=jnp.float32) * 2.0) / HEAD_DIM)
    angles = offsets.astype(jnp.float32)[:, None] * frequency[None, :]
    cosine, sine = jnp.cos(angles), jnp.sin(angles)
    return jnp.concatenate([cosine, cosine], axis=1), jnp.concatenate([-sine, sine], axis=1)


def rotated(values, cosine, sine):
    return values * cosine + pltpu.roll(values, HEAD_DIM // 2, 1) * sine


def project_kernel(rope_heads, layout, place, x_ref, *refs):
    w_refs = refs[: len(layout)]
    cos_ref, sin_ref, out_ref, w_all = refs[len(layout) :]

    @pl.when(pl.program_id(0) == 0)
    def _():
        for ref, (_, column, pieces) in zip(w_refs, layout):
            columns = slice(column, column + ref.shape[1])
            for source, rows, target in pieces:
                at = pl.multiple_of(target(place), rows)
                w_all[pl.ds(at, rows), columns] = ref[source : source + rows, :]

    total = jnp.dot(x_ref[...], w_all[...], preferred_element_type=jnp.float32)
    cosine, sine = cos_ref[...], sin_ref[...]
    for head in range(out_ref.shape[1] // HEAD_DIM):
        columns = slice(head * HEAD_DIM, (head + 1) * HEAD_DIM)
        part = total[:, columns]
        if head < rope_heads:
            part = rotated(part, cosine, sine)
        out_ref[:, columns] = part.astype(out_ref.dtype)


def project(place, tokens, weights, width, cosine, sine, rope_heads):
    rows, depth = tokens.shape
    tile = min(512, rows)
    arrays, blocks, layout = [], [], []
    for array, (block, columns), column, pieces in weights:
        arrays.append(array)
        blocks.append(pl.BlockSpec((array.shape[0], columns), lambda i, s, block=block: (0, block)))
        layout.append((array, column, pieces))
    layout = [(None, column, pieces) for _, column, pieces in layout]
    return pl.pallas_call(
        functools.partial(project_kernel, rope_heads, layout),
        out_shape=jax.ShapeDtypeStruct((rows, width), jnp.bfloat16),
        grid_spec=pltpu.PrefetchScalarGridSpec(
            num_scalar_prefetch=1,
            grid=(rows // tile,),
            in_specs=[pl.BlockSpec((tile, depth), lambda i, s: (i, 0))]
            + blocks
            + [pl.BlockSpec((tile, HEAD_DIM), lambda i, s: (i, 0))] * 2,
            out_specs=pl.BlockSpec((tile, width), lambda i, s: (i, 0)),
            scratch_shapes=[pltpu.VMEM((depth, width), tokens.dtype)],
        ),
        compiler_params=pltpu.CompilerParams(vmem_limit_bytes=PROJECT_BYTES),
        cost_estimate=pl.CostEstimate(
            flops=2 * rows * depth * width, bytes_accessed=2 * depth * (rows + width), transcendentals=0
        ),
    )(place, tokens, *arrays, cosine, sine)


def put_kernel(targets, place, *refs):
    sems, out_ref = refs[-1], refs[-2]
    copies = []
    for number, (ref, target) in enumerate(zip(refs, targets)):
        rows = ref.shape[0]
        at = pl.multiple_of(target(place), rows)
        copies.append(pltpu.make_async_copy(ref, out_ref.at[pl.ds(at, rows), :], sems.at[number]))
        copies[-1].start()
    for copy in copies:
        copy.wait()


def put(place, rows, blocks, into=None):
    arrays, targets = [block for block, _ in blocks], [target for _, target in blocks]
    spaces = [pl.BlockSpec(memory_space=pltpu.SMEM)] + [pl.BlockSpec(memory_space=pltpu.VMEM)] * len(arrays)
    aliases = {}
    if into is not None:
        aliases = {1 + len(arrays): 0}
        arrays.append(into)
        spaces.append(pl.BlockSpec(memory_space=pl.ANY))
    return pl.pallas_call(
        functools.partial(put_kernel, targets),
        out_shape=jax.ShapeDtypeStruct((rows, arrays[0].shape[1]), arrays[0].dtype),
        in_specs=spaces,
        out_specs=pl.BlockSpec(memory_space=pl.ANY),
        scratch_shapes=[pltpu.SemaphoreType.DMA((len(targets),))],
        input_output_aliases=aliases,
        compiler_params=pltpu.CompilerParams(vmem_limit_bytes=PUT_BYTES),
    )(place, *arrays)


def attend_kernel(kv_heads, share, halo_rows, first, bounds, q_ref, start_ref, halo_ref, kv_ref, out_ref, kv_all, sums, totals):
    tile_index = pl.program_id(0)

    @pl.when(tile_index == 0)
    def _():
        kv_all[:halo_rows, :] = halo_ref[...]
        kv_all[halo_rows:, :] = kv_ref[...]

    tile = q_ref.shape[0]
    place = bounds[0, first[0] + tile_index]
    first_start = bounds[1, first[0] + tile_index]
    last_start = bounds[2, first[0] + tile_index]
    q_first = halo_rows + place
    first_block = first_start // TILE
    last_block = (q_first + tile - 1) // TILE
    sums[...] = jnp.zeros_like(sums)
    totals[...] = jnp.zeros_like(totals)
    inner = 1.0 / (math.sqrt(HEAD_DIM) * LOGIT_CAP)
    outer = LOGIT_CAP * math.log2(math.e)

    def block_step(block, masked):
        rows = pl.ds(pl.multiple_of(block * TILE, TILE), TILE)
        if masked:
            k_ids = block * TILE + lax.broadcasted_iota(jnp.int32, (tile, TILE), 1)
            q_ids = q_first + lax.broadcasted_iota(jnp.int32, (tile, TILE), 0)
            allowed = (k_ids <= q_ids) & (k_ids >= start_ref[...])
        for kv_head in range(kv_heads):
            keys = kv_all[rows, kv_head * HEAD_DIM : (kv_head + 1) * HEAD_DIM]
            at = (kv_heads + kv_head) * HEAD_DIM
            values = kv_all[rows, at : at + HEAD_DIM]
            for member in range(share):
                head = kv_head * share + member
                query = q_ref[:, head * HEAD_DIM : (head + 1) * HEAD_DIM]
                raw = lax.dot_general(query, keys, (((1,), (1,)), ((), ())), preferred_element_type=jnp.float32)
                weights = jnp.exp2(outer * jnp.tanh(raw * inner))
                if masked:
                    weights = jnp.where(allowed, weights, 0.0)
                partial = weights[:, :HEAD_DIM]
                for part in range(1, TILE // HEAD_DIM):
                    partial = partial + weights[:, part * HEAD_DIM : (part + 1) * HEAD_DIM]
                totals[head] += partial
                sums[head] += jnp.dot(weights.astype(jnp.bfloat16), values, preferred_element_type=jnp.float32)

    def either(block, carry):
        begin = block * TILE
        whole = (begin >= last_start) & (begin + TILE - 1 <= q_first)

        @pl.when(whole)
        def _():
            block_step(block, False)

        @pl.when(jnp.logical_not(whole))
        def _():
            block_step(block, True)

        return carry

    lax.fori_loop(first_block, last_block + 1, either, 0)
    for head in range(kv_heads * share):
        denominator = jnp.sum(totals[head], axis=1, keepdims=True)
        out_ref[:, head * HEAD_DIM : (head + 1) * HEAD_DIM] = (sums[head] / denominator).astype(out_ref.dtype)


def attend(chunk, chunk_rows, query, starts, bounds, halo, kv, kv_heads):
    width = query.shape[1]
    heads = width // HEAD_DIM
    halo_rows = halo.shape[0]
    tiles = chunk_rows // TILE
    first = (chunk * tiles).reshape(1).astype(jnp.int32)
    kernel = functools.partial(attend_kernel, kv_heads, heads // kv_heads, halo_rows)
    return pl.pallas_call(
        kernel,
        out_shape=jax.ShapeDtypeStruct((chunk_rows, width), jnp.bfloat16),
        grid_spec=pltpu.PrefetchScalarGridSpec(
            num_scalar_prefetch=2,
            grid=(tiles,),
            in_specs=[
                pl.BlockSpec((TILE, width), lambda i, c, s: (c[0] + i, 0)),
                pl.BlockSpec((TILE, 1), lambda i, c, s: (c[0] + i, 0)),
                pl.BlockSpec(halo.shape, lambda i, c, s: (0, 0)),
                pl.BlockSpec(kv.shape, lambda i, c, s: (0, 0)),
            ],
            out_specs=pl.BlockSpec((TILE, width), lambda i, c, s: (i, 0)),
            scratch_shapes=[
                pltpu.VMEM((halo_rows + kv.shape[0], kv.shape[1]), jnp.bfloat16),
                pltpu.VMEM((heads, TILE, HEAD_DIM), jnp.float32),
                pltpu.VMEM((heads, TILE, HEAD_DIM), jnp.float32),
            ],
        ),
        compiler_params=pltpu.CompilerParams(vmem_limit_bytes=VMEM_BYTES),
        cost_estimate=pl.CostEstimate(
            flops=4 * chunk_rows * width * (halo_rows + chunk_rows) // 2,
            bytes_accessed=4 * chunk_rows * width,
            transcendentals=chunk_rows * heads * (halo_rows + chunk_rows),
        ),
    )(first, bounds, query, starts, halo, kv)


def after(block, *others):
    space = pl.BlockSpec(memory_space=pl.ANY)
    return pl.pallas_call(
        lambda *refs: None,
        out_shape=jax.ShapeDtypeStruct(block.shape, block.dtype),
        in_specs=[space] * (1 + len(others)),
        out_specs=space,
        input_output_aliases={0: 0},
    )(block, *others)


def per_device(group, lines, cores, tokens, lengths, w_query, w_key, w_value):
    row_count, depth = tokens.shape
    slice_rows = w_query.shape[0]
    index = lax.axis_index("ca")
    mine, line = index % group, index // group
    core = lax.axis_index("tp")
    q_width = w_query.shape[1] // group
    one_width = w_key.shape[1] // group
    kv_width = 2 * one_width
    kv_heads = one_width // HEAD_DIM
    group_rows = group * row_count
    devices = range(group * lines)

    def slice_for(target):
        return jnp.concatenate(
            [
                lax.dynamic_slice_in_dim(w_query, target * q_width, q_width, 1),
                lax.dynamic_slice_in_dim(w_key, target * one_width, one_width, 1),
                lax.dynamic_slice_in_dim(w_value, target * one_width, one_width, 1),
            ],
            axis=1,
        )

    def to_partner(block, step):
        return lax.ppermute(block, "ca", [(i, i ^ step) for i in devices])

    def along_lines(block):
        lanes = [[place + group * i for i in range(lines)] for place in range(group)]
        return lax.all_gather(block, "ca", axis=0, tiled=True, axis_index_groups=lanes)

    def forwarded(block):
        return lax.ppermute(block, "ca", [(i, (i + group) % (group * lines)) for i in devices])

    def gathered(array, block, column, members):
        if group == 1:
            return (array, block, column, [(0, array.shape[0], lambda s: 0)])
        pieces = []
        for at in range(lines):
            for number, step in enumerate(members):
                source = (at * len(members) + number) * slice_rows
                pieces.append((source, slice_rows, lambda s, at=at, step=step: (at * group + (s[0] ^ step)) * slice_rows))
        return (array, block, column, pieces)

    def from_lines(held, column, members):
        entries = []
        for back, array in enumerate(held):
            pieces = []
            for number, step in enumerate(members):

                def target(s, back=back, step=step):
                    at = lax.rem(s[1] - back + lines, lines)
                    return (at * group + (s[0] ^ step)) * slice_rows

                pieces.append((number * slice_rows, slice_rows, target))
            entries.append((array, (0, array.shape[1]), column, pieces))
        return entries

    own_slices = along_lines(slice_for(mine))
    half = row_count // 2
    halo_rows = REACH * row_count
    tiles = row_count // TILE

    def tables():
        row_ids = line * group_rows + jnp.arange(group_rows, dtype=jnp.int32)
        starts = doc_starts(lengths, row_ids)
        window_starts = starts - (line * group_rows - halo_rows)
        places = jnp.arange(group * tiles, dtype=jnp.int32) * TILE
        first = window_starts.reshape(group * tiles, TILE)
        bounds = jnp.stack([places, first[:, 0], first[:, -1]])
        cosine, sine = rope_tables(row_ids - starts)
        return cosine, sine, window_starts[:, None], bounds

    place = jnp.stack([mine, line, core]).astype(jnp.int32)
    if group > 1:
        others = range(1, group)
        arrived = [to_partner(slice_for(mine ^ step), step) for step in others]
        split = q_width // 2
        rest_kv = along_lines(jnp.concatenate([a[:, q_width:] for a in arrived]))
        rest_first = jnp.concatenate([a[:, :split] for a in arrived])
        rest_second = along_lines(jnp.concatenate([a[:, split:q_width] for a in arrived]))
        both = ("ca", "tp")

        def cross(block, steps):
            pairs = [(i * 2 + c, (i ^ steps[c]) * 2 + c) for i in devices for c in range(2)]
            return lax.ppermute(block, both, pairs)

        def swap(block):
            return lax.ppermute(block, both, [(i * 2 + c, i * 2 + 1 - c) for i in devices for c in range(2)])

        begin = core * half

        own_half = lax.dynamic_slice_in_dim(tokens, begin, half, 0)

        def home(step_even, step_odd, mate):
            def target(s):
                step = jnp.where(s[2] == mate, step_even, step_odd)
                return (s[0] ^ step) * row_count + jnp.where(mate == 0, s[2], 1 - s[2]) * half

            return target

        def share_tokens(tokens, own_half, rest_first):
            held = [rest_first]
            for _ in range(1, lines):
                held.append(forwarded(held[-1]))
            near = cross(own_half, (1, 2))
            other = cross(own_half, (2, 1))
            lists = tables()
            everything = put(place, group_rows, [(tokens, lambda s: s[0] * row_count)])
            near = after(near, held[-2], *lists, everything)
            far = cross(near, (2, 1))
            near = after(near, held[-1])
            mates = [swap(block) for block in (near, other, far)]
            first = [(near, home(1, 2, 0)), (mates[0], home(1, 2, 1)), (other, home(2, 1, 0)), (mates[1], home(2, 1, 1))]
            everything = put(place, group_rows, first, everything)
            last = [(far, home(3, 3, 0)), (mates[2], home(3, 3, 1))]
            everything = put(place, group_rows, last, everything)
            return everything, lists, tuple(held[1:])

        def no_tokens(tokens, own_half, rest_first):
            nothing = tuple(jnp.zeros(t.shape, t.dtype) for t in jax.eval_shape(tables))
            blank = jnp.zeros((group_rows, depth), tokens.dtype)
            return blank, nothing, (jnp.zeros_like(rest_first),) * (lines - 1)

        known = sum(a[0, 0].astype(jnp.float32) for a in arrived)
        all_tokens, known_tables, held = lax.cond(
            known == known, share_tokens, no_tokens, tokens, own_half, rest_first
        )
        kv_block = (q_width // kv_width, kv_width)
        kv_weights = [gathered(own_slices, kv_block, 0, [0]), gathered(rest_kv, (0, kv_width), 0, others)]
        q_weights = [gathered(own_slices, (0, q_width), 0, [0])] + from_lines((rest_first, *held), 0, others)
        q_weights.append(gathered(rest_second, (0, q_width - split), split, others))
    else:
        all_tokens, known_tables = tokens, tables()
        kv_weights = [gathered(own_slices, (q_width // kv_width, kv_width), 0, [0])]
        q_weights = [gathered(own_slices, (0, q_width), 0, [0])]

    cosine, sine, window_starts, bounds = known_tables
    kv = project(place, all_tokens, kv_weights, kv_width, cosine, sine, kv_heads)

    hops = -(-halo_rows // group_rows)
    pieces, moving = [], kv
    for hop in range(hops):
        keep = min(halo_rows - hop * group_rows, group_rows)
        moving = moving[moving.shape[0] - keep :]
        moving = lax.ppermute(moving, "ca", [(i, i + group) for i in devices if i + group in devices])
        pieces.insert(0, moving)
    halo = pieces[0] if len(pieces) == 1 else jnp.concatenate(pieces)

    query = project(place, all_tokens, q_weights, q_width, cosine, sine, q_width // HEAD_DIM)
    result = jnp.zeros((row_count, w_query.shape[1]), jnp.bfloat16)
    for step in reversed(range(group)):
        part = attend(mine ^ step, row_count, query, window_starts, bounds, halo, kv, kv_heads)
        if step > 0:
            part = to_partner(part, step)
        elif group == 1:
            return part
        result = lax.dynamic_update_slice_in_dim(result, part, (mine ^ step) * q_width, 1)
    return result


def solution(mesh):
    size, cores = mesh.shape["ca"], mesh.shape["tp"]
    local_kv = KV_HEADS // cores
    group = 4 if cores == 2 and local_kv == 4 and size % 4 == 0 else 1
    placed = (P("ca", None), P(), P("ca", "tp"), P("ca", "tp"), P("ca", "tp"))
    body = functools.partial(per_device, group, size // group, cores)
    return jax.shard_map(body, mesh=mesh, in_specs=placed, out_specs=P("ca", "tp"), check_vma=False)
```

```python
import functools
import math

import jax
import jax.numpy as jnp
from jax import lax
from jax.experimental import pallas as pl
from jax.experimental.pallas import tpu as pltpu
from jax.sharding import PartitionSpec as P

HEADS = 32
KV_HEADS = 8
HEAD_DIM = 128
REACH = 3
ROPE_THETA = 500000.0
LOGIT_CAP = 5.0
TILE = 256
PUT_BYTES = 20 * 1024 * 1024
PROJECT_BYTES = 30 * 1024 * 1024
VMEM_BYTES = 48 * 1024 * 1024


def doc_starts(lengths, positions):
    doc_ends = jnp.cumsum(lengths).astype(jnp.int32)
    before = doc_ends[None, :] <= positions[:, None]
    return jnp.max(jnp.where(before, doc_ends[None, :], 0), axis=1).astype(jnp.int32)


def rope_tables(offsets):
    half_dim = HEAD_DIM // 2
    frequency = ROPE_THETA ** (-(jnp.arange(half_dim, dtype=jnp.float32) * 2.0) / HEAD_DIM)
    angles = offsets.astype(jnp.float32)[:, None] * frequency[None, :]
    cosine, sine = jnp.cos(angles), jnp.sin(angles)
    return jnp.concatenate([cosine, cosine], axis=1), jnp.concatenate([-sine, sine], axis=1)


def rotated(values, cosine, sine):
    return values * cosine + pltpu.roll(values, HEAD_DIM // 2, 1) * sine


def project_kernel(rope_heads, layout, given, place, x_ref, *refs):
    w_refs = refs[: len(layout)]
    cos_ref, sin_ref = refs[len(layout) : len(layout) + 2]
    out_ref, w_all = refs[len(layout) + 2 + given :]

    @pl.when(pl.program_id(0) == 0)
    def _():
        for ref, (_, column, pieces) in zip(w_refs, layout):
            columns = slice(column, column + ref.shape[1])
            for source, rows, target in pieces:
                at = pl.multiple_of(target(place), rows)
                w_all[pl.ds(at, rows), columns] = ref[source : source + rows, :]

    total = jnp.dot(x_ref[...], w_all[...], preferred_element_type=jnp.float32)
    cosine, sine = cos_ref[...], sin_ref[...]
    for head in range(out_ref.shape[1] // HEAD_DIM):
        columns = slice(head * HEAD_DIM, (head + 1) * HEAD_DIM)
        part = total[:, columns]
        if head < rope_heads:
            part = rotated(part, cosine, sine)
        out_ref[:, columns] = part.astype(out_ref.dtype)


def project(group, place, tokens, weights, width, cosine, sine, rope_heads, span, into=None):
    rows, depth = tokens.shape
    first, count = span
    tile = rows // group
    arrays, blocks, layout = [], [], []
    for array, (block, columns), column, pieces in weights:
        arrays.append(array)
        blocks.append(pl.BlockSpec((array.shape[0], columns), lambda i, s, block=block: (0, block)))
        layout.append((None, column, pieces))

    def row_block(i, s):
        return (s[0] ^ (first + i), 0)

    given = [] if into is None else [into]
    return pl.pallas_call(
        functools.partial(project_kernel, rope_heads, layout, len(given)),
        out_shape=jax.ShapeDtypeStruct((rows, width), jnp.bfloat16),
        grid_spec=pltpu.PrefetchScalarGridSpec(
            num_scalar_prefetch=1,
            grid=(count,),
            in_specs=[pl.BlockSpec((tile, depth), row_block)]
            + blocks
            + [pl.BlockSpec((tile, HEAD_DIM), row_block)] * 2
            + [pl.BlockSpec(memory_space=pl.ANY)] * len(given),
            out_specs=pl.BlockSpec((tile, width), row_block),
            scratch_shapes=[pltpu.VMEM((depth, width), tokens.dtype)],
        ),
        input_output_aliases={} if into is None else {4 + len(arrays): 0},
        compiler_params=pltpu.CompilerParams(vmem_limit_bytes=PROJECT_BYTES),
        cost_estimate=pl.CostEstimate(
            flops=2 * count * tile * depth * width,
            bytes_accessed=2 * depth * (count * tile + width),
            transcendentals=0,
        ),
    )(place, tokens, *arrays, cosine, sine, *given)


def put_kernel(targets, place, *refs):
    sems, out_ref = refs[-1], refs[-2]
    copies = []
    for number, (ref, target) in enumerate(zip(refs, targets)):
        rows = ref.shape[0]
        at = pl.multiple_of(target(place), rows)
        copies.append(pltpu.make_async_copy(ref, out_ref.at[pl.ds(at, rows), :], sems.at[number]))
        copies[-1].start()
    for copy in copies:
        copy.wait()


def put(place, rows, blocks, into=None):
    arrays, targets = [block for block, _ in blocks], [target for _, target in blocks]
    spaces = [pl.BlockSpec(memory_space=pltpu.SMEM)] + [pl.BlockSpec(memory_space=pltpu.VMEM)] * len(arrays)
    aliases = {}
    if into is not None:
        aliases = {1 + len(arrays): 0}
        arrays.append(into)
        spaces.append(pl.BlockSpec(memory_space=pl.ANY))
    return pl.pallas_call(
        functools.partial(put_kernel, targets),
        out_shape=jax.ShapeDtypeStruct((rows, arrays[0].shape[1]), arrays[0].dtype),
        in_specs=spaces,
        out_specs=pl.BlockSpec(memory_space=pl.ANY),
        scratch_shapes=[pltpu.SemaphoreType.DMA((len(targets),))],
        input_output_aliases=aliases,
        compiler_params=pltpu.CompilerParams(vmem_limit_bytes=PUT_BYTES),
    )(place, *arrays)


def attend_kernel(kv_heads, share, halo_rows, first, bounds, ends, q_ref, halo_ref, kv_ref, out_ref, kv_all, sums, totals):
    tile_index = pl.program_id(0)

    @pl.when(tile_index == 0)
    def _():
        kv_all[:halo_rows, :] = halo_ref[...]
        kv_all[halo_rows:, :] = kv_ref[...]

    tile = q_ref.shape[0]
    place = bounds[0, first[0] + tile_index]
    first_start = bounds[1, first[0] + tile_index]
    last_start = bounds[2, first[0] + tile_index]
    q_first = halo_rows + place
    first_block = first_start // TILE
    last_block = (q_first + tile - 1) // TILE
    sums[...] = jnp.zeros_like(sums)
    totals[...] = jnp.zeros_like(totals)
    inner = 1.0 / (math.sqrt(HEAD_DIM) * LOGIT_CAP)
    outer = LOGIT_CAP * math.log2(math.e)

    def block_step(block, masked):
        rows = pl.ds(pl.multiple_of(block * TILE, TILE), TILE)
        if masked:
            k_ids = block * TILE + lax.broadcasted_iota(jnp.int32, (tile, TILE), 1)
            q_ids = q_first + lax.broadcasted_iota(jnp.int32, (tile, TILE), 0)
            begins = jnp.zeros((tile, 1), jnp.int32)
            for number in range(ends.shape[0]):
                begins = jnp.where(q_ids[:, :1] >= ends[number], jnp.maximum(begins, ends[number]), begins)
            allowed = (k_ids <= q_ids) & (k_ids >= begins)
        for kv_head in range(kv_heads):
            keys = kv_all[rows, kv_head * HEAD_DIM : (kv_head + 1) * HEAD_DIM]
            at = (kv_heads + kv_head) * HEAD_DIM
            values = kv_all[rows, at : at + HEAD_DIM]
            for member in range(share):
                head = kv_head * share + member
                query = q_ref[:, head * HEAD_DIM : (head + 1) * HEAD_DIM]
                raw = lax.dot_general(query, keys, (((1,), (1,)), ((), ())), preferred_element_type=jnp.float32)
                weights = jnp.exp2(outer * jnp.tanh(raw * inner))
                if masked:
                    weights = jnp.where(allowed, weights, 0.0)
                partial = weights[:, :HEAD_DIM]
                for part in range(1, TILE // HEAD_DIM):
                    partial = partial + weights[:, part * HEAD_DIM : (part + 1) * HEAD_DIM]
                totals[head] += partial
                sums[head] += jnp.dot(weights.astype(jnp.bfloat16), values, preferred_element_type=jnp.float32)

    def either(block, carry):
        begin = block * TILE
        whole = (begin >= last_start) & (begin + TILE - 1 <= q_first)

        @pl.when(whole)
        def _():
            block_step(block, False)

        @pl.when(jnp.logical_not(whole))
        def _():
            block_step(block, True)

        return carry

    lax.fori_loop(first_block, last_block + 1, either, 0)
    for head in range(kv_heads * share):
        denominator = jnp.sum(totals[head], axis=1, keepdims=True)
        out_ref[:, head * HEAD_DIM : (head + 1) * HEAD_DIM] = (sums[head] / denominator).astype(out_ref.dtype)


def attend(chunk, chunk_rows, query, ends, bounds, halo, kv, kv_heads):
    width = query.shape[1]
    heads = width // HEAD_DIM
    halo_rows = halo.shape[0]
    tiles = chunk_rows // TILE
    first = (chunk * tiles).reshape(1).astype(jnp.int32)
    kernel = functools.partial(attend_kernel, kv_heads, heads // kv_heads, halo_rows)
    return pl.pallas_call(
        kernel,
        out_shape=jax.ShapeDtypeStruct((chunk_rows, width), jnp.bfloat16),
        grid_spec=pltpu.PrefetchScalarGridSpec(
            num_scalar_prefetch=3,
            grid=(tiles,),
            in_specs=[
                pl.BlockSpec((TILE, width), lambda i, c, s, e: (c[0] + i, 0)),
                pl.BlockSpec(halo.shape, lambda i, c, s, e: (0, 0)),
                pl.BlockSpec(kv.shape, lambda i, c, s, e: (0, 0)),
            ],
            out_specs=pl.BlockSpec((TILE, width), lambda i, c, s, e: (i, 0)),
            scratch_shapes=[
                pltpu.VMEM((halo_rows + kv.shape[0], kv.shape[1]), jnp.bfloat16),
                pltpu.VMEM((heads, TILE, HEAD_DIM), jnp.float32),
                pltpu.VMEM((heads, TILE, HEAD_DIM), jnp.float32),
            ],
        ),
        compiler_params=pltpu.CompilerParams(vmem_limit_bytes=VMEM_BYTES),
        cost_estimate=pl.CostEstimate(
            flops=4 * chunk_rows * width * (halo_rows + chunk_rows) // 2,
            bytes_accessed=4 * chunk_rows * width,
            transcendentals=chunk_rows * heads * (halo_rows + chunk_rows),
        ),
    )(first, bounds, ends, query, halo, kv)


def after(block, *others):
    space = pl.BlockSpec(memory_space=pl.ANY)
    return pl.pallas_call(
        lambda *refs: None,
        out_shape=jax.ShapeDtypeStruct(block.shape, block.dtype),
        in_specs=[space] * (1 + len(others)),
        out_specs=space,
        input_output_aliases={0: 0},
    )(block, *others)


def per_device(group, lines, cores, tokens, lengths, w_query, w_key, w_value):
    row_count, depth = tokens.shape
    slice_rows = w_query.shape[0]
    index = lax.axis_index("ca")
    mine, line = index % group, index // group
    core = lax.axis_index("tp")
    q_width = w_query.shape[1] // group
    one_width = w_key.shape[1] // group
    kv_width = 2 * one_width
    kv_heads = one_width // HEAD_DIM
    group_rows = group * row_count
    devices = range(group * lines)

    def slice_for(target):
        return jnp.concatenate(
            [
                lax.dynamic_slice_in_dim(w_query, target * q_width, q_width, 1),
                lax.dynamic_slice_in_dim(w_key, target * one_width, one_width, 1),
                lax.dynamic_slice_in_dim(w_value, target * one_width, one_width, 1),
            ],
            axis=1,
        )

    def to_partner(block, step):
        return lax.ppermute(block, "ca", [(i, i ^ step) for i in devices])

    def along_lines(block):
        lanes = [[place + group * i for i in range(lines)] for place in range(group)]
        return lax.all_gather(block, "ca", axis=0, tiled=True, axis_index_groups=lanes)

    def forwarded(block):
        return lax.ppermute(block, "ca", [(i, (i + group) % (group * lines)) for i in devices])

    def gathered(array, block, column, members):
        if group == 1:
            return (array, block, column, [(0, array.shape[0], lambda s: 0)])
        pieces = []
        for at in range(lines):
            for number, step in enumerate(members):
                source = (at * len(members) + number) * slice_rows
                pieces.append((source, slice_rows, lambda s, at=at, step=step: (at * group + (s[0] ^ step)) * slice_rows))
        return (array, block, column, pieces)

    def from_lines(held, column, members):
        entries = []
        for back, array in enumerate(held):
            pieces = []
            for number, step in enumerate(members):

                def target(s, back=back, step=step):
                    at = lax.rem(s[1] - back + lines, lines)
                    return (at * group + (s[0] ^ step)) * slice_rows

                pieces.append((number * slice_rows, slice_rows, target))
            entries.append((array, (0, array.shape[1]), column, pieces))
        return entries

    half = row_count // 2
    halo_rows = REACH * row_count
    tiles = row_count // TILE

    def tables():
        row_ids = line * group_rows + jnp.arange(group_rows, dtype=jnp.int32)
        starts = doc_starts(lengths, row_ids)
        window_starts = starts - (line * group_rows - halo_rows)
        places = jnp.arange(group * tiles, dtype=jnp.int32) * TILE
        first = window_starts.reshape(group * tiles, TILE)
        bounds = jnp.stack([places, first[:, 0], first[:, -1]])
        cosine, sine = rope_tables(row_ids - starts)
        ends = jnp.cumsum(lengths).astype(jnp.int32) - (line * group_rows - halo_rows)
        return cosine, sine, ends, bounds

    place = jnp.stack([mine, line, core]).astype(jnp.int32)
    if group > 1:
        slices = [slice_for(mine)] + [to_partner(slice_for(mine ^ step), step) for step in range(1, group)]
        members = range(group)
        own_q = along_lines(slices[0][:, :q_width])
        rest_q = along_lines(jnp.concatenate([a[:, :q_width] for a in slices[1:]]))
        rest_kv = jnp.concatenate([a[:, q_width:] for a in slices])
        both = ("ca", "tp")

        def cross(block, steps):
            pairs = [(i * 2 + c, (i ^ steps[c]) * 2 + c) for i in devices for c in range(2)]
            return lax.ppermute(block, both, pairs)

        def swap(block):
            return lax.ppermute(block, both, [(i * 2 + c, i * 2 + 1 - c) for i in devices for c in range(2)])

        begin = core * half

        own_half = lax.dynamic_slice_in_dim(tokens, begin, half, 0)

        def home(step_even, step_odd, mate):
            def target(s):
                step = jnp.where(s[2] == mate, step_even, step_odd)
                return (s[0] ^ step) * row_count + jnp.where(mate == 0, s[2], 1 - s[2]) * half

            return target


        def share(tokens, own_half, rest_kv):
            near = cross(own_half, (1, 2))
            other = cross(own_half, (2, 1))
            held = [rest_kv]
            for _ in range(1, lines):
                held.append(forwarded(held[-1]))
            lists = tables()
            everything = put(place, group_rows, [(tokens, lambda s: s[0] * row_count)])
            near = after(near, held[-1], *lists, everything)
            far = cross(near, (2, 1))
            mates = [swap(block) for block in (near, other)]
            first = [(near, home(1, 2, 0)), (mates[0], home(1, 2, 1)), (other, home(2, 1, 0)), (mates[1], home(2, 1, 1))]
            early = put(place, group_rows, first, everything)
            weights = from_lines(held, 0, members)
            kv = project(group, place, early, weights, kv_width, lists[0], lists[1], kv_heads, (0, group - 1))
            far = after(far, kv)
            last = [(far, home(3, 3, 0)), (swap(far), home(3, 3, 1))]
            everything = put(place, group_rows, last, early)
            kv = project(group, place, everything, weights, kv_width, lists[0], lists[1], kv_heads, (group - 1, 1), kv)
            return everything, lists, kv

        def nothing(*operands):
            shapes = jax.eval_shape(share, *operands)
            return jax.tree.map(lambda leaf: jnp.zeros(leaf.shape, leaf.dtype), shapes)

        known = rest_kv[0, 0].astype(jnp.float32)
        operands = (tokens, own_half, rest_kv)
        all_tokens, known_tables, kv = lax.cond(known == known, share, nothing, *operands)
        q_weights = [gathered(own_q, (0, q_width), 0, [0]), gathered(rest_q, (0, q_width), 0, members[1:])]
    else:
        all_tokens, known_tables = tokens, tables()
        own = along_lines(slice_for(mine))
        kv_weights = [gathered(own, (q_width // kv_width, kv_width), 0, [0])]
        q_weights = [gathered(own, (0, q_width), 0, [0])]
        kv = project(group, place, tokens, kv_weights, kv_width, *known_tables[:2], kv_heads, (0, 1))

    cosine, sine, ends, bounds = known_tables

    hops = -(-halo_rows // group_rows)
    pieces, moving = [], kv
    for hop in range(hops):
        keep = min(halo_rows - hop * group_rows, group_rows)
        moving = moving[moving.shape[0] - keep :]
        moving = lax.ppermute(moving, "ca", [(i, i + group) for i in devices if i + group in devices])
        pieces.insert(0, moving)
    halo = pieces[0] if len(pieces) == 1 else jnp.concatenate(pieces)

    query = project(group, place, all_tokens, q_weights, q_width, cosine, sine, q_width // HEAD_DIM, (0, group))
    result = jnp.zeros((row_count, w_query.shape[1]), jnp.bfloat16)
    for step in reversed(range(group)):
        part = attend(mine ^ step, row_count, query, ends, bounds, halo, kv, kv_heads)
        if step > 0:
            part = to_partner(part, step)
        elif group == 1:
            return part
        result = lax.dynamic_update_slice_in_dim(result, part, (mine ^ step) * q_width, 1)
    return result


def solution(mesh):
    size, cores = mesh.shape["ca"], mesh.shape["tp"]
    local_kv = KV_HEADS // cores
    group = 4 if cores == 2 and local_kv == 4 and size % 4 == 0 else 1
    placed = (P("ca", None), P(), P("ca", "tp"), P("ca", "tp"), P("ca", "tp"))
    body = functools.partial(per_device, group, size // group, cores)
    return jax.shard_map(body, mesh=mesh, in_specs=placed, out_specs=P("ca", "tp"), check_vma=False)
```

```python
import functools
import math

import jax
import jax.numpy as jnp
from jax import lax
from jax.experimental import pallas as pl
from jax.experimental.pallas import tpu as pltpu
from jax.sharding import PartitionSpec as P

HEADS = 32
KV_HEADS = 8
HEAD_DIM = 128
REACH = 3
ROPE_THETA = 500000.0
LOGIT_CAP = 5.0
TILE = 256
PUT_BYTES = 20 * 1024 * 1024
PROJECT_BYTES = 58 * 1024 * 1024
VMEM_BYTES = 58 * 1024 * 1024


def doc_starts(lengths, positions):
    doc_ends = jnp.cumsum(lengths).astype(jnp.int32)
    before = doc_ends[None, :] <= positions[:, None]
    return jnp.max(jnp.where(before, doc_ends[None, :], 0), axis=1).astype(jnp.int32)


def rope_tables(offsets):
    half_dim = HEAD_DIM // 2
    frequency = ROPE_THETA ** (-(jnp.arange(half_dim, dtype=jnp.float32) * 2.0) / HEAD_DIM)
    angles = offsets.astype(jnp.float32)[:, None] * frequency[None, :]
    cosine, sine = jnp.cos(angles), jnp.sin(angles)
    return jnp.concatenate([cosine, cosine], axis=1), jnp.concatenate([-sine, sine], axis=1)


def rotated(values, cosine, sine):
    return values * cosine + pltpu.roll(values, HEAD_DIM // 2, 1) * sine


def project_kernel(rope_heads, layout, given, place, x_ref, *refs):
    w_refs = refs[: len(layout)]
    cos_ref, sin_ref = refs[len(layout) : len(layout) + 2]
    out_ref, w_all = refs[len(layout) + 2 + given :]

    @pl.when(pl.program_id(0) == 0)
    def _():
        for ref, (_, column, pieces) in zip(w_refs, layout):
            columns = slice(column, column + ref.shape[1])
            for source, rows, target in pieces:
                at = pl.multiple_of(target(place), rows)
                w_all[pl.ds(at, rows), columns] = ref[source : source + rows, :]

    total = jnp.dot(x_ref[...], w_all[...], preferred_element_type=jnp.float32)
    cosine, sine = cos_ref[...], sin_ref[...]
    for head in range(out_ref.shape[1] // HEAD_DIM):
        columns = slice(head * HEAD_DIM, (head + 1) * HEAD_DIM)
        part = total[:, columns]
        if head < rope_heads:
            part = rotated(part, cosine, sine)
        out_ref[:, columns] = part.astype(out_ref.dtype)


def project(group, place, tokens, weights, width, cosine, sine, rope_heads, span, into=None):
    rows, depth = tokens.shape
    first, count = span
    tile = rows // group
    arrays, blocks, layout = [], [], []
    for array, (block, columns), column, pieces in weights:
        arrays.append(array)
        blocks.append(pl.BlockSpec((array.shape[0], columns), lambda i, s, block=block: (0, block)))
        layout.append((None, column, pieces))

    def row_block(i, s):
        return (s[0] ^ (first + i), 0)

    given = [] if into is None else [into]
    return pl.pallas_call(
        functools.partial(project_kernel, rope_heads, layout, len(given)),
        out_shape=jax.ShapeDtypeStruct((rows, width), jnp.bfloat16),
        grid_spec=pltpu.PrefetchScalarGridSpec(
            num_scalar_prefetch=1,
            grid=(count,),
            in_specs=[pl.BlockSpec((tile, depth), row_block)]
            + blocks
            + [pl.BlockSpec((tile, HEAD_DIM), row_block)] * 2
            + [pl.BlockSpec(memory_space=pl.ANY)] * len(given),
            out_specs=pl.BlockSpec((tile, width), row_block),
            scratch_shapes=[pltpu.VMEM((depth, width), tokens.dtype)],
        ),
        input_output_aliases={} if into is None else {4 + len(arrays): 0},
        compiler_params=pltpu.CompilerParams(vmem_limit_bytes=PROJECT_BYTES),
        cost_estimate=pl.CostEstimate(
            flops=2 * count * tile * depth * width,
            bytes_accessed=2 * depth * (count * tile + width),
            transcendentals=0,
        ),
    )(place, tokens, *arrays, cosine, sine, *given)


def put_kernel(targets, place, *refs):
    sems, out_ref = refs[-1], refs[-2]
    copies = []
    for number, (ref, target) in enumerate(zip(refs, targets)):
        rows = ref.shape[0]
        at = pl.multiple_of(target(place), rows)
        copies.append(pltpu.make_async_copy(ref, out_ref.at[pl.ds(at, rows), :], sems.at[number]))
        copies[-1].start()
    for copy in copies:
        copy.wait()


def put(place, rows, blocks, into=None):
    arrays, targets = [block for block, _ in blocks], [target for _, target in blocks]
    spaces = [pl.BlockSpec(memory_space=pltpu.SMEM)] + [pl.BlockSpec(memory_space=pltpu.VMEM)] * len(arrays)
    aliases = {}
    if into is not None:
        aliases = {1 + len(arrays): 0}
        arrays.append(into)
        spaces.append(pl.BlockSpec(memory_space=pl.ANY))
    return pl.pallas_call(
        functools.partial(put_kernel, targets),
        out_shape=jax.ShapeDtypeStruct((rows, arrays[0].shape[1]), arrays[0].dtype),
        in_specs=spaces,
        out_specs=pl.BlockSpec(memory_space=pl.ANY),
        scratch_shapes=[pltpu.SemaphoreType.DMA((len(targets),))],
        input_output_aliases=aliases,
        compiler_params=pltpu.CompilerParams(vmem_limit_bytes=PUT_BYTES),
    )(place, *arrays)


def attend_kernel(kv_heads, share, halo_rows, first, bounds, ends, q_ref, halo_ref, kv_ref, out_ref, kv_all, q_all, sums, totals):
    tile_index = pl.program_id(0)

    @pl.when(tile_index == 0)
    def _():
        kv_all[:halo_rows, :] = halo_ref[...]
        kv_all[halo_rows:, :] = kv_ref[...]

    tile = q_ref.shape[0]
    for head in range(kv_heads * share):
        q_all[head * tile : (head + 1) * tile, :] = q_ref[:, head * HEAD_DIM : (head + 1) * HEAD_DIM]
    place = bounds[0, first[0] + tile_index]
    first_start = bounds[1, first[0] + tile_index]
    last_start = bounds[2, first[0] + tile_index]
    q_first = halo_rows + place
    first_block = first_start // TILE
    last_block = (q_first + tile - 1) // TILE
    sums[...] = jnp.zeros_like(sums)
    totals[...] = jnp.zeros_like(totals)
    inner = 1.0 / (math.sqrt(HEAD_DIM) * LOGIT_CAP)
    outer = LOGIT_CAP * math.log2(math.e)

    def block_step(block, masked):
        rows = pl.ds(pl.multiple_of(block * TILE, TILE), TILE)
        if masked:
            k_ids = block * TILE + lax.broadcasted_iota(jnp.int32, (tile, TILE), 1)
            q_ids = q_first + lax.broadcasted_iota(jnp.int32, (tile, TILE), 0)
            begins = jnp.zeros((tile, 1), jnp.int32)
            for number in range(ends.shape[0]):
                begins = jnp.where(q_ids[:, :1] >= ends[number], jnp.maximum(begins, ends[number]), begins)
            allowed = (k_ids <= q_ids) & (k_ids >= begins)
        for kv_head in range(kv_heads):
            keys = kv_all[rows, kv_head * HEAD_DIM : (kv_head + 1) * HEAD_DIM]
            at = (kv_heads + kv_head) * HEAD_DIM
            values = kv_all[rows, at : at + HEAD_DIM]
            members = slice(kv_head * share * tile, (kv_head + 1) * share * tile)
            raw = lax.dot_general(
                q_all[members, :], keys, (((1,), (1,)), ((), ())), preferred_element_type=jnp.float32
            )
            weights = jnp.exp2(outer * jnp.tanh(raw * inner))
            if masked:
                weights = weights.reshape(share, tile, TILE)
                weights = jnp.where(allowed[None], weights, 0.0).reshape(share * tile, TILE)
            partial = weights[:, :HEAD_DIM]
            for part in range(1, TILE // HEAD_DIM):
                partial = partial + weights[:, part * HEAD_DIM : (part + 1) * HEAD_DIM]
            totals[members, :] += partial
            sums[members, :] += jnp.dot(weights.astype(jnp.bfloat16), values, preferred_element_type=jnp.float32)

    def either(block, carry):
        begin = block * TILE
        whole = (begin >= last_start) & (begin + TILE - 1 <= q_first)

        @pl.when(whole)
        def _():
            block_step(block, False)

        @pl.when(jnp.logical_not(whole))
        def _():
            block_step(block, True)

        return carry

    lax.fori_loop(first_block, last_block + 1, either, 0)
    for head in range(kv_heads * share):
        rows = slice(head * tile, (head + 1) * tile)
        denominator = jnp.sum(totals[rows, :], axis=1, keepdims=True)
        out_ref[:, head * HEAD_DIM : (head + 1) * HEAD_DIM] = (sums[rows, :] / denominator).astype(out_ref.dtype)


def attend(chunk, chunk_rows, query, ends, bounds, halo, kv, kv_heads):
    width = query.shape[1]
    heads = width // HEAD_DIM
    halo_rows = halo.shape[0]
    tiles = chunk_rows // TILE
    first = (chunk * tiles).reshape(1).astype(jnp.int32)
    kernel = functools.partial(attend_kernel, kv_heads, heads // kv_heads, halo_rows)
    return pl.pallas_call(
        kernel,
        out_shape=jax.ShapeDtypeStruct((chunk_rows, width), jnp.bfloat16),
        grid_spec=pltpu.PrefetchScalarGridSpec(
            num_scalar_prefetch=3,
            grid=(tiles,),
            in_specs=[
                pl.BlockSpec((TILE, width), lambda i, c, s, e: (c[0] + i, 0)),
                pl.BlockSpec(halo.shape, lambda i, c, s, e: (0, 0)),
                pl.BlockSpec(kv.shape, lambda i, c, s, e: (0, 0)),
            ],
            out_specs=pl.BlockSpec((TILE, width), lambda i, c, s, e: (i, 0)),
            scratch_shapes=[
                pltpu.VMEM((halo_rows + kv.shape[0], kv.shape[1]), jnp.bfloat16),
                pltpu.VMEM((heads * TILE, HEAD_DIM), jnp.bfloat16),
                pltpu.VMEM((heads * TILE, HEAD_DIM), jnp.float32),
                pltpu.VMEM((heads * TILE, HEAD_DIM), jnp.float32),
            ],
        ),
        compiler_params=pltpu.CompilerParams(vmem_limit_bytes=VMEM_BYTES),
        cost_estimate=pl.CostEstimate(
            flops=4 * chunk_rows * width * (halo_rows + chunk_rows) // 2,
            bytes_accessed=4 * chunk_rows * width,
            transcendentals=chunk_rows * heads * (halo_rows + chunk_rows),
        ),
    )(first, bounds, ends, query, halo, kv)


def after(block, *others):
    space = pl.BlockSpec(memory_space=pl.ANY)
    return pl.pallas_call(
        lambda *refs: None,
        out_shape=jax.ShapeDtypeStruct(block.shape, block.dtype),
        in_specs=[space] * (1 + len(others)),
        out_specs=space,
        input_output_aliases={0: 0},
    )(block, *others)


def per_device(group, lines, cores, tokens, lengths, w_query, w_key, w_value):
    row_count, depth = tokens.shape
    slice_rows = w_query.shape[0]
    index = lax.axis_index("ca")
    mine, line = index % group, index // group
    core = lax.axis_index("tp")
    q_width = w_query.shape[1] // group
    one_width = w_key.shape[1] // group
    kv_width = 2 * one_width
    kv_heads = one_width // HEAD_DIM
    group_rows = group * row_count
    devices = range(group * lines)

    def slice_for(target):
        return jnp.concatenate(
            [
                lax.dynamic_slice_in_dim(w_query, target * q_width, q_width, 1),
                lax.dynamic_slice_in_dim(w_key, target * one_width, one_width, 1),
                lax.dynamic_slice_in_dim(w_value, target * one_width, one_width, 1),
            ],
            axis=1,
        )

    def to_partner(block, step):
        return lax.ppermute(block, "ca", [(i, i ^ step) for i in devices])

    def along_lines(block):
        lanes = [[place + group * i for i in range(lines)] for place in range(group)]
        return lax.all_gather(block, "ca", axis=0, tiled=True, axis_index_groups=lanes)

    def forwarded(block):
        return lax.ppermute(block, "ca", [(i, (i + group) % (group * lines)) for i in devices])

    def gathered(array, block, column, members):
        if group == 1:
            return (array, block, column, [(0, array.shape[0], lambda s: 0)])
        pieces = []
        for at in range(lines):
            for number, step in enumerate(members):
                source = (at * len(members) + number) * slice_rows
                pieces.append((source, slice_rows, lambda s, at=at, step=step: (at * group + (s[0] ^ step)) * slice_rows))
        return (array, block, column, pieces)

    def from_lines(held, column, members):
        entries = []
        for back, array in enumerate(held):
            pieces = []
            for number, step in enumerate(members):

                def target(s, back=back, step=step):
                    at = lax.rem(s[1] - back + lines, lines)
                    return (at * group + (s[0] ^ step)) * slice_rows

                pieces.append((number * slice_rows, slice_rows, target))
            entries.append((array, (0, array.shape[1]), column, pieces))
        return entries

    half = row_count // 2
    halo_rows = REACH * row_count
    tiles = row_count // TILE

    def tables():
        row_ids = line * group_rows + jnp.arange(group_rows, dtype=jnp.int32)
        starts = doc_starts(lengths, row_ids)
        window_starts = starts - (line * group_rows - halo_rows)
        places = jnp.arange(group * tiles, dtype=jnp.int32) * TILE
        first = window_starts.reshape(group * tiles, TILE)
        bounds = jnp.stack([places, first[:, 0], first[:, -1]])
        cosine, sine = rope_tables(row_ids - starts)
        ends = jnp.cumsum(lengths).astype(jnp.int32) - (line * group_rows - halo_rows)
        return cosine, sine, ends, bounds

    place = jnp.stack([mine, line, core]).astype(jnp.int32)
    if group > 1:
        slices = [slice_for(mine)] + [to_partner(slice_for(mine ^ step), step) for step in range(1, group)]
        own_slices = along_lines(slices[0])
        rest_q = along_lines(jnp.concatenate([a[:, :q_width] for a in slices[1:]]))
        rest_kv = jnp.concatenate([a[:, q_width:] for a in slices[1:]])
        both = ("ca", "tp")

        def cross(block, steps):
            pairs = [(i * 2 + c, (i ^ steps[c]) * 2 + c) for i in devices for c in range(2)]
            return lax.ppermute(block, both, pairs)

        def swap(block):
            return lax.ppermute(block, both, [(i * 2 + c, i * 2 + 1 - c) for i in devices for c in range(2)])

        begin = core * half

        own_half = lax.dynamic_slice_in_dim(tokens, begin, half, 0)

        def home(step_even, step_odd, mate):
            def target(s):
                step = jnp.where(s[2] == mate, step_even, step_odd)
                return (s[0] ^ step) * row_count + jnp.where(mate == 0, s[2], 1 - s[2]) * half

            return target


        def share(tokens, own_half, rest_kv):
            near = cross(own_half, (1, 2))
            other = cross(own_half, (2, 1))
            held = [rest_kv]
            for _ in range(1, lines):
                held.append(forwarded(held[-1]))
            lists = tables()
            everything = put(place, group_rows, [(tokens, lambda s: s[0] * row_count)])
            near = after(near, held[-1], *lists, everything)
            far = cross(near, (2, 1))
            mates = [swap(block) for block in (near, other)]
            first = [(near, home(1, 2, 0)), (mates[0], home(1, 2, 1)), (other, home(2, 1, 0)), (mates[1], home(2, 1, 1))]
            early = put(place, group_rows, first, everything)
            last = [(far, home(3, 3, 0)), (swap(far), home(3, 3, 1))]
            everything = put(place, group_rows, last, early)
            return everything, lists, tuple(held[1:])

        def nothing(*operands):
            shapes = jax.eval_shape(share, *operands)
            return jax.tree.map(lambda leaf: jnp.zeros(leaf.shape, leaf.dtype), shapes)

        known = rest_kv[0, 0].astype(jnp.float32)
        operands = (tokens, own_half, rest_kv)
        all_tokens, known_tables, held = lax.cond(known == known, share, nothing, *operands)
        others = range(1, group)
        kv_weights = [gathered(own_slices, (q_width // kv_width, kv_width), 0, [0])]
        kv_weights += from_lines((rest_kv, *held), 0, others)
        q_weights = [gathered(own_slices, (0, q_width), 0, [0]), gathered(rest_q, (0, q_width), 0, others)]
    else:
        all_tokens, known_tables = tokens, tables()
        own = along_lines(slice_for(mine))
        kv_weights = [gathered(own, (q_width // kv_width, kv_width), 0, [0])]
        q_weights = [gathered(own, (0, q_width), 0, [0])]
    cosine, sine, ends, bounds = known_tables

    kv = project(group, place, all_tokens, kv_weights, kv_width, cosine, sine, kv_heads, (0, group))
    hops = -(-halo_rows // group_rows)
    pieces, moving = [], kv
    for hop in range(hops):
        keep = min(halo_rows - hop * group_rows, group_rows)
        moving = moving[moving.shape[0] - keep :]
        moving = lax.ppermute(moving, "ca", [(i, i + group) for i in devices if i + group in devices])
        pieces.insert(0, moving)
    halo = pieces[0] if len(pieces) == 1 else jnp.concatenate(pieces)

    query = project(group, place, all_tokens, q_weights, q_width, cosine, sine, q_width // HEAD_DIM, (0, group))
    result = jnp.zeros((row_count, w_query.shape[1]), jnp.bfloat16)
    for step in reversed(range(group)):
        part = attend(mine ^ step, row_count, query, ends, bounds, halo, kv, kv_heads)
        if step > 0:
            part = to_partner(part, step)
        elif group == 1:
            return part
        result = lax.dynamic_update_slice_in_dim(result, part, (mine ^ step) * q_width, 1)
    return result


def solution(mesh):
    size, cores = mesh.shape["ca"], mesh.shape["tp"]
    local_kv = KV_HEADS // cores
    group = 4 if cores == 2 and local_kv == 4 and size % 4 == 0 else 1
    placed = (P("ca", None), P(), P("ca", "tp"), P("ca", "tp"), P("ca", "tp"))
    body = functools.partial(per_device, group, size // group, cores)
    return jax.shard_map(body, mesh=mesh, in_specs=placed, out_specs=P("ca", "tp"), check_vma=False)
```

```python
import functools
import math

import jax
import jax.numpy as jnp
from jax import lax
from jax.experimental import pallas as pl
from jax.experimental.pallas import tpu as pltpu
from jax.sharding import PartitionSpec as P

HEADS = 32
KV_HEADS = 8
HEAD_DIM = 128
REACH = 3
ROPE_THETA = 500000.0
LOGIT_CAP = 5.0
TILE = 256
PUT_BYTES = 20 * 1024 * 1024
PROJECT_BYTES = 30 * 1024 * 1024
VMEM_BYTES = 58 * 1024 * 1024


def doc_starts(lengths, positions):
    doc_ends = jnp.cumsum(lengths).astype(jnp.int32)
    before = doc_ends[None, :] <= positions[:, None]
    return jnp.max(jnp.where(before, doc_ends[None, :], 0), axis=1).astype(jnp.int32)


def rope_tables(offsets):
    half_dim = HEAD_DIM // 2
    frequency = ROPE_THETA ** (-(jnp.arange(half_dim, dtype=jnp.float32) * 2.0) / HEAD_DIM)
    angles = offsets.astype(jnp.float32)[:, None] * frequency[None, :]
    cosine, sine = jnp.cos(angles), jnp.sin(angles)
    return jnp.concatenate([cosine, cosine], axis=1), jnp.concatenate([-sine, sine], axis=1)


def rotated(values, cosine, sine):
    return values * cosine + pltpu.roll(values, HEAD_DIM // 2, 1) * sine


def project_kernel(rope_heads, layout, given, place, x_ref, *refs):
    w_refs = refs[: len(layout)]
    cos_ref, sin_ref = refs[len(layout) : len(layout) + 2]
    out_ref, w_all = refs[len(layout) + 2 + given :]

    @pl.when(pl.program_id(0) == 0)
    def _():
        for ref, (_, column, pieces) in zip(w_refs, layout):
            columns = slice(column, column + ref.shape[1])
            for source, rows, target in pieces:
                at = pl.multiple_of(target(place), rows)
                w_all[pl.ds(at, rows), columns] = ref[source : source + rows, :]

    total = jnp.dot(x_ref[...], w_all[...], preferred_element_type=jnp.float32)
    cosine, sine = cos_ref[...], sin_ref[...]
    for head in range(out_ref.shape[1] // HEAD_DIM):
        columns = slice(head * HEAD_DIM, (head + 1) * HEAD_DIM)
        part = total[:, columns]
        if head < rope_heads:
            part = rotated(part, cosine, sine)
        out_ref[:, columns] = part.astype(out_ref.dtype)


def project(group, place, tokens, weights, width, cosine, sine, rope_heads, span, into=None):
    rows, depth = tokens.shape
    first, count = span
    tile = rows // group
    arrays, blocks, layout = [], [], []
    for array, (block, columns), column, pieces in weights:
        arrays.append(array)
        blocks.append(pl.BlockSpec((array.shape[0], columns), lambda i, s, block=block: (0, block)))
        layout.append((None, column, pieces))

    def row_block(i, s):
        return (s[0] ^ (first + i), 0)

    given = [] if into is None else [into]
    return pl.pallas_call(
        functools.partial(project_kernel, rope_heads, layout, len(given)),
        out_shape=jax.ShapeDtypeStruct((rows, width), jnp.bfloat16),
        grid_spec=pltpu.PrefetchScalarGridSpec(
            num_scalar_prefetch=1,
            grid=(count,),
            in_specs=[pl.BlockSpec((tile, depth), row_block)]
            + blocks
            + [pl.BlockSpec((tile, HEAD_DIM), row_block)] * 2
            + [pl.BlockSpec(memory_space=pl.ANY)] * len(given),
            out_specs=pl.BlockSpec((tile, width), row_block),
            scratch_shapes=[pltpu.VMEM((depth, width), tokens.dtype)],
        ),
        input_output_aliases={} if into is None else {4 + len(arrays): 0},
        compiler_params=pltpu.CompilerParams(vmem_limit_bytes=PROJECT_BYTES),
        cost_estimate=pl.CostEstimate(
            flops=2 * count * tile * depth * width,
            bytes_accessed=2 * depth * (count * tile + width),
            transcendentals=0,
        ),
    )(place, tokens, *arrays, cosine, sine, *given)


def put_kernel(targets, place, *refs):
    sems, out_ref = refs[-1], refs[-2]
    copies = []
    for number, (ref, target) in enumerate(zip(refs, targets)):
        rows = ref.shape[0]
        at = pl.multiple_of(target(place), rows)
        copies.append(pltpu.make_async_copy(ref, out_ref.at[pl.ds(at, rows), :], sems.at[number]))
        copies[-1].start()
    for copy in copies:
        copy.wait()


def put(place, rows, blocks, into=None):
    arrays, targets = [block for block, _ in blocks], [target for _, target in blocks]
    spaces = [pl.BlockSpec(memory_space=pltpu.SMEM)] + [pl.BlockSpec(memory_space=pltpu.VMEM)] * len(arrays)
    aliases = {}
    if into is not None:
        aliases = {1 + len(arrays): 0}
        arrays.append(into)
        spaces.append(pl.BlockSpec(memory_space=pl.ANY))
    return pl.pallas_call(
        functools.partial(put_kernel, targets),
        out_shape=jax.ShapeDtypeStruct((rows, arrays[0].shape[1]), arrays[0].dtype),
        in_specs=spaces,
        out_specs=pl.BlockSpec(memory_space=pl.ANY),
        scratch_shapes=[pltpu.SemaphoreType.DMA((len(targets),))],
        input_output_aliases=aliases,
        compiler_params=pltpu.CompilerParams(vmem_limit_bytes=PUT_BYTES),
    )(place, *arrays)


def attend_kernel(kv_heads, share, halo_rows, first, bounds, ends, q_ref, halo_ref, kv_ref, out_ref, kv_all, q_all, sums, totals):
    tile_index = pl.program_id(0)

    @pl.when(tile_index == 0)
    def _():
        kv_all[:halo_rows, :] = halo_ref[...]
        kv_all[halo_rows:, :] = kv_ref[...]

    tile = q_ref.shape[0]
    for head in range(kv_heads * share):
        q_all[head * tile : (head + 1) * tile, :] = q_ref[:, head * HEAD_DIM : (head + 1) * HEAD_DIM]
    place = bounds[0, first[0] + tile_index]
    first_start = bounds[1, first[0] + tile_index]
    last_start = bounds[2, first[0] + tile_index]
    q_first = halo_rows + place
    first_block = first_start // TILE
    last_block = (q_first + tile - 1) // TILE
    sums[...] = jnp.zeros_like(sums)
    totals[...] = jnp.zeros_like(totals)
    inner = 1.0 / (math.sqrt(HEAD_DIM) * LOGIT_CAP)
    outer = LOGIT_CAP * math.log2(math.e)

    def block_step(block, masked):
        rows = pl.ds(pl.multiple_of(block * TILE, TILE), TILE)
        if masked:
            k_ids = block * TILE + lax.broadcasted_iota(jnp.int32, (tile, TILE), 1)
            q_ids = q_first + lax.broadcasted_iota(jnp.int32, (tile, TILE), 0)
            begins = jnp.zeros((tile, 1), jnp.int32)
            for number in range(ends.shape[0]):
                begins = jnp.where(q_ids[:, :1] >= ends[number], jnp.maximum(begins, ends[number]), begins)
            allowed = (k_ids <= q_ids) & (k_ids >= begins)
        for kv_head in range(kv_heads):
            keys = kv_all[rows, kv_head * HEAD_DIM : (kv_head + 1) * HEAD_DIM]
            at = (kv_heads + kv_head) * HEAD_DIM
            values = kv_all[rows, at : at + HEAD_DIM]
            members = slice(kv_head * share * tile, (kv_head + 1) * share * tile)
            raw = lax.dot_general(
                q_all[members, :], keys, (((1,), (1,)), ((), ())), preferred_element_type=jnp.float32
            )
            weights = jnp.exp2(outer * jnp.tanh(raw * inner))
            if masked:
                weights = weights.reshape(share, tile, TILE)
                weights = jnp.where(allowed[None], weights, 0.0).reshape(share * tile, TILE)
            partial = weights[:, :HEAD_DIM]
            for part in range(1, TILE // HEAD_DIM):
                partial = partial + weights[:, part * HEAD_DIM : (part + 1) * HEAD_DIM]
            totals[members, :] += partial
            sums[members, :] += jnp.dot(weights.astype(jnp.bfloat16), values, preferred_element_type=jnp.float32)

    def either(block, carry):
        begin = block * TILE
        whole = (begin >= last_start) & (begin + TILE - 1 <= q_first)

        @pl.when(whole)
        def _():
            block_step(block, False)

        @pl.when(jnp.logical_not(whole))
        def _():
            block_step(block, True)

        return carry

    lax.fori_loop(first_block, last_block + 1, either, 0)
    for head in range(kv_heads * share):
        rows = slice(head * tile, (head + 1) * tile)
        denominator = jnp.sum(totals[rows, :], axis=1, keepdims=True)
        out_ref[:, head * HEAD_DIM : (head + 1) * HEAD_DIM] = (sums[rows, :] / denominator).astype(out_ref.dtype)


def attend(chunk, chunk_rows, query, ends, bounds, halo, kv, kv_heads):
    width = query.shape[1]
    heads = width // HEAD_DIM
    halo_rows = halo.shape[0]
    tiles = chunk_rows // TILE
    first = (chunk * tiles).reshape(1).astype(jnp.int32)
    kernel = functools.partial(attend_kernel, kv_heads, heads // kv_heads, halo_rows)
    return pl.pallas_call(
        kernel,
        out_shape=jax.ShapeDtypeStruct((chunk_rows, width), jnp.bfloat16),
        grid_spec=pltpu.PrefetchScalarGridSpec(
            num_scalar_prefetch=3,
            grid=(tiles,),
            in_specs=[
                pl.BlockSpec((TILE, width), lambda i, c, s, e: (c[0] + i, 0)),
                pl.BlockSpec(halo.shape, lambda i, c, s, e: (0, 0)),
                pl.BlockSpec(kv.shape, lambda i, c, s, e: (0, 0)),
            ],
            out_specs=pl.BlockSpec((TILE, width), lambda i, c, s, e: (i, 0)),
            scratch_shapes=[
                pltpu.VMEM((halo_rows + kv.shape[0], kv.shape[1]), jnp.bfloat16),
                pltpu.VMEM((heads * TILE, HEAD_DIM), jnp.bfloat16),
                pltpu.VMEM((heads * TILE, HEAD_DIM), jnp.float32),
                pltpu.VMEM((heads * TILE, HEAD_DIM), jnp.float32),
            ],
        ),
        compiler_params=pltpu.CompilerParams(vmem_limit_bytes=VMEM_BYTES),
        cost_estimate=pl.CostEstimate(
            flops=4 * chunk_rows * width * (halo_rows + chunk_rows) // 2,
            bytes_accessed=4 * chunk_rows * width,
            transcendentals=chunk_rows * heads * (halo_rows + chunk_rows),
        ),
    )(first, bounds, ends, query, halo, kv)


def after(block, *others):
    space = pl.BlockSpec(memory_space=pl.ANY)
    return pl.pallas_call(
        lambda *refs: None,
        out_shape=jax.ShapeDtypeStruct(block.shape, block.dtype),
        in_specs=[space] * (1 + len(others)),
        out_specs=space,
        input_output_aliases={0: 0},
    )(block, *others)


def per_device(group, lines, cores, tokens, lengths, w_query, w_key, w_value):
    row_count, depth = tokens.shape
    slice_rows = w_query.shape[0]
    index = lax.axis_index("ca")
    mine, line = index % group, index // group
    core = lax.axis_index("tp")
    q_width = w_query.shape[1] // group
    one_width = w_key.shape[1] // group
    kv_width = 2 * one_width
    kv_heads = one_width // HEAD_DIM
    group_rows = group * row_count
    devices = range(group * lines)

    def slice_for(target):
        return jnp.concatenate(
            [
                lax.dynamic_slice_in_dim(w_query, target * q_width, q_width, 1),
                lax.dynamic_slice_in_dim(w_key, target * one_width, one_width, 1),
                lax.dynamic_slice_in_dim(w_value, target * one_width, one_width, 1),
            ],
            axis=1,
        )

    def to_partner(block, step):
        return lax.ppermute(block, "ca", [(i, i ^ step) for i in devices])

    def along_lines(block):
        lanes = [[place + group * i for i in range(lines)] for place in range(group)]
        return lax.all_gather(block, "ca", axis=0, tiled=True, axis_index_groups=lanes)

    def forwarded(block):
        return lax.ppermute(block, "ca", [(i, (i + group) % (group * lines)) for i in devices])

    def gathered(array, block, column, members):
        if group == 1:
            return (array, block, column, [(0, array.shape[0], lambda s: 0)])
        pieces = []
        for at in range(lines):
            for number, step in enumerate(members):
                source = (at * len(members) + number) * slice_rows
                pieces.append((source, slice_rows, lambda s, at=at, step=step: (at * group + (s[0] ^ step)) * slice_rows))
        return (array, block, column, pieces)

    def from_lines(held, column, members):
        entries = []
        for back, array in enumerate(held):
            pieces = []
            for number, step in enumerate(members):

                def target(s, back=back, step=step):
                    at = lax.rem(s[1] - back + lines, lines)
                    return (at * group + (s[0] ^ step)) * slice_rows

                pieces.append((number * slice_rows, slice_rows, target))
            entries.append((array, (0, array.shape[1]), column, pieces))
        return entries

    half = row_count // 2
    halo_rows = REACH * row_count
    tiles = row_count // TILE

    def tables():
        row_ids = line * group_rows + jnp.arange(group_rows, dtype=jnp.int32)
        starts = doc_starts(lengths, row_ids)
        window_starts = starts - (line * group_rows - halo_rows)
        places = jnp.arange(group * tiles, dtype=jnp.int32) * TILE
        first = window_starts.reshape(group * tiles, TILE)
        bounds = jnp.stack([places, first[:, 0], first[:, -1]])
        cosine, sine = rope_tables(row_ids - starts)
        ends = jnp.cumsum(lengths).astype(jnp.int32) - (line * group_rows - halo_rows)
        return cosine, sine, ends, bounds

    place = jnp.stack([mine, line, core]).astype(jnp.int32)
    if group > 1:
        slices = [slice_for(mine)] + [to_partner(slice_for(mine ^ step), step) for step in range(1, group)]
        own_slices = along_lines(slices[0])
        rest_q = along_lines(jnp.concatenate([a[:, :q_width] for a in slices[1:]]))
        rest_kv = jnp.concatenate([a[:, q_width:] for a in slices[1:]])
        both = ("ca", "tp")

        def cross(block, steps):
            pairs = [(i * 2 + c, (i ^ steps[c]) * 2 + c) for i in devices for c in range(2)]
            return lax.ppermute(block, both, pairs)

        def swap(block):
            return lax.ppermute(block, both, [(i * 2 + c, i * 2 + 1 - c) for i in devices for c in range(2)])

        begin = core * half

        own_half = lax.dynamic_slice_in_dim(tokens, begin, half, 0)

        def home(step_even, step_odd, mate):
            def target(s):
                step = jnp.where(s[2] == mate, step_even, step_odd)
                return (s[0] ^ step) * row_count + jnp.where(mate == 0, s[2], 1 - s[2]) * half

            return target


        near = cross(own_half, (1, 2))
        other = cross(own_half, (2, 1))

        def prepare(tokens, rest_kv):
            held = [rest_kv]
            for _ in range(1, lines - 1):
                held.append(forwarded(held[-1]))
            return put(place, group_rows, [(tokens, lambda s: s[0] * row_count)]), tables(), tuple(held[1:])

        def share(everything, near, other, block):
            far = cross(near, (2, 1))
            block = forwarded(block)
            mates = [swap(block) for block in (near, other)]
            first = [(near, home(1, 2, 0)), (mates[0], home(1, 2, 1)), (other, home(2, 1, 0)), (mates[1], home(2, 1, 1))]
            everything = put(place, group_rows, first, after(everything, block))
            far = after(far, everything)
            last = [(far, home(3, 3, 0)), (swap(far), home(3, 3, 1))]
            return put(place, group_rows, last, everything), block

        def region(body, flag, *operands):
            def nothing(*operands):
                shapes = jax.eval_shape(body, *operands)
                return jax.tree.map(lambda leaf: jnp.zeros(leaf.shape, leaf.dtype), shapes)

            known = flag.reshape(-1)[0].astype(jnp.float32)
            return lax.cond(known == known, body, nothing, *operands)

        all_tokens, known_tables, held = region(prepare, rest_kv[:1, :1], tokens, rest_kv)
        all_tokens, furthest = region(share, held[-1][:1, :1], all_tokens, near, other, held[-1])
        held = (*held, furthest)
        others = range(1, group)
        kv_weights = [gathered(own_slices, (q_width // kv_width, kv_width), 0, [0])]
        kv_weights += from_lines((rest_kv, *held), 0, others)
        q_weights = [gathered(own_slices, (0, q_width), 0, [0]), gathered(rest_q, (0, q_width), 0, others)]
    else:
        all_tokens, known_tables = tokens, tables()
        own = along_lines(slice_for(mine))
        kv_weights = [gathered(own, (q_width // kv_width, kv_width), 0, [0])]
        q_weights = [gathered(own, (0, q_width), 0, [0])]
    cosine, sine, ends, bounds = known_tables

    kv = project(group, place, all_tokens, kv_weights, kv_width, cosine, sine, kv_heads, (0, group))
    hops = -(-halo_rows // group_rows)
    pieces, moving = [], kv
    for hop in range(hops):
        keep = min(halo_rows - hop * group_rows, group_rows)
        moving = moving[moving.shape[0] - keep :]
        moving = lax.ppermute(moving, "ca", [(i, i + group) for i in devices if i + group in devices])
        pieces.insert(0, moving)
    halo = pieces[0] if len(pieces) == 1 else jnp.concatenate(pieces)

    query = project(group, place, all_tokens, q_weights, q_width, cosine, sine, q_width // HEAD_DIM, (0, group))
    result = jnp.zeros((row_count, w_query.shape[1]), jnp.bfloat16)
    for step in reversed(range(group)):
        part = attend(mine ^ step, row_count, query, ends, bounds, halo, kv, kv_heads)
        if step > 0:
            part = to_partner(part, step)
        elif group == 1:
            return part
        result = lax.dynamic_update_slice_in_dim(result, part, (mine ^ step) * q_width, 1)
    return result


def solution(mesh):
    size, cores = mesh.shape["ca"], mesh.shape["tp"]
    local_kv = KV_HEADS // cores
    group = 4 if cores == 2 and local_kv == 4 and size % 4 == 0 else 1
    placed = (P("ca", None), P(), P("ca", "tp"), P("ca", "tp"), P("ca", "tp"))
    body = functools.partial(per_device, group, size // group, cores)
    return jax.shard_map(body, mesh=mesh, in_specs=placed, out_specs=P("ca", "tp"), check_vma=False)
```

```python
import functools
import math

import jax
import jax.numpy as jnp
from jax import lax
from jax.experimental import pallas as pl
from jax.experimental.pallas import tpu as pltpu
from jax.sharding import PartitionSpec as P

HEADS = 32
KV_HEADS = 8
HEAD_DIM = 128
REACH = 3
ROPE_THETA = 500000.0
LOGIT_CAP = 5.0
TILE = 128
PUT_BYTES = 20 * 1024 * 1024
PROJECT_BYTES = 30 * 1024 * 1024
VMEM_BYTES = 58 * 1024 * 1024


def doc_starts(lengths, positions):
    doc_ends = jnp.cumsum(lengths).astype(jnp.int32)
    before = doc_ends[None, :] <= positions[:, None]
    return jnp.max(jnp.where(before, doc_ends[None, :], 0), axis=1).astype(jnp.int32)


def rope_tables(offsets):
    half_dim = HEAD_DIM // 2
    frequency = ROPE_THETA ** (-(jnp.arange(half_dim, dtype=jnp.float32) * 2.0) / HEAD_DIM)
    angles = offsets.astype(jnp.float32)[:, None] * frequency[None, :]
    cosine, sine = jnp.cos(angles), jnp.sin(angles)
    return jnp.concatenate([cosine, cosine], axis=1), jnp.concatenate([-sine, sine], axis=1)


def rotated(values, cosine, sine):
    return values * cosine + pltpu.roll(values, HEAD_DIM // 2, 1) * sine


def project_kernel(rope_heads, layout, given, place, x_ref, *refs):
    w_refs = refs[: len(layout)]
    cos_ref, sin_ref = refs[len(layout) : len(layout) + 2]
    out_ref, w_all = refs[len(layout) + 2 + given :]

    @pl.when(pl.program_id(0) == 0)
    def _():
        for ref, (_, column, pieces) in zip(w_refs, layout):
            columns = slice(column, column + ref.shape[1])
            for source, rows, target in pieces:
                at = pl.multiple_of(target(place), rows)
                w_all[pl.ds(at, rows), columns] = ref[source : source + rows, :]

    total = jnp.dot(x_ref[...], w_all[...], preferred_element_type=jnp.float32)
    cosine, sine = cos_ref[...], sin_ref[...]
    for head in range(out_ref.shape[1] // HEAD_DIM):
        columns = slice(head * HEAD_DIM, (head + 1) * HEAD_DIM)
        part = total[:, columns]
        if head < rope_heads:
            part = rotated(part, cosine, sine)
        out_ref[:, columns] = part.astype(out_ref.dtype)


def project(group, place, tokens, weights, width, cosine, sine, rope_heads, span, into=None):
    rows, depth = tokens.shape
    first, count = span
    tile = rows // group
    arrays, blocks, layout = [], [], []
    for array, (block, columns), column, pieces in weights:
        arrays.append(array)
        blocks.append(pl.BlockSpec((array.shape[0], columns), lambda i, s, block=block: (0, block)))
        layout.append((None, column, pieces))

    def row_block(i, s):
        return (s[0] ^ (first + i), 0)

    given = [] if into is None else [into]
    return pl.pallas_call(
        functools.partial(project_kernel, rope_heads, layout, len(given)),
        out_shape=jax.ShapeDtypeStruct((rows, width), jnp.bfloat16),
        grid_spec=pltpu.PrefetchScalarGridSpec(
            num_scalar_prefetch=1,
            grid=(count,),
            in_specs=[pl.BlockSpec((tile, depth), row_block)]
            + blocks
            + [pl.BlockSpec((tile, HEAD_DIM), row_block)] * 2
            + [pl.BlockSpec(memory_space=pl.ANY)] * len(given),
            out_specs=pl.BlockSpec((tile, width), row_block),
            scratch_shapes=[pltpu.VMEM((depth, width), tokens.dtype)],
        ),
        input_output_aliases={} if into is None else {4 + len(arrays): 0},
        compiler_params=pltpu.CompilerParams(vmem_limit_bytes=PROJECT_BYTES),
        cost_estimate=pl.CostEstimate(
            flops=2 * count * tile * depth * width,
            bytes_accessed=2 * depth * (count * tile + width),
            transcendentals=0,
        ),
    )(place, tokens, *arrays, cosine, sine, *given)


def put_kernel(targets, place, *refs):
    sems, out_ref = refs[-1], refs[-2]
    copies = []
    for number, (ref, target) in enumerate(zip(refs, targets)):
        rows = ref.shape[0]
        at = pl.multiple_of(target(place), rows)
        copies.append(pltpu.make_async_copy(ref, out_ref.at[pl.ds(at, rows), :], sems.at[number]))
        copies[-1].start()
    for copy in copies:
        copy.wait()


def put(place, rows, blocks, into=None):
    arrays, targets = [block for block, _ in blocks], [target for _, target in blocks]
    spaces = [pl.BlockSpec(memory_space=pltpu.SMEM)] + [pl.BlockSpec(memory_space=pltpu.VMEM)] * len(arrays)
    aliases = {}
    if into is not None:
        aliases = {1 + len(arrays): 0}
        arrays.append(into)
        spaces.append(pl.BlockSpec(memory_space=pl.ANY))
    return pl.pallas_call(
        functools.partial(put_kernel, targets),
        out_shape=jax.ShapeDtypeStruct((rows, arrays[0].shape[1]), arrays[0].dtype),
        in_specs=spaces,
        out_specs=pl.BlockSpec(memory_space=pl.ANY),
        scratch_shapes=[pltpu.SemaphoreType.DMA((len(targets),))],
        input_output_aliases=aliases,
        compiler_params=pltpu.CompilerParams(vmem_limit_bytes=PUT_BYTES),
    )(place, *arrays)


def attend_kernel(kv_heads, share, halo_rows, first, bounds, ends, q_ref, halo_ref, kv_ref, out_ref, kv_all, q_all, sums, totals):
    tile_index = pl.program_id(0)

    @pl.when(tile_index == 0)
    def _():
        kv_all[:halo_rows, :] = halo_ref[...]
        kv_all[halo_rows:, :] = kv_ref[...]

    tile = q_ref.shape[0]
    for head in range(kv_heads * share):
        q_all[head * tile : (head + 1) * tile, :] = q_ref[:, head * HEAD_DIM : (head + 1) * HEAD_DIM]
    place = bounds[0, first[0] + tile_index]
    first_start = bounds[1, first[0] + tile_index]
    last_start = bounds[2, first[0] + tile_index]
    q_first = halo_rows + place
    lowest = first_start // TILE * TILE
    units = (q_first + tile - lowest) // TILE
    sums[...] = jnp.zeros_like(sums)
    totals[...] = jnp.zeros_like(totals)
    inner = 1.0 / (math.sqrt(HEAD_DIM) * LOGIT_CAP)
    outer = LOGIT_CAP * math.log2(math.e)

    def block_step(begin, size, masked):
        rows = pl.ds(pl.multiple_of(begin, TILE), size)
        if masked:
            k_ids = begin + lax.broadcasted_iota(jnp.int32, (tile, size), 1)
            q_ids = q_first + lax.broadcasted_iota(jnp.int32, (tile, size), 0)
            begins = jnp.zeros((tile, 1), jnp.int32)
            for number in range(ends.shape[0]):
                begins = jnp.where(q_ids[:, :1] >= ends[number], jnp.maximum(begins, ends[number]), begins)
            allowed = (k_ids <= q_ids) & (k_ids >= begins)
        for kv_head in range(kv_heads):
            keys = kv_all[rows, kv_head * HEAD_DIM : (kv_head + 1) * HEAD_DIM]
            at = (kv_heads + kv_head) * HEAD_DIM
            values = kv_all[rows, at : at + HEAD_DIM]
            members = slice(kv_head * share * tile, (kv_head + 1) * share * tile)
            raw = lax.dot_general(
                q_all[members, :], keys, (((1,), (1,)), ((), ())), preferred_element_type=jnp.float32
            )
            weights = jnp.exp2(outer * jnp.tanh(raw * inner))
            if masked:
                weights = weights.reshape(share, tile, size)
                weights = jnp.where(allowed[None], weights, 0.0).reshape(share * tile, size)
            partial = weights[:, :HEAD_DIM]
            for part in range(1, size // HEAD_DIM):
                partial = partial + weights[:, part * HEAD_DIM : (part + 1) * HEAD_DIM]
            totals[members, :] += partial
            sums[members, :] += jnp.dot(weights.astype(jnp.bfloat16), values, preferred_element_type=jnp.float32)

    def either(begin, size):
        whole = (begin >= last_start) & (begin + size - 1 <= q_first)

        @pl.when(whole)
        def _():
            block_step(begin, size, False)

        @pl.when(jnp.logical_not(whole))
        def _():
            block_step(begin, size, True)

    def pair(number, carry):
        either(q_first + tile - 2 * TILE * (number + 1), 2 * TILE)
        return carry

    lax.fori_loop(0, units // 2, pair, 0)

    @pl.when(lax.rem(units, 2) == 1)
    def _():
        either(lowest, TILE)

    for head in range(kv_heads * share):
        rows = slice(head * tile, (head + 1) * tile)
        denominator = jnp.sum(totals[rows, :], axis=1, keepdims=True)
        out_ref[:, head * HEAD_DIM : (head + 1) * HEAD_DIM] = (sums[rows, :] / denominator).astype(out_ref.dtype)


def attend(chunk, chunk_rows, query, ends, bounds, halo, kv, kv_heads):
    width = query.shape[1]
    heads = width // HEAD_DIM
    halo_rows = halo.shape[0]
    tiles = chunk_rows // TILE
    first = (chunk * tiles).reshape(1).astype(jnp.int32)
    kernel = functools.partial(attend_kernel, kv_heads, heads // kv_heads, halo_rows)
    return pl.pallas_call(
        kernel,
        out_shape=jax.ShapeDtypeStruct((chunk_rows, width), jnp.bfloat16),
        grid_spec=pltpu.PrefetchScalarGridSpec(
            num_scalar_prefetch=3,
            grid=(tiles,),
            in_specs=[
                pl.BlockSpec((TILE, width), lambda i, c, s, e: (c[0] + i, 0)),
                pl.BlockSpec(halo.shape, lambda i, c, s, e: (0, 0)),
                pl.BlockSpec(kv.shape, lambda i, c, s, e: (0, 0)),
            ],
            out_specs=pl.BlockSpec((TILE, width), lambda i, c, s, e: (i, 0)),
            scratch_shapes=[
                pltpu.VMEM((halo_rows + kv.shape[0], kv.shape[1]), jnp.bfloat16),
                pltpu.VMEM((heads * TILE, HEAD_DIM), jnp.bfloat16),
                pltpu.VMEM((heads * TILE, HEAD_DIM), jnp.float32),
                pltpu.VMEM((heads * TILE, HEAD_DIM), jnp.float32),
            ],
        ),
        compiler_params=pltpu.CompilerParams(vmem_limit_bytes=VMEM_BYTES),
        cost_estimate=pl.CostEstimate(
            flops=4 * chunk_rows * width * (halo_rows + chunk_rows) // 2,
            bytes_accessed=4 * chunk_rows * width,
            transcendentals=chunk_rows * heads * (halo_rows + chunk_rows),
        ),
    )(first, bounds, ends, query, halo, kv)


def after(block, *others):
    space = pl.BlockSpec(memory_space=pl.ANY)
    return pl.pallas_call(
        lambda *refs: None,
        out_shape=jax.ShapeDtypeStruct(block.shape, block.dtype),
        in_specs=[space] * (1 + len(others)),
        out_specs=space,
        input_output_aliases={0: 0},
    )(block, *others)


def per_device(group, lines, cores, tokens, lengths, w_query, w_key, w_value):
    row_count, depth = tokens.shape
    slice_rows = w_query.shape[0]
    index = lax.axis_index("ca")
    mine, line = index % group, index // group
    core = lax.axis_index("tp")
    q_width = w_query.shape[1] // group
    one_width = w_key.shape[1] // group
    kv_width = 2 * one_width
    kv_heads = one_width // HEAD_DIM
    group_rows = group * row_count
    devices = range(group * lines)

    def slice_for(target):
        return jnp.concatenate(
            [
                lax.dynamic_slice_in_dim(w_query, target * q_width, q_width, 1),
                lax.dynamic_slice_in_dim(w_key, target * one_width, one_width, 1),
                lax.dynamic_slice_in_dim(w_value, target * one_width, one_width, 1),
            ],
            axis=1,
        )

    def to_partner(block, step):
        return lax.ppermute(block, "ca", [(i, i ^ step) for i in devices])

    def along_lines(block):
        lanes = [[place + group * i for i in range(lines)] for place in range(group)]
        return lax.all_gather(block, "ca", axis=0, tiled=True, axis_index_groups=lanes)

    def forwarded(block):
        return lax.ppermute(block, "ca", [(i, (i + group) % (group * lines)) for i in devices])

    def gathered(array, block, column, members):
        if group == 1:
            return (array, block, column, [(0, array.shape[0], lambda s: 0)])
        pieces = []
        for at in range(lines):
            for number, step in enumerate(members):
                source = (at * len(members) + number) * slice_rows
                pieces.append((source, slice_rows, lambda s, at=at, step=step: (at * group + (s[0] ^ step)) * slice_rows))
        return (array, block, column, pieces)

    def from_lines(held, column, members):
        entries = []
        for back, array in enumerate(held):
            pieces = []
            for number, step in enumerate(members):

                def target(s, back=back, step=step):
                    at = lax.rem(s[1] - back + lines, lines)
                    return (at * group + (s[0] ^ step)) * slice_rows

                pieces.append((number * slice_rows, slice_rows, target))
            entries.append((array, (0, array.shape[1]), column, pieces))
        return entries

    half = row_count // 2
    halo_rows = REACH * row_count
    tiles = row_count // TILE

    def tables():
        row_ids = line * group_rows + jnp.arange(group_rows, dtype=jnp.int32)
        starts = doc_starts(lengths, row_ids)
        window_starts = starts - (line * group_rows - halo_rows)
        places = jnp.arange(group * tiles, dtype=jnp.int32) * TILE
        first = window_starts.reshape(group * tiles, TILE)
        bounds = jnp.stack([places, first[:, 0], first[:, -1]])
        cosine, sine = rope_tables(row_ids - starts)
        ends = jnp.cumsum(lengths).astype(jnp.int32) - (line * group_rows - halo_rows)
        return cosine, sine, ends, bounds

    place = jnp.stack([mine, line, core]).astype(jnp.int32)
    if group > 1:
        slices = [slice_for(mine)] + [to_partner(slice_for(mine ^ step), step) for step in range(1, group)]
        own_slices = along_lines(slices[0])
        rest_q = along_lines(jnp.concatenate([a[:, :q_width] for a in slices[1:]]))
        rest_kv = jnp.concatenate([a[:, q_width:] for a in slices[1:]])
        both = ("ca", "tp")

        def cross(block, steps):
            pairs = [(i * 2 + c, (i ^ steps[c]) * 2 + c) for i in devices for c in range(2)]
            return lax.ppermute(block, both, pairs)

        def swap(block):
            return lax.ppermute(block, both, [(i * 2 + c, i * 2 + 1 - c) for i in devices for c in range(2)])

        begin = core * half

        own_half = lax.dynamic_slice_in_dim(tokens, begin, half, 0)

        def home(step_even, step_odd, mate):
            def target(s):
                step = jnp.where(s[2] == mate, step_even, step_odd)
                return (s[0] ^ step) * row_count + jnp.where(mate == 0, s[2], 1 - s[2]) * half

            return target


        near = cross(own_half, (1, 2))
        other = cross(own_half, (2, 1))

        def prepare(tokens, rest_kv):
            held = [rest_kv]
            for _ in range(1, lines - 1):
                held.append(forwarded(held[-1]))
            return put(place, group_rows, [(tokens, lambda s: s[0] * row_count)]), tables(), tuple(held[1:])

        def share(everything, near, other):
            far = cross(near, (2, 1))
            mates = [swap(block) for block in (near, other)]
            first = [(near, home(1, 2, 0)), (mates[0], home(1, 2, 1)), (other, home(2, 1, 0)), (mates[1], home(2, 1, 1))]
            everything = put(place, group_rows, first, everything)
            far = after(far, everything)
            last = [(far, home(3, 3, 0)), (swap(far), home(3, 3, 1))]
            return put(place, group_rows, last, everything)

        def region(body, flag, *operands):
            def nothing(*operands):
                shapes = jax.eval_shape(body, *operands)
                return jax.tree.map(lambda leaf: jnp.zeros(leaf.shape, leaf.dtype), shapes)

            known = flag.reshape(-1)[0].astype(jnp.float32)
            return lax.cond(known == known, body, nothing, *operands)

        all_tokens, known_tables, held = region(prepare, rest_kv[:1, :1], tokens, rest_kv)
        held = (*held, forwarded(held[-1]))
        all_tokens = region(share, near[:1, :1], all_tokens, near, other)
        others = range(1, group)
        kv_weights = [gathered(own_slices, (q_width // kv_width, kv_width), 0, [0])]
        kv_weights += from_lines((rest_kv, *held), 0, others)
        q_weights = [gathered(own_slices, (0, q_width), 0, [0]), gathered(rest_q, (0, q_width), 0, others)]
    else:
        all_tokens, known_tables = tokens, tables()
        own = along_lines(slice_for(mine))
        kv_weights = [gathered(own, (q_width // kv_width, kv_width), 0, [0])]
        q_weights = [gathered(own, (0, q_width), 0, [0])]
    cosine, sine, ends, bounds = known_tables

    kv = project(group, place, all_tokens, kv_weights, kv_width, cosine, sine, kv_heads, (0, group))
    hops = -(-halo_rows // group_rows)
    pieces, moving = [], kv
    for hop in range(hops):
        keep = min(halo_rows - hop * group_rows, group_rows)
        moving = moving[moving.shape[0] - keep :]
        moving = lax.ppermute(moving, "ca", [(i, i + group) for i in devices if i + group in devices])
        pieces.insert(0, moving)
    halo = pieces[0] if len(pieces) == 1 else jnp.concatenate(pieces)

    query = project(group, place, all_tokens, q_weights, q_width, cosine, sine, q_width // HEAD_DIM, (0, group))
    result = jnp.zeros((row_count, w_query.shape[1]), jnp.bfloat16)
    for step in reversed(range(group)):
        part = attend(mine ^ step, row_count, query, ends, bounds, halo, kv, kv_heads)
        if step > 0:
            part = to_partner(part, step)
        elif group == 1:
            return part
        result = lax.dynamic_update_slice_in_dim(result, part, (mine ^ step) * q_width, 1)
    return result


def solution(mesh):
    size, cores = mesh.shape["ca"], mesh.shape["tp"]
    local_kv = KV_HEADS // cores
    group = 4 if cores == 2 and local_kv == 4 and size % 4 == 0 else 1
    placed = (P("ca", None), P(), P("ca", "tp"), P("ca", "tp"), P("ca", "tp"))
    body = functools.partial(per_device, group, size // group, cores)
    return jax.shard_map(body, mesh=mesh, in_specs=placed, out_specs=P("ca", "tp"), check_vma=False)
```

```python
import functools
import math

import jax
import jax.numpy as jnp
from jax import lax
from jax.experimental import pallas as pl
from jax.experimental.pallas import tpu as pltpu
from jax.sharding import PartitionSpec as P

HEADS = 32
KV_HEADS = 8
HEAD_DIM = 128
REACH = 3
ROPE_THETA = 500000.0
LOGIT_CAP = 5.0
TILE = 256
UNIT = 128
PUT_BYTES = 20 * 1024 * 1024
PROJECT_BYTES = 30 * 1024 * 1024
VMEM_BYTES = 58 * 1024 * 1024


def doc_starts(lengths, positions):
    doc_ends = jnp.cumsum(lengths).astype(jnp.int32)
    before = doc_ends[None, :] <= positions[:, None]
    return jnp.max(jnp.where(before, doc_ends[None, :], 0), axis=1).astype(jnp.int32)


def rope_tables(offsets):
    half_dim = HEAD_DIM // 2
    frequency = ROPE_THETA ** (-(jnp.arange(half_dim, dtype=jnp.float32) * 2.0) / HEAD_DIM)
    angles = offsets.astype(jnp.float32)[:, None] * frequency[None, :]
    cosine, sine = jnp.cos(angles), jnp.sin(angles)
    return jnp.concatenate([cosine, cosine], axis=1), jnp.concatenate([-sine, sine], axis=1)


def rotated(values, cosine, sine):
    return values * cosine + pltpu.roll(values, HEAD_DIM // 2, 1) * sine


def project_kernel(rope_heads, layout, given, place, x_ref, *refs):
    w_refs = refs[: len(layout)]
    cos_ref, sin_ref = refs[len(layout) : len(layout) + 2]
    out_ref, w_all = refs[len(layout) + 2 + given :]

    @pl.when(pl.program_id(0) == 0)
    def _():
        for ref, (_, column, pieces) in zip(w_refs, layout):
            columns = slice(column, column + ref.shape[1])
            for source, rows, target in pieces:
                at = pl.multiple_of(target(place), rows)
                w_all[pl.ds(at, rows), columns] = ref[source : source + rows, :]

    total = jnp.dot(x_ref[...], w_all[...], preferred_element_type=jnp.float32)
    cosine, sine = cos_ref[...], sin_ref[...]
    for head in range(out_ref.shape[1] // HEAD_DIM):
        columns = slice(head * HEAD_DIM, (head + 1) * HEAD_DIM)
        part = total[:, columns]
        if head < rope_heads:
            part = rotated(part, cosine, sine)
        out_ref[:, columns] = part.astype(out_ref.dtype)


def project(group, place, tokens, weights, width, cosine, sine, rope_heads, span, into=None):
    rows, depth = tokens.shape
    first, count = span
    tile = rows // group
    arrays, blocks, layout = [], [], []
    for array, (block, columns), column, pieces in weights:
        arrays.append(array)
        blocks.append(pl.BlockSpec((array.shape[0], columns), lambda i, s, block=block: (0, block)))
        layout.append((None, column, pieces))

    def row_block(i, s):
        return (s[0] ^ (first + i), 0)

    given = [] if into is None else [into]
    return pl.pallas_call(
        functools.partial(project_kernel, rope_heads, layout, len(given)),
        out_shape=jax.ShapeDtypeStruct((rows, width), jnp.bfloat16),
        grid_spec=pltpu.PrefetchScalarGridSpec(
            num_scalar_prefetch=1,
            grid=(count,),
            in_specs=[pl.BlockSpec((tile, depth), row_block)]
            + blocks
            + [pl.BlockSpec((tile, HEAD_DIM), row_block)] * 2
            + [pl.BlockSpec(memory_space=pl.ANY)] * len(given),
            out_specs=pl.BlockSpec((tile, width), row_block),
            scratch_shapes=[pltpu.VMEM((depth, width), tokens.dtype)],
        ),
        input_output_aliases={} if into is None else {4 + len(arrays): 0},
        compiler_params=pltpu.CompilerParams(vmem_limit_bytes=PROJECT_BYTES),
        cost_estimate=pl.CostEstimate(
            flops=2 * count * tile * depth * width,
            bytes_accessed=2 * depth * (count * tile + width),
            transcendentals=0,
        ),
    )(place, tokens, *arrays, cosine, sine, *given)


def put_kernel(targets, place, *refs):
    sems, out_ref = refs[-1], refs[-2]
    copies = []
    for number, (ref, target) in enumerate(zip(refs, targets)):
        rows = ref.shape[0]
        at = pl.multiple_of(target(place), rows)
        copies.append(pltpu.make_async_copy(ref, out_ref.at[pl.ds(at, rows), :], sems.at[number]))
        copies[-1].start()
    for copy in copies:
        copy.wait()


def put(place, rows, blocks, into=None):
    arrays, targets = [block for block, _ in blocks], [target for _, target in blocks]
    spaces = [pl.BlockSpec(memory_space=pltpu.SMEM)] + [pl.BlockSpec(memory_space=pltpu.VMEM)] * len(arrays)
    aliases = {}
    if into is not None:
        aliases = {1 + len(arrays): 0}
        arrays.append(into)
        spaces.append(pl.BlockSpec(memory_space=pl.ANY))
    return pl.pallas_call(
        functools.partial(put_kernel, targets),
        out_shape=jax.ShapeDtypeStruct((rows, arrays[0].shape[1]), arrays[0].dtype),
        in_specs=spaces,
        out_specs=pl.BlockSpec(memory_space=pl.ANY),
        scratch_shapes=[pltpu.SemaphoreType.DMA((len(targets),))],
        input_output_aliases=aliases,
        compiler_params=pltpu.CompilerParams(vmem_limit_bytes=PUT_BYTES),
    )(place, *arrays)


def attend_kernel(kv_heads, share, halo_rows, first, bounds, ends, q_ref, halo_ref, kv_ref, out_ref, kv_all, q_all, sums, totals):
    tile_index = pl.program_id(0)

    @pl.when(tile_index == 0)
    def _():
        kv_all[:halo_rows, :] = halo_ref[...]
        kv_all[halo_rows:, :] = kv_ref[...]

    tile = q_ref.shape[0]
    for head in range(kv_heads * share):
        q_all[head * tile : (head + 1) * tile, :] = q_ref[:, head * HEAD_DIM : (head + 1) * HEAD_DIM]
    place = bounds[0, first[0] + tile_index]
    first_start = bounds[1, first[0] + tile_index]
    last_start = bounds[2, first[0] + tile_index]
    q_first = halo_rows + place
    lowest = first_start // UNIT * UNIT
    units = (q_first - lowest) // UNIT
    sums[...] = jnp.zeros_like(sums)
    totals[...] = jnp.zeros_like(totals)
    inner = 1.0 / (math.sqrt(HEAD_DIM) * LOGIT_CAP)
    outer = LOGIT_CAP * math.log2(math.e)

    def block_step(begin, size, masked):
        rows = pl.ds(pl.multiple_of(begin, UNIT), size)
        if masked:
            k_ids = begin + lax.broadcasted_iota(jnp.int32, (tile, size), 1)
            q_ids = q_first + lax.broadcasted_iota(jnp.int32, (tile, size), 0)
            begins = jnp.zeros((tile, 1), jnp.int32)
            for number in range(ends.shape[0]):
                begins = jnp.where(q_ids[:, :1] >= ends[number], jnp.maximum(begins, ends[number]), begins)
            allowed = (k_ids <= q_ids) & (k_ids >= begins)
        for kv_head in range(kv_heads):
            keys = kv_all[rows, kv_head * HEAD_DIM : (kv_head + 1) * HEAD_DIM]
            at = (kv_heads + kv_head) * HEAD_DIM
            values = kv_all[rows, at : at + HEAD_DIM]
            members = slice(kv_head * share * tile, (kv_head + 1) * share * tile)
            raw = lax.dot_general(
                q_all[members, :], keys, (((1,), (1,)), ((), ())), preferred_element_type=jnp.float32
            )
            weights = jnp.exp2(outer * jnp.tanh(raw * inner))
            if masked:
                weights = weights.reshape(share, tile, size)
                weights = jnp.where(allowed[None], weights, 0.0).reshape(share * tile, size)
            partial = weights[:, :HEAD_DIM]
            for part in range(1, size // HEAD_DIM):
                partial = partial + weights[:, part * HEAD_DIM : (part + 1) * HEAD_DIM]
            totals[members, :] += partial
            sums[members, :] += jnp.dot(weights.astype(jnp.bfloat16), values, preferred_element_type=jnp.float32)

    def either(begin, size):
        whole = (begin >= last_start) & (begin + size - 1 <= q_first)

        @pl.when(whole)
        def _():
            block_step(begin, size, False)

        @pl.when(jnp.logical_not(whole))
        def _():
            block_step(begin, size, True)

    def long_step(number, carry):
        either(q_first - 4 * UNIT * (number + 1), 4 * UNIT)
        return carry

    block_step(q_first, tile, True)
    lax.fori_loop(0, units // 4, long_step, 0)
    rest = lax.rem(units, 4)

    @pl.when(rest >= 2)
    def _():
        either(lowest + lax.rem(rest, 2) * UNIT, 2 * UNIT)

    @pl.when(lax.rem(rest, 2) == 1)
    def _():
        either(lowest, UNIT)

    for head in range(kv_heads * share):
        rows = slice(head * tile, (head + 1) * tile)
        denominator = jnp.sum(totals[rows, :], axis=1, keepdims=True)
        out_ref[:, head * HEAD_DIM : (head + 1) * HEAD_DIM] = (sums[rows, :] / denominator).astype(out_ref.dtype)


def attend(chunk, chunk_rows, query, ends, bounds, halo, kv, kv_heads):
    width = query.shape[1]
    heads = width // HEAD_DIM
    halo_rows = halo.shape[0]
    tiles = chunk_rows // TILE
    first = (chunk * tiles).reshape(1).astype(jnp.int32)
    kernel = functools.partial(attend_kernel, kv_heads, heads // kv_heads, halo_rows)
    return pl.pallas_call(
        kernel,
        out_shape=jax.ShapeDtypeStruct((chunk_rows, width), jnp.bfloat16),
        grid_spec=pltpu.PrefetchScalarGridSpec(
            num_scalar_prefetch=3,
            grid=(tiles,),
            in_specs=[
                pl.BlockSpec((TILE, width), lambda i, c, s, e: (c[0] + i, 0)),
                pl.BlockSpec(halo.shape, lambda i, c, s, e: (0, 0)),
                pl.BlockSpec(kv.shape, lambda i, c, s, e: (0, 0)),
            ],
            out_specs=pl.BlockSpec((TILE, width), lambda i, c, s, e: (i, 0)),
            scratch_shapes=[
                pltpu.VMEM((halo_rows + kv.shape[0], kv.shape[1]), jnp.bfloat16),
                pltpu.VMEM((heads * TILE, HEAD_DIM), jnp.bfloat16),
                pltpu.VMEM((heads * TILE, HEAD_DIM), jnp.float32),
                pltpu.VMEM((heads * TILE, HEAD_DIM), jnp.float32),
            ],
        ),
        compiler_params=pltpu.CompilerParams(vmem_limit_bytes=VMEM_BYTES),
        cost_estimate=pl.CostEstimate(
            flops=4 * chunk_rows * width * (halo_rows + chunk_rows) // 2,
            bytes_accessed=4 * chunk_rows * width,
            transcendentals=chunk_rows * heads * (halo_rows + chunk_rows),
        ),
    )(first, bounds, ends, query, halo, kv)


def after(block, *others):
    space = pl.BlockSpec(memory_space=pl.ANY)
    return pl.pallas_call(
        lambda *refs: None,
        out_shape=jax.ShapeDtypeStruct(block.shape, block.dtype),
        in_specs=[space] * (1 + len(others)),
        out_specs=space,
        input_output_aliases={0: 0},
    )(block, *others)


def per_device(group, lines, cores, tokens, lengths, w_query, w_key, w_value):
    row_count, depth = tokens.shape
    slice_rows = w_query.shape[0]
    index = lax.axis_index("ca")
    mine, line = index % group, index // group
    core = lax.axis_index("tp")
    q_width = w_query.shape[1] // group
    one_width = w_key.shape[1] // group
    kv_width = 2 * one_width
    kv_heads = one_width // HEAD_DIM
    group_rows = group * row_count
    devices = range(group * lines)

    def slice_for(target):
        return jnp.concatenate(
            [
                lax.dynamic_slice_in_dim(w_query, target * q_width, q_width, 1),
                lax.dynamic_slice_in_dim(w_key, target * one_width, one_width, 1),
                lax.dynamic_slice_in_dim(w_value, target * one_width, one_width, 1),
            ],
            axis=1,
        )

    def to_partner(block, step):
        return lax.ppermute(block, "ca", [(i, i ^ step) for i in devices])

    def along_lines(block):
        lanes = [[place + group * i for i in range(lines)] for place in range(group)]
        return lax.all_gather(block, "ca", axis=0, tiled=True, axis_index_groups=lanes)

    def forwarded(block):
        return lax.ppermute(block, "ca", [(i, (i + group) % (group * lines)) for i in devices])

    def gathered(array, block, column, members):
        if group == 1:
            return (array, block, column, [(0, array.shape[0], lambda s: 0)])
        pieces = []
        for at in range(lines):
            for number, step in enumerate(members):
                source = (at * len(members) + number) * slice_rows
                pieces.append((source, slice_rows, lambda s, at=at, step=step: (at * group + (s[0] ^ step)) * slice_rows))
        return (array, block, column, pieces)

    def from_lines(held, column, members):
        entries = []
        for back, array in enumerate(held):
            pieces = []
            for number, step in enumerate(members):

                def target(s, back=back, step=step):
                    at = lax.rem(s[1] - back + lines, lines)
                    return (at * group + (s[0] ^ step)) * slice_rows

                pieces.append((number * slice_rows, slice_rows, target))
            entries.append((array, (0, array.shape[1]), column, pieces))
        return entries

    half = row_count // 2
    halo_rows = REACH * row_count
    tiles = row_count // TILE

    def tables():
        row_ids = line * group_rows + jnp.arange(group_rows, dtype=jnp.int32)
        starts = doc_starts(lengths, row_ids)
        window_starts = starts - (line * group_rows - halo_rows)
        places = jnp.arange(group * tiles, dtype=jnp.int32) * TILE
        first = window_starts.reshape(group * tiles, TILE)
        bounds = jnp.stack([places, first[:, 0], first[:, -1]])
        cosine, sine = rope_tables(row_ids - starts)
        ends = jnp.cumsum(lengths).astype(jnp.int32) - (line * group_rows - halo_rows)
        return cosine, sine, ends, bounds

    place = jnp.stack([mine, line, core]).astype(jnp.int32)
    if group > 1:
        slices = [slice_for(mine)] + [to_partner(slice_for(mine ^ step), step) for step in range(1, group)]
        own_slices = along_lines(slices[0])
        rest_q = along_lines(jnp.concatenate([a[:, :q_width] for a in slices[1:]]))
        rest_kv = jnp.concatenate([a[:, q_width:] for a in slices[1:]])
        both = ("ca", "tp")

        def cross(block, steps):
            pairs = [(i * 2 + c, (i ^ steps[c]) * 2 + c) for i in devices for c in range(2)]
            return lax.ppermute(block, both, pairs)

        def swap(block):
            return lax.ppermute(block, both, [(i * 2 + c, i * 2 + 1 - c) for i in devices for c in range(2)])

        begin = core * half

        own_half = lax.dynamic_slice_in_dim(tokens, begin, half, 0)

        def home(step_even, step_odd, mate):
            def target(s):
                step = jnp.where(s[2] == mate, step_even, step_odd)
                return (s[0] ^ step) * row_count + jnp.where(mate == 0, s[2], 1 - s[2]) * half

            return target


        near = cross(own_half, (1, 2))
        other = cross(own_half, (2, 1))

        def prepare(tokens, rest_kv):
            held = [rest_kv]
            for _ in range(1, lines - 1):
                held.append(forwarded(held[-1]))
            return put(place, group_rows, [(tokens, lambda s: s[0] * row_count)]), tables(), tuple(held[1:])

        def share(everything, near, other):
            far = cross(near, (2, 1))
            mates = [swap(block) for block in (near, other)]
            first = [(near, home(1, 2, 0)), (mates[0], home(1, 2, 1)), (other, home(2, 1, 0)), (mates[1], home(2, 1, 1))]
            everything = put(place, group_rows, first, everything)
            far = after(far, everything)
            last = [(far, home(3, 3, 0)), (swap(far), home(3, 3, 1))]
            return put(place, group_rows, last, everything)

        def region(body, flag, *operands):
            def nothing(*operands):
                shapes = jax.eval_shape(body, *operands)
                return jax.tree.map(lambda leaf: jnp.zeros(leaf.shape, leaf.dtype), shapes)

            known = flag.reshape(-1)[0].astype(jnp.float32)
            return lax.cond(known == known, body, nothing, *operands)

        all_tokens, known_tables, held = prepare(tokens, rest_kv)
        held = (*held, forwarded(held[-1]))
        near = after(near, held[1], *known_tables)
        all_tokens = region(share, near[:1, :1], all_tokens, near, other)
        others = range(1, group)
        kv_weights = [gathered(own_slices, (q_width // kv_width, kv_width), 0, [0])]
        kv_weights += from_lines((rest_kv, *held), 0, others)
        q_weights = [gathered(own_slices, (0, q_width), 0, [0]), gathered(rest_q, (0, q_width), 0, others)]
    else:
        all_tokens, known_tables = tokens, tables()
        own = along_lines(slice_for(mine))
        kv_weights = [gathered(own, (q_width // kv_width, kv_width), 0, [0])]
        q_weights = [gathered(own, (0, q_width), 0, [0])]
    cosine, sine, ends, bounds = known_tables

    kv = project(group, place, all_tokens, kv_weights, kv_width, cosine, sine, kv_heads, (0, group))
    hops = -(-halo_rows // group_rows)
    pieces, moving = [], kv
    for hop in range(hops):
        keep = min(halo_rows - hop * group_rows, group_rows)
        moving = moving[moving.shape[0] - keep :]
        moving = lax.ppermute(moving, "ca", [(i, i + group) for i in devices if i + group in devices])
        pieces.insert(0, moving)
    halo = pieces[0] if len(pieces) == 1 else jnp.concatenate(pieces)

    query = project(group, place, all_tokens, q_weights, q_width, cosine, sine, q_width // HEAD_DIM, (0, group))
    result = jnp.zeros((row_count, w_query.shape[1]), jnp.bfloat16)
    for step in reversed(range(group)):
        part = attend(mine ^ step, row_count, query, ends, bounds, halo, kv, kv_heads)
        if step > 0:
            part = to_partner(part, step)
        elif group == 1:
            return part
        result = lax.dynamic_update_slice_in_dim(result, part, (mine ^ step) * q_width, 1)
    return result


def solution(mesh):
    size, cores = mesh.shape["ca"], mesh.shape["tp"]
    local_kv = KV_HEADS // cores
    group = 4 if cores == 2 and local_kv == 4 and size % 4 == 0 else 1
    placed = (P("ca", None), P(), P("ca", "tp"), P("ca", "tp"), P("ca", "tp"))
    body = functools.partial(per_device, group, size // group, cores)
    return jax.shard_map(body, mesh=mesh, in_specs=placed, out_specs=P("ca", "tp"), check_vma=False)
```

```python
import functools
import math

import jax
import jax.numpy as jnp
from jax import lax
from jax.experimental import pallas as pl
from jax.experimental.pallas import tpu as pltpu
from jax.sharding import PartitionSpec as P

HEADS = 32
KV_HEADS = 8
HEAD_DIM = 128
REACH = 3
ROPE_THETA = 500000.0
LOGIT_CAP = 5.0
TILE = 256
UNIT = 128
PUT_BYTES = 20 * 1024 * 1024
PROJECT_BYTES = 30 * 1024 * 1024
VMEM_BYTES = 58 * 1024 * 1024


def doc_starts(lengths, positions):
    doc_ends = jnp.cumsum(lengths).astype(jnp.int32)
    before = doc_ends[None, :] <= positions[:, None]
    return jnp.max(jnp.where(before, doc_ends[None, :], 0), axis=1).astype(jnp.int32)


def rope_tables(offsets):
    half_dim = HEAD_DIM // 2
    frequency = ROPE_THETA ** (-(jnp.arange(half_dim, dtype=jnp.float32) * 2.0) / HEAD_DIM)
    angles = offsets.astype(jnp.float32)[:, None] * frequency[None, :]
    cosine, sine = jnp.cos(angles), jnp.sin(angles)
    return jnp.concatenate([cosine, cosine], axis=1), jnp.concatenate([-sine, sine], axis=1)


def rotated(values, cosine, sine):
    return values * cosine + pltpu.roll(values, HEAD_DIM // 2, 1) * sine


def project_kernel(rope_heads, layout, given, place, x_ref, *refs):
    w_refs = refs[: len(layout)]
    cos_ref, sin_ref = refs[len(layout) : len(layout) + 2]
    out_ref, w_all = refs[len(layout) + 2 + given :]

    @pl.when(pl.program_id(0) == 0)
    def _():
        for ref, (_, column, pieces) in zip(w_refs, layout):
            columns = slice(column, column + ref.shape[1])
            for source, rows, target in pieces:
                at = pl.multiple_of(target(place), rows)
                w_all[pl.ds(at, rows), columns] = ref[source : source + rows, :]

    total = jnp.dot(x_ref[...], w_all[...], preferred_element_type=jnp.float32)
    cosine, sine = cos_ref[...], sin_ref[...]
    for head in range(out_ref.shape[1] // HEAD_DIM):
        columns = slice(head * HEAD_DIM, (head + 1) * HEAD_DIM)
        part = total[:, columns]
        if head < rope_heads:
            part = rotated(part, cosine, sine)
        out_ref[:, columns] = part.astype(out_ref.dtype)


def project(group, place, tokens, weights, width, cosine, sine, rope_heads, span, into=None):
    rows, depth = tokens.shape
    first, count = span
    tile = rows // group
    arrays, blocks, layout = [], [], []
    for array, (block, columns), column, pieces in weights:
        arrays.append(array)
        blocks.append(pl.BlockSpec((array.shape[0], columns), lambda i, s, block=block: (0, block)))
        layout.append((None, column, pieces))

    def row_block(i, s):
        return (s[0] ^ (first + i), 0)

    given = [] if into is None else [into]
    return pl.pallas_call(
        functools.partial(project_kernel, rope_heads, layout, len(given)),
        out_shape=jax.ShapeDtypeStruct((rows, width), jnp.bfloat16),
        grid_spec=pltpu.PrefetchScalarGridSpec(
            num_scalar_prefetch=1,
            grid=(count,),
            in_specs=[pl.BlockSpec((tile, depth), row_block)]
            + blocks
            + [pl.BlockSpec((tile, HEAD_DIM), row_block)] * 2
            + [pl.BlockSpec(memory_space=pl.ANY)] * len(given),
            out_specs=pl.BlockSpec((tile, width), row_block),
            scratch_shapes=[pltpu.VMEM((depth, width), tokens.dtype)],
        ),
        input_output_aliases={} if into is None else {4 + len(arrays): 0},
        compiler_params=pltpu.CompilerParams(vmem_limit_bytes=PROJECT_BYTES),
        cost_estimate=pl.CostEstimate(
            flops=2 * count * tile * depth * width,
            bytes_accessed=2 * depth * (count * tile + width),
            transcendentals=0,
        ),
    )(place, tokens, *arrays, cosine, sine, *given)


def put_kernel(targets, place, *refs):
    sems, out_ref = refs[-1], refs[-2]
    copies = []
    for number, (ref, target) in enumerate(zip(refs, targets)):
        rows = ref.shape[0]
        at = pl.multiple_of(target(place), rows)
        copies.append(pltpu.make_async_copy(ref, out_ref.at[pl.ds(at, rows), :], sems.at[number]))
        copies[-1].start()
    for copy in copies:
        copy.wait()


def put(place, rows, blocks, into=None):
    arrays, targets = [block for block, _ in blocks], [target for _, target in blocks]
    spaces = [pl.BlockSpec(memory_space=pltpu.SMEM)] + [pl.BlockSpec(memory_space=pltpu.VMEM)] * len(arrays)
    aliases = {}
    if into is not None:
        aliases = {1 + len(arrays): 0}
        arrays.append(into)
        spaces.append(pl.BlockSpec(memory_space=pl.ANY))
    return pl.pallas_call(
        functools.partial(put_kernel, targets),
        out_shape=jax.ShapeDtypeStruct((rows, arrays[0].shape[1]), arrays[0].dtype),
        in_specs=spaces,
        out_specs=pl.BlockSpec(memory_space=pl.ANY),
        scratch_shapes=[pltpu.SemaphoreType.DMA((len(targets),))],
        input_output_aliases=aliases,
        compiler_params=pltpu.CompilerParams(vmem_limit_bytes=PUT_BYTES),
    )(place, *arrays)


def attend_kernel(kv_heads, share, halo_rows, first, bounds, ends, q_ref, halo_ref, kv_ref, out_ref, kv_all, q_all, sums, totals):
    tile_index = pl.program_id(0)

    @pl.when(tile_index == 0)
    def _():
        kv_all[:halo_rows, :] = halo_ref[...]
        kv_all[halo_rows:, :] = kv_ref[...]

    tile = q_ref.shape[0]
    for head in range(kv_heads * share):
        q_all[head * tile : (head + 1) * tile, :] = q_ref[:, head * HEAD_DIM : (head + 1) * HEAD_DIM]
    place = bounds[0, first[0] + tile_index]
    first_start = bounds[1, first[0] + tile_index]
    last_start = bounds[2, first[0] + tile_index]
    q_first = halo_rows + place
    lowest = first_start // UNIT * UNIT
    units = (q_first - lowest) // UNIT
    sums[...] = jnp.zeros_like(sums)
    totals[...] = jnp.zeros_like(totals)
    inner = 1.0 / (math.sqrt(HEAD_DIM) * LOGIT_CAP)
    outer = LOGIT_CAP * math.log2(math.e)

    def block_step(begin, size, masked):
        rows = pl.ds(pl.multiple_of(begin, UNIT), size)
        if masked:
            k_ids = begin + lax.broadcasted_iota(jnp.int32, (tile, size), 1)
            q_ids = q_first + lax.broadcasted_iota(jnp.int32, (tile, size), 0)
            begins = jnp.zeros((tile, 1), jnp.int32)
            for number in range(ends.shape[0]):
                begins = jnp.where(q_ids[:, :1] >= ends[number], jnp.maximum(begins, ends[number]), begins)
            allowed = (k_ids <= q_ids) & (k_ids >= begins)
        for kv_head in range(kv_heads):
            keys = kv_all[rows, kv_head * HEAD_DIM : (kv_head + 1) * HEAD_DIM]
            at = (kv_heads + kv_head) * HEAD_DIM
            values = kv_all[rows, at : at + HEAD_DIM]
            members = slice(kv_head * share * tile, (kv_head + 1) * share * tile)
            raw = lax.dot_general(
                q_all[members, :], keys, (((1,), (1,)), ((), ())), preferred_element_type=jnp.float32
            )
            weights = jnp.exp2(outer * jnp.tanh(raw * inner))
            if masked:
                weights = weights.reshape(share, tile, size)
                weights = jnp.where(allowed[None], weights, 0.0).reshape(share * tile, size)
            partial = weights[:, :HEAD_DIM]
            for part in range(1, size // HEAD_DIM):
                partial = partial + weights[:, part * HEAD_DIM : (part + 1) * HEAD_DIM]
            totals[members, :] += partial
            sums[members, :] += jnp.dot(weights.astype(jnp.bfloat16), values, preferred_element_type=jnp.float32)

    def either(begin, size):
        whole = (begin >= last_start) & (begin + size - 1 <= q_first)

        @pl.when(whole)
        def _():
            block_step(begin, size, False)

        @pl.when(jnp.logical_not(whole))
        def _():
            block_step(begin, size, True)

    def long_step(number, carry):
        either(q_first - 4 * UNIT * (number + 1), 4 * UNIT)
        return carry

    block_step(q_first, tile, True)
    lax.fori_loop(0, units // 4, long_step, 0)
    rest = lax.rem(units, 4)

    @pl.when(rest >= 2)
    def _():
        either(lowest + lax.rem(rest, 2) * UNIT, 2 * UNIT)

    @pl.when(lax.rem(rest, 2) == 1)
    def _():
        either(lowest, UNIT)

    for head in range(kv_heads * share):
        rows = slice(head * tile, (head + 1) * tile)
        denominator = jnp.sum(totals[rows, :], axis=1, keepdims=True)
        out_ref[:, head * HEAD_DIM : (head + 1) * HEAD_DIM] = (sums[rows, :] / denominator).astype(out_ref.dtype)


def attend(chunk, chunk_rows, query, ends, bounds, halo, kv, kv_heads):
    width = query.shape[1]
    heads = width // HEAD_DIM
    halo_rows = halo.shape[0]
    tiles = chunk_rows // TILE
    first = (chunk * tiles).reshape(1).astype(jnp.int32)
    kernel = functools.partial(attend_kernel, kv_heads, heads // kv_heads, halo_rows)
    return pl.pallas_call(
        kernel,
        out_shape=jax.ShapeDtypeStruct((chunk_rows, width), jnp.bfloat16),
        grid_spec=pltpu.PrefetchScalarGridSpec(
            num_scalar_prefetch=3,
            grid=(tiles,),
            in_specs=[
                pl.BlockSpec((TILE, width), lambda i, c, s, e: (c[0] + i, 0)),
                pl.BlockSpec(halo.shape, lambda i, c, s, e: (0, 0)),
                pl.BlockSpec(kv.shape, lambda i, c, s, e: (0, 0)),
            ],
            out_specs=pl.BlockSpec((TILE, width), lambda i, c, s, e: (i, 0)),
            scratch_shapes=[
                pltpu.VMEM((halo_rows + kv.shape[0], kv.shape[1]), jnp.bfloat16),
                pltpu.VMEM((heads * TILE, HEAD_DIM), jnp.bfloat16),
                pltpu.VMEM((heads * TILE, HEAD_DIM), jnp.float32),
                pltpu.VMEM((heads * TILE, HEAD_DIM), jnp.float32),
            ],
        ),
        compiler_params=pltpu.CompilerParams(vmem_limit_bytes=VMEM_BYTES),
        cost_estimate=pl.CostEstimate(
            flops=4 * chunk_rows * width * (halo_rows + chunk_rows) // 2,
            bytes_accessed=4 * chunk_rows * width,
            transcendentals=chunk_rows * heads * (halo_rows + chunk_rows),
        ),
    )(first, bounds, ends, query, halo, kv)


def after(block, *others):
    space = pl.BlockSpec(memory_space=pl.ANY)
    return pl.pallas_call(
        lambda *refs: None,
        out_shape=jax.ShapeDtypeStruct(block.shape, block.dtype),
        in_specs=[space] * (1 + len(others)),
        out_specs=space,
        input_output_aliases={0: 0},
    )(block, *others)


def per_device(group, lines, cores, tokens, lengths, w_query, w_key, w_value):
    row_count, depth = tokens.shape
    slice_rows = w_query.shape[0]
    index = lax.axis_index("ca")
    mine, line = index % group, index // group
    core = lax.axis_index("tp")
    q_width = w_query.shape[1] // group
    one_width = w_key.shape[1] // group
    kv_width = 2 * one_width
    kv_heads = one_width // HEAD_DIM
    group_rows = group * row_count
    devices = range(group * lines)

    def slice_for(target):
        return jnp.concatenate(
            [
                lax.dynamic_slice_in_dim(w_query, target * q_width, q_width, 1),
                lax.dynamic_slice_in_dim(w_key, target * one_width, one_width, 1),
                lax.dynamic_slice_in_dim(w_value, target * one_width, one_width, 1),
            ],
            axis=1,
        )

    def to_partner(block, step):
        return lax.ppermute(block, "ca", [(i, i ^ step) for i in devices])

    def along_lines(block):
        lanes = [[place + group * i for i in range(lines)] for place in range(group)]
        return lax.all_gather(block, "ca", axis=0, tiled=True, axis_index_groups=lanes)

    def forwarded(block):
        return lax.ppermute(block, "ca", [(i, (i + group) % (group * lines)) for i in devices])

    def gathered(array, block, column, members):
        if group == 1:
            return (array, block, column, [(0, array.shape[0], lambda s: 0)])
        pieces = []
        for at in range(lines):
            for number, step in enumerate(members):
                source = (at * len(members) + number) * slice_rows
                pieces.append((source, slice_rows, lambda s, at=at, step=step: (at * group + (s[0] ^ step)) * slice_rows))
        return (array, block, column, pieces)

    def from_lines(held, column, members):
        entries = []
        for back, array in enumerate(held):
            pieces = []
            for number, step in enumerate(members):

                def target(s, back=back, step=step):
                    at = lax.rem(s[1] - back + lines, lines)
                    return (at * group + (s[0] ^ step)) * slice_rows

                pieces.append((number * slice_rows, slice_rows, target))
            entries.append((array, (0, array.shape[1]), column, pieces))
        return entries

    half = row_count // 2
    halo_rows = REACH * row_count
    tiles = row_count // TILE

    def tables():
        row_ids = line * group_rows + jnp.arange(group_rows, dtype=jnp.int32)
        starts = doc_starts(lengths, row_ids)
        window_starts = starts - (line * group_rows - halo_rows)
        places = jnp.arange(group * tiles, dtype=jnp.int32) * TILE
        first = window_starts.reshape(group * tiles, TILE)
        bounds = jnp.stack([places, first[:, 0], first[:, -1]])
        cosine, sine = rope_tables(row_ids - starts)
        ends = jnp.cumsum(lengths).astype(jnp.int32) - (line * group_rows - halo_rows)
        return cosine, sine, ends, bounds

    place = jnp.stack([mine, line, core]).astype(jnp.int32)
    if group > 1:
        slices = [slice_for(mine)] + [to_partner(slice_for(mine ^ step), step) for step in range(1, group)]
        own_slices = along_lines(slices[0])
        rest_q = along_lines(jnp.concatenate([a[:, :q_width] for a in slices[1:]]))
        rest_kv = jnp.concatenate([a[:, q_width:] for a in slices[1:]])
        both = ("ca", "tp")

        def cross(block, steps):
            pairs = [(i * 2 + c, (i ^ steps[c]) * 2 + c) for i in devices for c in range(2)]
            return lax.ppermute(block, both, pairs)

        def swap(block):
            return lax.ppermute(block, both, [(i * 2 + c, i * 2 + 1 - c) for i in devices for c in range(2)])

        begin = core * half

        own_half = lax.dynamic_slice_in_dim(tokens, begin, half, 0)

        def home(step_even, step_odd, mate):
            def target(s):
                step = jnp.where(s[2] == mate, step_even, step_odd)
                return (s[0] ^ step) * row_count + jnp.where(mate == 0, s[2], 1 - s[2]) * half

            return target


        others = range(1, group)
        near = cross(own_half, (1, 2))
        other = cross(own_half, (2, 1))

        def prepare(tokens, rest_kv):
            held = [rest_kv]
            for _ in range(1, lines - 1):
                held.append(forwarded(held[-1]))
            return put(place, group_rows, [(tokens, lambda s: s[0] * row_count)]), tables(), tuple(held[1:])

        def share(everything, near, other, own_slices, held, cosine, sine):
            far = cross(near, (2, 1))
            mates = [swap(block) for block in (near, other)]
            first = [(near, home(1, 2, 0)), (mates[0], home(1, 2, 1)), (other, home(2, 1, 0)), (mates[1], home(2, 1, 1))]
            everything = put(place, group_rows, first, everything)
            weights = [gathered(own_slices, (q_width // kv_width, kv_width), 0, [0])] + from_lines(held, 0, others)
            kv = project(group, place, everything, weights, kv_width, cosine, sine, kv_heads, (0, group - 1))
            far = after(far, kv)
            last = [(far, home(3, 3, 0)), (swap(far), home(3, 3, 1))]
            everything = put(place, group_rows, last, everything)
            span = (group - 1, 1)
            return everything, project(group, place, everything, weights, kv_width, cosine, sine, kv_heads, span, kv)

        def region(body, flag, *operands):
            def nothing(*operands):
                shapes = jax.eval_shape(body, *operands)
                return jax.tree.map(lambda leaf: jnp.zeros(leaf.shape, leaf.dtype), shapes)

            known = flag.reshape(-1)[0].astype(jnp.float32)
            return lax.cond(known == known, body, nothing, *operands)

        all_tokens, known_tables, held = prepare(tokens, rest_kv)
        held = (rest_kv, *held, forwarded(held[-1]))
        near = after(near, held[2], *known_tables)
        operands = (all_tokens, near, other, own_slices, held, *known_tables[:2])
        all_tokens, kv = region(share, near[:1, :1], *operands)
        q_weights = [gathered(own_slices, (0, q_width), 0, [0]), gathered(rest_q, (0, q_width), 0, others)]
    else:
        all_tokens, known_tables = tokens, tables()
        own = along_lines(slice_for(mine))
        kv_weights = [gathered(own, (q_width // kv_width, kv_width), 0, [0])]
        q_weights = [gathered(own, (0, q_width), 0, [0])]
        kv = project(group, place, tokens, kv_weights, kv_width, *known_tables[:2], kv_heads, (0, group))
    cosine, sine, ends, bounds = known_tables

    hops = -(-halo_rows // group_rows)
    pieces, moving = [], kv
    for hop in range(hops):
        keep = min(halo_rows - hop * group_rows, group_rows)
        moving = moving[moving.shape[0] - keep :]
        moving = lax.ppermute(moving, "ca", [(i, i + group) for i in devices if i + group in devices])
        pieces.insert(0, moving)
    halo = pieces[0] if len(pieces) == 1 else jnp.concatenate(pieces)

    query = project(group, place, all_tokens, q_weights, q_width, cosine, sine, q_width // HEAD_DIM, (0, group))
    result = jnp.zeros((row_count, w_query.shape[1]), jnp.bfloat16)
    for step in reversed(range(group)):
        part = attend(mine ^ step, row_count, query, ends, bounds, halo, kv, kv_heads)
        if step > 0:
            part = to_partner(part, step)
        elif group == 1:
            return part
        result = lax.dynamic_update_slice_in_dim(result, part, (mine ^ step) * q_width, 1)
    return result


def solution(mesh):
    size, cores = mesh.shape["ca"], mesh.shape["tp"]
    local_kv = KV_HEADS // cores
    group = 4 if cores == 2 and local_kv == 4 and size % 4 == 0 else 1
    placed = (P("ca", None), P(), P("ca", "tp"), P("ca", "tp"), P("ca", "tp"))
    body = functools.partial(per_device, group, size // group, cores)
    return jax.shard_map(body, mesh=mesh, in_specs=placed, out_specs=P("ca", "tp"), check_vma=False)
```

```python
import functools
import math

import jax
import jax.numpy as jnp
from jax import lax
from jax.experimental import pallas as pl
from jax.experimental.pallas import tpu as pltpu
from jax.sharding import PartitionSpec as P

HEADS = 32
KV_HEADS = 8
HEAD_DIM = 128
REACH = 3
ROPE_THETA = 500000.0
LOGIT_CAP = 5.0
TILE = 256
UNIT = 128
PUT_BYTES = 20 * 1024 * 1024
PROJECT_BYTES = 58 * 1024 * 1024
VMEM_BYTES = 58 * 1024 * 1024


def doc_starts(lengths, positions):
    doc_ends = jnp.cumsum(lengths).astype(jnp.int32)
    before = doc_ends[None, :] <= positions[:, None]
    return jnp.max(jnp.where(before, doc_ends[None, :], 0), axis=1).astype(jnp.int32)


def rope_tables(offsets):
    half_dim = HEAD_DIM // 2
    frequency = ROPE_THETA ** (-(jnp.arange(half_dim, dtype=jnp.float32) * 2.0) / HEAD_DIM)
    angles = offsets.astype(jnp.float32)[:, None] * frequency[None, :]
    cosine, sine = jnp.cos(angles), jnp.sin(angles)
    return jnp.concatenate([cosine, cosine], axis=1), jnp.concatenate([-sine, sine], axis=1)


def rotated(values, cosine, sine):
    return values * cosine + pltpu.roll(values, HEAD_DIM // 2, 1) * sine


def project_kernel(rope_heads, layout, given, place, x_ref, *refs):
    w_refs = refs[: len(layout)]
    cos_ref, sin_ref = refs[len(layout) : len(layout) + 2]
    out_ref, w_all = refs[len(layout) + 2 + given :]

    @pl.when(pl.program_id(0) == 0)
    def _():
        for ref, (_, column, pieces) in zip(w_refs, layout):
            columns = slice(column, column + ref.shape[1])
            for source, rows, target in pieces:
                at = pl.multiple_of(target(place), rows)
                w_all[pl.ds(at, rows), columns] = ref[source : source + rows, :]

    total = jnp.dot(x_ref[...], w_all[...], preferred_element_type=jnp.float32)
    cosine, sine = cos_ref[...], sin_ref[...]
    for head in range(out_ref.shape[1] // HEAD_DIM):
        columns = slice(head * HEAD_DIM, (head + 1) * HEAD_DIM)
        part = total[:, columns]
        if head < rope_heads:
            part = rotated(part, cosine, sine)
        out_ref[:, columns] = part.astype(out_ref.dtype)


def project(group, place, tokens, weights, width, cosine, sine, rope_heads, span, into=None):
    rows, depth = tokens.shape
    first, count = span
    tile = rows // group
    arrays, blocks, layout = [], [], []
    for array, (block, columns), column, pieces in weights:
        arrays.append(array)
        blocks.append(pl.BlockSpec((array.shape[0], columns), lambda i, s, block=block: (0, block)))
        layout.append((None, column, pieces))

    def row_block(i, s):
        return (s[0] ^ (first + i), 0)

    given = [] if into is None else [into]
    return pl.pallas_call(
        functools.partial(project_kernel, rope_heads, layout, len(given)),
        out_shape=jax.ShapeDtypeStruct((rows, width), jnp.bfloat16),
        grid_spec=pltpu.PrefetchScalarGridSpec(
            num_scalar_prefetch=1,
            grid=(count,),
            in_specs=[pl.BlockSpec((tile, depth), row_block)]
            + blocks
            + [pl.BlockSpec((tile, HEAD_DIM), row_block)] * 2
            + [pl.BlockSpec(memory_space=pl.ANY)] * len(given),
            out_specs=pl.BlockSpec((tile, width), row_block),
            scratch_shapes=[pltpu.VMEM((depth, width), tokens.dtype)],
        ),
        input_output_aliases={} if into is None else {4 + len(arrays): 0},
        compiler_params=pltpu.CompilerParams(vmem_limit_bytes=PROJECT_BYTES),
        cost_estimate=pl.CostEstimate(
            flops=2 * count * tile * depth * width,
            bytes_accessed=2 * depth * (count * tile + width),
            transcendentals=0,
        ),
    )(place, tokens, *arrays, cosine, sine, *given)


def put_kernel(targets, place, *refs):
    sems, out_ref = refs[-1], refs[-2]
    copies = []
    for number, (ref, target) in enumerate(zip(refs, targets)):
        rows = ref.shape[0]
        at = pl.multiple_of(target(place), rows)
        copies.append(pltpu.make_async_copy(ref, out_ref.at[pl.ds(at, rows), :], sems.at[number]))
        copies[-1].start()
    for copy in copies:
        copy.wait()


def put(place, rows, blocks, into=None):
    arrays, targets = [block for block, _ in blocks], [target for _, target in blocks]
    spaces = [pl.BlockSpec(memory_space=pltpu.SMEM)] + [pl.BlockSpec(memory_space=pltpu.VMEM)] * len(arrays)
    aliases = {}
    if into is not None:
        aliases = {1 + len(arrays): 0}
        arrays.append(into)
        spaces.append(pl.BlockSpec(memory_space=pl.ANY))
    return pl.pallas_call(
        functools.partial(put_kernel, targets),
        out_shape=jax.ShapeDtypeStruct((rows, arrays[0].shape[1]), arrays[0].dtype),
        in_specs=spaces,
        out_specs=pl.BlockSpec(memory_space=pl.ANY),
        scratch_shapes=[pltpu.SemaphoreType.DMA((len(targets),))],
        input_output_aliases=aliases,
        compiler_params=pltpu.CompilerParams(vmem_limit_bytes=PUT_BYTES),
    )(place, *arrays)


def attend_kernel(kv_heads, share, halo_rows, first, bounds, ends, q_ref, halo_ref, kv_ref, out_ref, k_all, v_all, q_all, sums, begins):
    tile_index = pl.program_id(0)
    wide = 2 * HEAD_DIM

    @pl.when(tile_index == 0)
    def _():
        for source, start in ((halo_ref, 0), (kv_ref, halo_rows)):
            rows = slice(start, start + source.shape[0])
            for head in range(kv_heads):
                columns = slice(head * HEAD_DIM, (head + 1) * HEAD_DIM)
                at = (kv_heads + head) * HEAD_DIM
                k_all[rows, columns] = source[:, columns]
                v_all[rows, head * wide : head * wide + HEAD_DIM] = source[:, at : at + HEAD_DIM]
                v_all[rows, head * wide + HEAD_DIM : (head + 1) * wide] = jnp.ones(
                    (source.shape[0], HEAD_DIM), v_all.dtype
                )

    tile = q_ref.shape[0]
    for head in range(kv_heads * share):
        q_all[head * tile : (head + 1) * tile, :] = q_ref[:, head * HEAD_DIM : (head + 1) * HEAD_DIM]
    place = bounds[0, first[0] + tile_index]
    first_start = bounds[1, first[0] + tile_index]
    last_start = bounds[2, first[0] + tile_index]
    q_first = halo_rows + place
    lowest = first_start // UNIT * UNIT
    units = (q_first - lowest) // UNIT
    sums[...] = jnp.zeros_like(sums)
    inner = 1.0 / (math.sqrt(HEAD_DIM) * LOGIT_CAP)
    outer = LOGIT_CAP * math.log2(math.e)
    rows_at = q_first + lax.broadcasted_iota(jnp.int32, (tile, UNIT), 0)
    starts = jnp.zeros((tile, UNIT), jnp.int32)
    for number in range(ends.shape[0]):
        starts = jnp.where(rows_at >= ends[number], jnp.maximum(starts, ends[number]), starts)
    begins[...] = starts

    def block_step(begin, size, masked):
        rows = pl.ds(pl.multiple_of(begin, UNIT), size)
        if masked:
            parts = []
            for part in range(size // UNIT):
                k_ids = begin + part * UNIT + lax.broadcasted_iota(jnp.int32, (tile, UNIT), 1)
                q_ids = q_first + lax.broadcasted_iota(jnp.int32, (tile, UNIT), 0)
                parts.append((k_ids <= q_ids) & (k_ids >= begins[...]))
            allowed = parts[0] if len(parts) == 1 else jnp.concatenate(parts, axis=1)
        for kv_head in range(kv_heads):
            keys = k_all[rows, kv_head * HEAD_DIM : (kv_head + 1) * HEAD_DIM]
            values = v_all[rows, kv_head * wide : (kv_head + 1) * wide]
            members = slice(kv_head * share * tile, (kv_head + 1) * share * tile)
            raw = lax.dot_general(
                q_all[members, :], keys, (((1,), (1,)), ((), ())), preferred_element_type=jnp.float32
            )
            weights = jnp.exp2(outer * jnp.tanh(raw * inner))
            if masked:
                weights = weights.reshape(share, tile, size)
                weights = jnp.where(allowed[None], weights, 0.0).reshape(share * tile, size)
            sums[members, :] += jnp.dot(weights.astype(jnp.bfloat16), values, preferred_element_type=jnp.float32)

    def either(begin, size):
        whole = (begin >= last_start) & (begin + size - 1 <= q_first)

        @pl.when(whole)
        def _():
            block_step(begin, size, False)

        @pl.when(jnp.logical_not(whole))
        def _():
            block_step(begin, size, True)

    def long_step(number, carry):
        either(q_first - 4 * UNIT * (number + 1), 4 * UNIT)
        return carry

    block_step(q_first, tile, True)
    lax.fori_loop(0, units // 4, long_step, 0)
    rest = lax.rem(units, 4)

    @pl.when(rest >= 2)
    def _():
        either(lowest + lax.rem(rest, 2) * UNIT, 2 * UNIT)

    @pl.when(lax.rem(rest, 2) == 1)
    def _():
        either(lowest, UNIT)

    for head in range(kv_heads * share):
        rows = slice(head * tile, (head + 1) * tile)
        mixed = sums[rows, :HEAD_DIM] / sums[rows, HEAD_DIM:]
        out_ref[:, head * HEAD_DIM : (head + 1) * HEAD_DIM] = mixed.astype(out_ref.dtype)


def attend(chunk, chunk_rows, query, ends, bounds, halo, kv, kv_heads):
    width = query.shape[1]
    heads = width // HEAD_DIM
    halo_rows = halo.shape[0]
    tiles = chunk_rows // TILE
    first = (chunk * tiles).reshape(1).astype(jnp.int32)
    kernel = functools.partial(attend_kernel, kv_heads, heads // kv_heads, halo_rows)
    return pl.pallas_call(
        kernel,
        out_shape=jax.ShapeDtypeStruct((chunk_rows, width), jnp.bfloat16),
        grid_spec=pltpu.PrefetchScalarGridSpec(
            num_scalar_prefetch=3,
            grid=(tiles,),
            in_specs=[
                pl.BlockSpec((TILE, width), lambda i, c, s, e: (c[0] + i, 0)),
                pl.BlockSpec(halo.shape, lambda i, c, s, e: (0, 0)),
                pl.BlockSpec(kv.shape, lambda i, c, s, e: (0, 0)),
            ],
            out_specs=pl.BlockSpec((TILE, width), lambda i, c, s, e: (i, 0)),
            scratch_shapes=[
                pltpu.VMEM((halo_rows + kv.shape[0], kv_heads * HEAD_DIM), jnp.bfloat16),
                pltpu.VMEM((halo_rows + kv.shape[0], kv_heads * 2 * HEAD_DIM), jnp.bfloat16),
                pltpu.VMEM((heads * TILE, HEAD_DIM), jnp.bfloat16),
                pltpu.VMEM((heads * TILE, 2 * HEAD_DIM), jnp.float32),
                pltpu.VMEM((TILE, UNIT), jnp.int32),
            ],
        ),
        compiler_params=pltpu.CompilerParams(vmem_limit_bytes=VMEM_BYTES),
        cost_estimate=pl.CostEstimate(
            flops=4 * chunk_rows * width * (halo_rows + chunk_rows) // 2,
            bytes_accessed=4 * chunk_rows * width,
            transcendentals=chunk_rows * heads * (halo_rows + chunk_rows),
        ),
    )(first, bounds, ends, query, halo, kv)


def after(block, *others):
    space = pl.BlockSpec(memory_space=pl.ANY)
    return pl.pallas_call(
        lambda *refs: None,
        out_shape=jax.ShapeDtypeStruct(block.shape, block.dtype),
        in_specs=[space] * (1 + len(others)),
        out_specs=space,
        input_output_aliases={0: 0},
    )(block, *others)


def per_device(group, lines, cores, tokens, lengths, w_query, w_key, w_value):
    row_count, depth = tokens.shape
    slice_rows = w_query.shape[0]
    index = lax.axis_index("ca")
    mine, line = index % group, index // group
    core = lax.axis_index("tp")
    q_width = w_query.shape[1] // group
    one_width = w_key.shape[1] // group
    kv_width = 2 * one_width
    kv_heads = one_width // HEAD_DIM
    group_rows = group * row_count
    devices = range(group * lines)

    def slice_for(target):
        return jnp.concatenate(
            [
                lax.dynamic_slice_in_dim(w_query, target * q_width, q_width, 1),
                lax.dynamic_slice_in_dim(w_key, target * one_width, one_width, 1),
                lax.dynamic_slice_in_dim(w_value, target * one_width, one_width, 1),
            ],
            axis=1,
        )

    def to_partner(block, step):
        return lax.ppermute(block, "ca", [(i, i ^ step) for i in devices])

    def along_lines(block):
        lanes = [[place + group * i for i in range(lines)] for place in range(group)]
        return lax.all_gather(block, "ca", axis=0, tiled=True, axis_index_groups=lanes)

    def forwarded(block):
        return lax.ppermute(block, "ca", [(i, (i + group) % (group * lines)) for i in devices])

    def gathered(array, block, column, members):
        if group == 1:
            return (array, block, column, [(0, array.shape[0], lambda s: 0)])
        pieces = []
        for at in range(lines):
            for number, step in enumerate(members):
                source = (at * len(members) + number) * slice_rows
                pieces.append((source, slice_rows, lambda s, at=at, step=step: (at * group + (s[0] ^ step)) * slice_rows))
        return (array, block, column, pieces)

    def from_lines(held, column, members):
        entries = []
        for back, array in enumerate(held):
            pieces = []
            for number, step in enumerate(members):

                def target(s, back=back, step=step):
                    at = lax.rem(s[1] - back + lines, lines)
                    return (at * group + (s[0] ^ step)) * slice_rows

                pieces.append((number * slice_rows, slice_rows, target))
            entries.append((array, (0, array.shape[1]), column, pieces))
        return entries

    half = row_count // 2
    halo_rows = REACH * row_count
    tiles = row_count // TILE

    def tables():
        row_ids = line * group_rows + jnp.arange(group_rows, dtype=jnp.int32)
        starts = doc_starts(lengths, row_ids)
        window_starts = starts - (line * group_rows - halo_rows)
        places = jnp.arange(group * tiles, dtype=jnp.int32) * TILE
        first = window_starts.reshape(group * tiles, TILE)
        bounds = jnp.stack([places, first[:, 0], first[:, -1]])
        cosine, sine = rope_tables(row_ids - starts)
        ends = jnp.cumsum(lengths).astype(jnp.int32) - (line * group_rows - halo_rows)
        return cosine, sine, ends, bounds

    place = jnp.stack([mine, line, core]).astype(jnp.int32)
    if group > 1:
        slices = [slice_for(mine)] + [to_partner(slice_for(mine ^ step), step) for step in range(1, group)]
        own_slices = along_lines(slices[0])
        rest_q = along_lines(jnp.concatenate([a[:, :q_width] for a in slices[1:]]))
        rest_kv = jnp.concatenate([a[:, q_width:] for a in slices[1:]])
        both = ("ca", "tp")

        def cross(block, steps):
            pairs = [(i * 2 + c, (i ^ steps[c]) * 2 + c) for i in devices for c in range(2)]
            return lax.ppermute(block, both, pairs)

        def swap(block):
            return lax.ppermute(block, both, [(i * 2 + c, i * 2 + 1 - c) for i in devices for c in range(2)])

        begin = core * half

        own_half = lax.dynamic_slice_in_dim(tokens, begin, half, 0)

        def home(step_even, step_odd, mate):
            def target(s):
                step = jnp.where(s[2] == mate, step_even, step_odd)
                return (s[0] ^ step) * row_count + jnp.where(mate == 0, s[2], 1 - s[2]) * half

            return target


        near = cross(own_half, (1, 2))
        other = cross(own_half, (2, 1))

        def prepare(tokens, rest_kv):
            held = [rest_kv]
            for _ in range(1, lines - 1):
                held.append(forwarded(held[-1]))
            return put(place, group_rows, [(tokens, lambda s: s[0] * row_count)]), tables(), tuple(held[1:])

        def share(everything, near, other):
            far = cross(near, (2, 1))
            mates = [swap(block) for block in (near, other)]
            first = [(near, home(1, 2, 0)), (mates[0], home(1, 2, 1)), (other, home(2, 1, 0)), (mates[1], home(2, 1, 1))]
            everything = put(place, group_rows, first, everything)
            far = after(far, everything)
            last = [(far, home(3, 3, 0)), (swap(far), home(3, 3, 1))]
            return put(place, group_rows, last, everything)

        def region(body, flag, *operands):
            def nothing(*operands):
                shapes = jax.eval_shape(body, *operands)
                return jax.tree.map(lambda leaf: jnp.zeros(leaf.shape, leaf.dtype), shapes)

            known = flag.reshape(-1)[0].astype(jnp.float32)
            return lax.cond(known == known, body, nothing, *operands)

        all_tokens, known_tables, held = prepare(tokens, rest_kv)
        held = (*held, forwarded(held[-1]))
        near = after(near, held[1], *known_tables)
        all_tokens = region(share, near[:1, :1], all_tokens, near, other)
        others = range(1, group)
        kv_weights = [gathered(own_slices, (q_width // kv_width, kv_width), 0, [0])]
        kv_weights += from_lines((rest_kv, *held), 0, others)
        q_weights = [gathered(own_slices, (0, q_width), 0, [0]), gathered(rest_q, (0, q_width), 0, others)]
    else:
        all_tokens, known_tables = tokens, tables()
        own = along_lines(slice_for(mine))
        kv_weights = [gathered(own, (q_width // kv_width, kv_width), 0, [0])]
        q_weights = [gathered(own, (0, q_width), 0, [0])]
    cosine, sine, ends, bounds = known_tables

    kv = project(group, place, all_tokens, kv_weights, kv_width, cosine, sine, kv_heads, (0, group))
    hops = -(-halo_rows // group_rows)
    pieces, moving = [], kv
    for hop in range(hops):
        keep = min(halo_rows - hop * group_rows, group_rows)
        moving = moving[moving.shape[0] - keep :]
        moving = lax.ppermute(moving, "ca", [(i, i + group) for i in devices if i + group in devices])
        pieces.insert(0, moving)
    halo = pieces[0] if len(pieces) == 1 else jnp.concatenate(pieces)

    query = project(group, place, all_tokens, q_weights, q_width, cosine, sine, q_width // HEAD_DIM, (0, group))
    result = jnp.zeros((row_count, w_query.shape[1]), jnp.bfloat16)
    for step in reversed(range(group)):
        part = attend(mine ^ step, row_count, query, ends, bounds, halo, kv, kv_heads)
        if step > 0:
            part = to_partner(part, step)
        elif group == 1:
            return part
        result = lax.dynamic_update_slice_in_dim(result, part, (mine ^ step) * q_width, 1)
    return result


def solution(mesh):
    size, cores = mesh.shape["ca"], mesh.shape["tp"]
    local_kv = KV_HEADS // cores
    group = 4 if cores == 2 and local_kv == 4 and size % 4 == 0 else 1
    placed = (P("ca", None), P(), P("ca", "tp"), P("ca", "tp"), P("ca", "tp"))
    body = functools.partial(per_device, group, size // group, cores)
    return jax.shard_map(body, mesh=mesh, in_specs=placed, out_specs=P("ca", "tp"), check_vma=False)
```

```python
import functools
import math

import jax
import jax.numpy as jnp
from jax import lax
from jax.experimental import pallas as pl
from jax.experimental.pallas import tpu as pltpu
from jax.sharding import PartitionSpec as P

HEADS = 32
KV_HEADS = 8
HEAD_DIM = 128
REACH = 3
ROPE_THETA = 500000.0
LOGIT_CAP = 5.0
TILE = 256
UNIT = 128
PUT_BYTES = 20 * 1024 * 1024
PROJECT_BYTES = 58 * 1024 * 1024
VMEM_BYTES = 58 * 1024 * 1024


def doc_starts(lengths, positions):
    doc_ends = jnp.cumsum(lengths).astype(jnp.int32)
    before = doc_ends[None, :] <= positions[:, None]
    return jnp.max(jnp.where(before, doc_ends[None, :], 0), axis=1).astype(jnp.int32)


def rope_tables(offsets):
    half_dim = HEAD_DIM // 2
    frequency = ROPE_THETA ** (-(jnp.arange(half_dim, dtype=jnp.float32) * 2.0) / HEAD_DIM)
    angles = offsets.astype(jnp.float32)[:, None] * frequency[None, :]
    cosine, sine = jnp.cos(angles), jnp.sin(angles)
    return jnp.concatenate([cosine, cosine], axis=1), jnp.concatenate([-sine, sine], axis=1)


def rotated(values, cosine, sine):
    return values * cosine + pltpu.roll(values, HEAD_DIM // 2, 1) * sine


def project_kernel(rope_heads, layout, given, place, x_ref, *refs):
    w_refs = refs[: len(layout)]
    cos_ref, sin_ref = refs[len(layout) : len(layout) + 2]
    out_ref, w_all = refs[len(layout) + 2 + given :]

    @pl.when(pl.program_id(0) == 0)
    def _():
        for ref, (_, column, pieces) in zip(w_refs, layout):
            columns = slice(column, column + ref.shape[1])
            for source, rows, target in pieces:
                at = pl.multiple_of(target(place), rows)
                w_all[pl.ds(at, rows), columns] = ref[source : source + rows, :]

    total = jnp.dot(x_ref[...], w_all[...], preferred_element_type=jnp.float32)
    cosine, sine = cos_ref[...], sin_ref[...]
    for head in range(out_ref.shape[1] // HEAD_DIM):
        columns = slice(head * HEAD_DIM, (head + 1) * HEAD_DIM)
        part = total[:, columns]
        if head < rope_heads:
            part = rotated(part, cosine, sine)
        out_ref[:, columns] = part.astype(out_ref.dtype)


def project(group, place, tokens, weights, width, cosine, sine, rope_heads, span, into=None):
    rows, depth = tokens.shape
    first, count = span
    tile = rows // group
    arrays, blocks, layout = [], [], []
    for array, (block, columns), column, pieces in weights:
        arrays.append(array)
        blocks.append(pl.BlockSpec((array.shape[0], columns), lambda i, s, block=block: (0, block)))
        layout.append((None, column, pieces))

    def row_block(i, s):
        return (s[0] ^ (first + i), 0)

    given = [] if into is None else [into]
    return pl.pallas_call(
        functools.partial(project_kernel, rope_heads, layout, len(given)),
        out_shape=jax.ShapeDtypeStruct((rows, width), jnp.bfloat16),
        grid_spec=pltpu.PrefetchScalarGridSpec(
            num_scalar_prefetch=1,
            grid=(count,),
            in_specs=[pl.BlockSpec((tile, depth), row_block)]
            + blocks
            + [pl.BlockSpec((tile, HEAD_DIM), row_block)] * 2
            + [pl.BlockSpec(memory_space=pl.ANY)] * len(given),
            out_specs=pl.BlockSpec((tile, width), row_block),
            scratch_shapes=[pltpu.VMEM((depth, width), tokens.dtype)],
        ),
        input_output_aliases={} if into is None else {4 + len(arrays): 0},
        compiler_params=pltpu.CompilerParams(vmem_limit_bytes=PROJECT_BYTES),
        cost_estimate=pl.CostEstimate(
            flops=2 * count * tile * depth * width,
            bytes_accessed=2 * depth * (count * tile + width),
            transcendentals=0,
        ),
    )(place, tokens, *arrays, cosine, sine, *given)


def put_kernel(targets, place, *refs):
    sems, out_ref = refs[-1], refs[-2]
    copies = []
    for number, (ref, target) in enumerate(zip(refs, targets)):
        rows = ref.shape[0]
        at = pl.multiple_of(target(place), rows)
        copies.append(pltpu.make_async_copy(ref, out_ref.at[pl.ds(at, rows), :], sems.at[number]))
        copies[-1].start()
    for copy in copies:
        copy.wait()


def put(place, rows, blocks, into=None):
    arrays, targets = [block for block, _ in blocks], [target for _, target in blocks]
    spaces = [pl.BlockSpec(memory_space=pltpu.SMEM)] + [pl.BlockSpec(memory_space=pltpu.VMEM)] * len(arrays)
    aliases = {}
    if into is not None:
        aliases = {1 + len(arrays): 0}
        arrays.append(into)
        spaces.append(pl.BlockSpec(memory_space=pl.ANY))
    return pl.pallas_call(
        functools.partial(put_kernel, targets),
        out_shape=jax.ShapeDtypeStruct((rows, arrays[0].shape[1]), arrays[0].dtype),
        in_specs=spaces,
        out_specs=pl.BlockSpec(memory_space=pl.ANY),
        scratch_shapes=[pltpu.SemaphoreType.DMA((len(targets),))],
        input_output_aliases=aliases,
        compiler_params=pltpu.CompilerParams(vmem_limit_bytes=PUT_BYTES),
        cost_estimate=pl.CostEstimate(
            flops=0, bytes_accessed=sum(4 * block.size for block, _ in blocks), transcendentals=0
        ),
    )(place, *arrays)


def attend_kernel(kv_heads, share, halo_rows, chunk, first, bounds, ends, q_ref, halo_ref, kv_ref, out_ref, k_all, v_all, q_all, sums, begins):
    tile_index = pl.program_id(0)
    wide = 2 * HEAD_DIM

    @pl.when(tile_index == 0)
    def _():
        for source, start in ((halo_ref, 0), (kv_ref, halo_rows)):
            for number in range(source.shape[0] // chunk):
                here = slice(number * chunk, (number + 1) * chunk)
                rows = slice(start + number * chunk, start + (number + 1) * chunk)
                back = halo_rows + bounds[0, first[0]] - rows.start

                @pl.when((back >= 0) & (back <= halo_rows))
                def _(source=source, here=here, rows=rows):
                    for head in range(kv_heads):
                        columns = slice(head * HEAD_DIM, (head + 1) * HEAD_DIM)
                        at = (kv_heads + head) * HEAD_DIM
                        k_all[rows, columns] = source[here, columns]
                        v_all[rows, head * wide : head * wide + HEAD_DIM] = source[here, at : at + HEAD_DIM]
                        v_all[rows, head * wide + HEAD_DIM : (head + 1) * wide] = jnp.ones(
                            (chunk, HEAD_DIM), v_all.dtype
                        )

    tile = q_ref.shape[0]
    for head in range(kv_heads * share):
        q_all[head * tile : (head + 1) * tile, :] = q_ref[:, head * HEAD_DIM : (head + 1) * HEAD_DIM]
    place = bounds[0, first[0] + tile_index]
    first_start = bounds[1, first[0] + tile_index]
    last_start = bounds[2, first[0] + tile_index]
    q_first = halo_rows + place
    lowest = first_start // UNIT * UNIT
    units = (q_first - lowest) // UNIT
    sums[...] = jnp.zeros_like(sums)
    inner = 1.0 / (math.sqrt(HEAD_DIM) * LOGIT_CAP)
    outer = LOGIT_CAP * math.log2(math.e)
    rows_at = q_first + lax.broadcasted_iota(jnp.int32, (tile, UNIT), 0)
    starts = jnp.zeros((tile, UNIT), jnp.int32)
    for number in range(ends.shape[0]):
        starts = jnp.where(rows_at >= ends[number], jnp.maximum(starts, ends[number]), starts)
    begins[...] = starts

    def block_step(begin, size, masked):
        rows = pl.ds(pl.multiple_of(begin, UNIT), size)
        if masked:
            parts = []
            for part in range(size // UNIT):
                k_ids = begin + part * UNIT + lax.broadcasted_iota(jnp.int32, (tile, UNIT), 1)
                q_ids = q_first + lax.broadcasted_iota(jnp.int32, (tile, UNIT), 0)
                parts.append((k_ids <= q_ids) & (k_ids >= begins[...]))
            allowed = parts[0] if len(parts) == 1 else jnp.concatenate(parts, axis=1)
        for kv_head in range(kv_heads):
            keys = k_all[rows, kv_head * HEAD_DIM : (kv_head + 1) * HEAD_DIM]
            values = v_all[rows, kv_head * wide : (kv_head + 1) * wide]
            members = slice(kv_head * share * tile, (kv_head + 1) * share * tile)
            raw = lax.dot_general(
                q_all[members, :], keys, (((1,), (1,)), ((), ())), preferred_element_type=jnp.float32
            )
            weights = jnp.exp2(outer * jnp.tanh(raw * inner))
            if masked:
                weights = weights.reshape(share, tile, size)
                weights = jnp.where(allowed[None], weights, 0.0).reshape(share * tile, size)
            sums[members, :] += jnp.dot(weights.astype(jnp.bfloat16), values, preferred_element_type=jnp.float32)

    def either(begin, size):
        whole = (begin >= last_start) & (begin + size - 1 <= q_first)

        @pl.when(whole)
        def _():
            block_step(begin, size, False)

        @pl.when(jnp.logical_not(whole))
        def _():
            block_step(begin, size, True)

    def long_step(number, carry):
        either(q_first - 4 * UNIT * (number + 1), 4 * UNIT)
        return carry

    block_step(q_first, tile, True)
    lax.fori_loop(0, units // 4, long_step, 0)
    rest = lax.rem(units, 4)

    @pl.when(rest >= 2)
    def _():
        either(lowest + lax.rem(rest, 2) * UNIT, 2 * UNIT)

    @pl.when(lax.rem(rest, 2) == 1)
    def _():
        either(lowest, UNIT)

    for head in range(kv_heads * share):
        rows = slice(head * tile, (head + 1) * tile)
        mixed = sums[rows, :HEAD_DIM] / sums[rows, HEAD_DIM:]
        out_ref[:, head * HEAD_DIM : (head + 1) * HEAD_DIM] = mixed.astype(out_ref.dtype)


def attend(chunk, chunk_rows, query, ends, bounds, halo, kv, kv_heads):
    width = query.shape[1]
    heads = width // HEAD_DIM
    halo_rows = halo.shape[0]
    tiles = chunk_rows // TILE
    first = (chunk * tiles).reshape(1).astype(jnp.int32)
    kernel = functools.partial(attend_kernel, kv_heads, heads // kv_heads, halo_rows, chunk_rows)
    return pl.pallas_call(
        kernel,
        out_shape=jax.ShapeDtypeStruct((chunk_rows, width), jnp.bfloat16),
        grid_spec=pltpu.PrefetchScalarGridSpec(
            num_scalar_prefetch=3,
            grid=(tiles,),
            in_specs=[
                pl.BlockSpec((TILE, width), lambda i, c, s, e: (c[0] + i, 0)),
                pl.BlockSpec(halo.shape, lambda i, c, s, e: (0, 0)),
                pl.BlockSpec(kv.shape, lambda i, c, s, e: (0, 0)),
            ],
            out_specs=pl.BlockSpec((TILE, width), lambda i, c, s, e: (i, 0)),
            scratch_shapes=[
                pltpu.VMEM((halo_rows + kv.shape[0], kv_heads * HEAD_DIM), jnp.bfloat16),
                pltpu.VMEM((halo_rows + kv.shape[0], kv_heads * 2 * HEAD_DIM), jnp.bfloat16),
                pltpu.VMEM((heads * TILE, HEAD_DIM), jnp.bfloat16),
                pltpu.VMEM((heads * TILE, 2 * HEAD_DIM), jnp.float32),
                pltpu.VMEM((TILE, UNIT), jnp.int32),
            ],
        ),
        compiler_params=pltpu.CompilerParams(vmem_limit_bytes=VMEM_BYTES),
        cost_estimate=pl.CostEstimate(
            flops=4 * chunk_rows * width * (halo_rows + chunk_rows) // 2,
            bytes_accessed=4 * chunk_rows * width,
            transcendentals=chunk_rows * heads * (halo_rows + chunk_rows),
        ),
    )(first, bounds, ends, query, halo, kv)


def copied_kernel(block_ref, other_ref, out_ref):
    out_ref[...] = block_ref[...]


def copied_after(block, other):
    return pl.pallas_call(
        copied_kernel,
        out_shape=jax.ShapeDtypeStruct(block.shape, block.dtype),
        in_specs=[pl.BlockSpec(memory_space=pltpu.VMEM), pl.BlockSpec(memory_space=pl.ANY)],
        out_specs=pl.BlockSpec(memory_space=pltpu.VMEM),
        compiler_params=pltpu.CompilerParams(vmem_limit_bytes=PUT_BYTES),
    )(block, other)


def pick_kernel(which, block_ref, out_ref):
    out_ref[...] = block_ref[...]


def pick(which, rows, array):
    return pl.pallas_call(
        pick_kernel,
        out_shape=jax.ShapeDtypeStruct((rows, array.shape[1]), array.dtype),
        grid_spec=pltpu.PrefetchScalarGridSpec(
            num_scalar_prefetch=1,
            grid=(4,),
            in_specs=[pl.BlockSpec((rows // 4, array.shape[1]), lambda i, s: (4 * s[0] + i, 0))],
            out_specs=pl.BlockSpec((rows // 4, array.shape[1]), lambda i, s: (i, 0)),
        ),
    )(which.reshape(1).astype(jnp.int32), array)


def after(block, *others):
    space = pl.BlockSpec(memory_space=pl.ANY)
    return pl.pallas_call(
        lambda *refs: None,
        out_shape=jax.ShapeDtypeStruct(block.shape, block.dtype),
        in_specs=[space] * (1 + len(others)),
        out_specs=space,
        input_output_aliases={0: 0},
    )(block, *others)


def per_device(group, lines, cores, tokens, lengths, w_query, w_key, w_value):
    row_count, depth = tokens.shape
    slice_rows = w_query.shape[0]
    index = lax.axis_index("ca")
    mine, line = index % group, index // group
    core = lax.axis_index("tp")
    q_width = w_query.shape[1] // group
    one_width = w_key.shape[1] // group
    kv_width = 2 * one_width
    kv_heads = one_width // HEAD_DIM
    group_rows = group * row_count
    devices = range(group * lines)

    def slice_for(target):
        return jnp.concatenate(
            [
                lax.dynamic_slice_in_dim(w_query, target * q_width, q_width, 1),
                lax.dynamic_slice_in_dim(w_key, target * one_width, one_width, 1),
                lax.dynamic_slice_in_dim(w_value, target * one_width, one_width, 1),
            ],
            axis=1,
        )

    def to_partner(block, step):
        return lax.ppermute(block, "ca", [(i, i ^ step) for i in devices])

    def along_lines(block):
        lanes = [[place + group * i for i in range(lines)] for place in range(group)]
        return lax.all_gather(block, "ca", axis=0, tiled=True, axis_index_groups=lanes)

    def forwarded(block):
        return lax.ppermute(block, "ca", [(i, (i + group) % (group * lines)) for i in devices])

    def gathered(array, block, column, members):
        if group == 1:
            return (array, block, column, [(0, array.shape[0], lambda s: 0)])
        pieces = []
        for at in range(lines):
            for number, step in enumerate(members):
                source = (at * len(members) + number) * slice_rows
                pieces.append((source, slice_rows, lambda s, at=at, step=step: (at * group + (s[0] ^ step)) * slice_rows))
        return (array, block, column, pieces)

    def from_lines(held, column, members):
        entries = []
        for back, array in enumerate(held):
            pieces = []
            for number, step in enumerate(members):

                def target(s, back=back, step=step):
                    at = lax.rem(s[1] - back + lines, lines)
                    return (at * group + (s[0] ^ step)) * slice_rows

                pieces.append((number * slice_rows, slice_rows, target))
            entries.append((array, (0, array.shape[1]), column, pieces))
        return entries

    half = row_count // 2
    halo_rows = REACH * row_count
    tiles = row_count // TILE

    def tables():
        row_ids = line * group_rows + jnp.arange(group_rows, dtype=jnp.int32)
        starts = doc_starts(lengths, row_ids)
        window_starts = starts - (line * group_rows - halo_rows)
        places = jnp.arange(group * tiles, dtype=jnp.int32) * TILE
        first = window_starts.reshape(group * tiles, TILE)
        bounds = jnp.stack([places, first[:, 0], first[:, -1]])
        cosine, sine = rope_tables(row_ids - starts)
        ends = jnp.cumsum(lengths).astype(jnp.int32) - (line * group_rows - halo_rows)
        return cosine, sine, ends, bounds

    place = jnp.stack([mine, line, core]).astype(jnp.int32)
    if group > 1:
        slices = [slice_for(mine)] + [to_partner(slice_for(mine ^ step), step) for step in range(1, group)]
        own_slices = along_lines(slices[0])
        rest_q = along_lines(jnp.concatenate([a[:, :q_width] for a in slices[1:]]))
        rest_kv = jnp.concatenate([a[:, q_width:] for a in slices[1:]])
        both = ("ca", "tp")

        def cross(block, steps):
            pairs = [(i * 2 + c, (i ^ steps[c]) * 2 + c) for i in devices for c in range(2)]
            return lax.ppermute(block, both, pairs)

        def swap(block):
            return lax.ppermute(block, both, [(i * 2 + c, i * 2 + 1 - c) for i in devices for c in range(2)])


        own_half = pick(core, half, tokens)

        def home(step_even, step_odd, mate):
            def target(s):
                step = jnp.where(s[2] == mate, step_even, step_odd)
                return (s[0] ^ step) * row_count + jnp.where(mate == 0, s[2], 1 - s[2]) * half

            return target


        near = cross(own_half, (1, 2))
        other = cross(own_half, (2, 1))

        def prepare(tokens, rest_kv):
            held = [rest_kv]
            for _ in range(1, lines - 1):
                held.append(forwarded(held[-1]))
            return put(place, group_rows, [(tokens, lambda s: s[0] * row_count)]), tables(), tuple(held[1:])

        def share(everything, near, other):
            far = cross(near, (2, 1))
            mates = [swap(block) for block in (near, other)]
            first = [(near, home(1, 2, 0)), (mates[0], home(1, 2, 1)), (other, home(2, 1, 0)), (mates[1], home(2, 1, 1))]
            everything = put(place, group_rows, first, everything)
            far = copied_after(far, everything)
            last = [(far, home(3, 3, 0)), (swap(far), home(3, 3, 1))]
            return put(place, group_rows, last, everything)

        def region(body, flag, *operands):
            def nothing(*operands):
                shapes = jax.eval_shape(body, *operands)
                return jax.tree.map(lambda leaf: jnp.zeros(leaf.shape, leaf.dtype), shapes)

            known = flag.reshape(-1)[0].astype(jnp.float32)
            return lax.cond(known == known, body, nothing, *operands)

        all_tokens, known_tables, held = prepare(tokens, rest_kv)
        held = (*held, forwarded(held[-1]))
        near = after(near, held[1], *known_tables)
        all_tokens = region(share, rest_kv[:1, :1], all_tokens, near, other)
        others = range(1, group)
        kv_weights = [gathered(own_slices, (q_width // kv_width, kv_width), 0, [0])]
        kv_weights += from_lines((rest_kv, *held), 0, others)
        q_weights = [gathered(own_slices, (0, q_width), 0, [0]), gathered(rest_q, (0, q_width), 0, others)]
    else:
        all_tokens, known_tables = tokens, tables()
        own = along_lines(slice_for(mine))
        kv_weights = [gathered(own, (q_width // kv_width, kv_width), 0, [0])]
        q_weights = [gathered(own, (0, q_width), 0, [0])]
    cosine, sine, ends, bounds = known_tables

    kv = project(group, place, all_tokens, kv_weights, kv_width, cosine, sine, kv_heads, (0, group))
    hops = -(-halo_rows // group_rows)
    pieces, moving = [], kv
    for hop in range(hops):
        keep = min(halo_rows - hop * group_rows, group_rows)
        moving = moving[moving.shape[0] - keep :]
        moving = lax.ppermute(moving, "ca", [(i, i + group) for i in devices if i + group in devices])
        pieces.insert(0, moving)
    halo = pieces[0] if len(pieces) == 1 else jnp.concatenate(pieces)

    query = project(group, place, all_tokens, q_weights, q_width, cosine, sine, q_width // HEAD_DIM, (0, group))
    result = jnp.zeros((row_count, w_query.shape[1]), jnp.bfloat16)
    for step in reversed(range(group)):
        part = attend(mine ^ step, row_count, query, ends, bounds, halo, kv, kv_heads)
        if step > 0:
            part = to_partner(part, step)
        elif group == 1:
            return part
        result = lax.dynamic_update_slice_in_dim(result, part, (mine ^ step) * q_width, 1)
    return result


def solution(mesh):
    size, cores = mesh.shape["ca"], mesh.shape["tp"]
    local_kv = KV_HEADS // cores
    group = 4 if cores == 2 and local_kv == 4 and size % 4 == 0 else 1
    placed = (P("ca", None), P(), P("ca", "tp"), P("ca", "tp"), P("ca", "tp"))
    body = functools.partial(per_device, group, size // group, cores)
    return jax.shard_map(body, mesh=mesh, in_specs=placed, out_specs=P("ca", "tp"), check_vma=False)
```

```python
import functools
import math

import jax
import jax.numpy as jnp
from jax import lax
from jax.experimental import pallas as pl
from jax.experimental.pallas import tpu as pltpu
from jax.sharding import PartitionSpec as P

HEADS = 32
KV_HEADS = 8
HEAD_DIM = 128
REACH = 3
ROPE_THETA = 500000.0
LOGIT_CAP = 5.0
TILE = 256
UNIT = 128
PUT_BYTES = 20 * 1024 * 1024
PROJECT_BYTES = 58 * 1024 * 1024
VMEM_BYTES = 58 * 1024 * 1024


def doc_starts(lengths, positions):
    doc_ends = jnp.cumsum(lengths).astype(jnp.int32)
    before = doc_ends[None, :] <= positions[:, None]
    return jnp.max(jnp.where(before, doc_ends[None, :], 0), axis=1).astype(jnp.int32)


def rope_tables(offsets):
    half_dim = HEAD_DIM // 2
    frequency = ROPE_THETA ** (-(jnp.arange(half_dim, dtype=jnp.float32) * 2.0) / HEAD_DIM)
    angles = offsets.astype(jnp.float32)[:, None] * frequency[None, :]
    cosine, sine = jnp.cos(angles), jnp.sin(angles)
    return jnp.concatenate([cosine, cosine], axis=1), jnp.concatenate([-sine, sine], axis=1)


def rotated(values, cosine, sine):
    return values * cosine + pltpu.roll(values, HEAD_DIM // 2, 1) * sine


def project_kernel(rope_heads, layout, given, place, x_ref, *refs):
    w_refs = refs[: len(layout)]
    cos_ref, sin_ref = refs[len(layout) : len(layout) + 2]
    out_ref, w_all = refs[len(layout) + 2 + given :]

    @pl.when(pl.program_id(0) == 0)
    def _():
        for ref, (_, column, pieces) in zip(w_refs, layout):
            columns = slice(column, column + ref.shape[1])
            for source, rows, target in pieces:
                at = pl.multiple_of(target(place), rows)
                w_all[pl.ds(at, rows), columns] = ref[source : source + rows, :]

    total = jnp.dot(x_ref[...], w_all[...], preferred_element_type=jnp.float32)
    cosine, sine = cos_ref[...], sin_ref[...]
    for head in range(out_ref.shape[1] // HEAD_DIM):
        columns = slice(head * HEAD_DIM, (head + 1) * HEAD_DIM)
        part = total[:, columns]
        if head < rope_heads:
            part = rotated(part, cosine, sine)
        out_ref[:, columns] = part.astype(out_ref.dtype)


def project(group, place, tokens, weights, width, cosine, sine, rope_heads, span, into=None):
    rows, depth = tokens.shape
    first, count = span
    tile = rows // group
    arrays, blocks, layout = [], [], []
    for array, (block, columns), column, pieces in weights:
        arrays.append(array)
        blocks.append(pl.BlockSpec((array.shape[0], columns), lambda i, s, block=block: (0, block)))
        layout.append((None, column, pieces))

    def row_block(i, s):
        return (s[0] ^ (first + i), 0)

    given = [] if into is None else [into]
    return pl.pallas_call(
        functools.partial(project_kernel, rope_heads, layout, len(given)),
        out_shape=jax.ShapeDtypeStruct((rows, width), jnp.bfloat16),
        grid_spec=pltpu.PrefetchScalarGridSpec(
            num_scalar_prefetch=1,
            grid=(count,),
            in_specs=[pl.BlockSpec((tile, depth), row_block)]
            + blocks
            + [pl.BlockSpec((tile, HEAD_DIM), row_block)] * 2
            + [pl.BlockSpec(memory_space=pl.ANY)] * len(given),
            out_specs=pl.BlockSpec((tile, width), row_block),
            scratch_shapes=[pltpu.VMEM((depth, width), tokens.dtype)],
        ),
        input_output_aliases={} if into is None else {4 + len(arrays): 0},
        compiler_params=pltpu.CompilerParams(vmem_limit_bytes=PROJECT_BYTES),
        cost_estimate=pl.CostEstimate(
            flops=2 * count * tile * depth * width,
            bytes_accessed=2 * depth * (count * tile + width),
            transcendentals=0,
        ),
    )(place, tokens, *arrays, cosine, sine, *given)


def put_kernel(targets, place, *refs):
    sems, out_ref = refs[-1], refs[-2]
    copies = []
    for number, (ref, target) in enumerate(zip(refs, targets)):
        rows = ref.shape[0]
        at = pl.multiple_of(target(place), rows)
        copies.append(pltpu.make_async_copy(ref, out_ref.at[pl.ds(at, rows), :], sems.at[number]))
        copies[-1].start()
    for copy in copies:
        copy.wait()


def put(place, rows, blocks, into=None):
    arrays, targets = [block for block, _ in blocks], [target for _, target in blocks]
    spaces = [pl.BlockSpec(memory_space=pltpu.SMEM)] + [pl.BlockSpec(memory_space=pltpu.VMEM)] * len(arrays)
    aliases = {}
    if into is not None:
        aliases = {1 + len(arrays): 0}
        arrays.append(into)
        spaces.append(pl.BlockSpec(memory_space=pl.ANY))
    return pl.pallas_call(
        functools.partial(put_kernel, targets),
        out_shape=jax.ShapeDtypeStruct((rows, arrays[0].shape[1]), arrays[0].dtype),
        in_specs=spaces,
        out_specs=pl.BlockSpec(memory_space=pl.ANY),
        scratch_shapes=[pltpu.SemaphoreType.DMA((len(targets),))],
        input_output_aliases=aliases,
        compiler_params=pltpu.CompilerParams(vmem_limit_bytes=PUT_BYTES),
        cost_estimate=pl.CostEstimate(
            flops=0, bytes_accessed=sum(4 * block.size for block, _ in blocks), transcendentals=0
        ),
    )(place, *arrays)


def attend_kernel(kv_heads, share, halo_rows, chunk, first, bounds, ends, q_ref, halo_ref, kv_ref, out_ref, k_all, v_all, q_all, sums, begins):
    tile_index = pl.program_id(0)
    wide = 2 * HEAD_DIM

    @pl.when(tile_index == 0)
    def _():
        for source, start in ((halo_ref, 0), (kv_ref, halo_rows)):
            for number in range(source.shape[0] // chunk):
                here = slice(number * chunk, (number + 1) * chunk)
                rows = slice(start + number * chunk, start + (number + 1) * chunk)
                back = halo_rows + bounds[0, first[0]] - rows.start

                @pl.when((back >= 0) & (back <= halo_rows))
                def _(source=source, here=here, rows=rows):
                    for head in range(kv_heads):
                        columns = slice(head * HEAD_DIM, (head + 1) * HEAD_DIM)
                        at = (kv_heads + head) * HEAD_DIM
                        k_all[rows, columns] = source[here, columns]
                        v_all[rows, head * wide : head * wide + HEAD_DIM] = source[here, at : at + HEAD_DIM]
                        v_all[rows, head * wide + HEAD_DIM : (head + 1) * wide] = jnp.ones(
                            (chunk, HEAD_DIM), v_all.dtype
                        )

    tile = q_ref.shape[0]
    for head in range(kv_heads * share):
        q_all[head * tile : (head + 1) * tile, :] = q_ref[:, head * HEAD_DIM : (head + 1) * HEAD_DIM]
    place = bounds[0, first[0] + tile_index]
    first_start = bounds[1, first[0] + tile_index]
    last_start = bounds[2, first[0] + tile_index]
    q_first = halo_rows + place
    lowest = first_start // UNIT * UNIT
    units = (q_first - lowest) // UNIT
    sums[...] = jnp.zeros_like(sums)
    inner = 1.0 / (math.sqrt(HEAD_DIM) * LOGIT_CAP)
    outer = LOGIT_CAP * math.log2(math.e)
    rows_at = q_first + lax.broadcasted_iota(jnp.int32, (tile, UNIT), 0)
    starts = jnp.zeros((tile, UNIT), jnp.int32)
    for number in range(ends.shape[0]):
        starts = jnp.where(rows_at >= ends[number], jnp.maximum(starts, ends[number]), starts)
    begins[...] = starts

    def block_step(begin, size, masked):
        rows = pl.ds(pl.multiple_of(begin, UNIT), size)
        if masked:
            parts = []
            for part in range(size // UNIT):
                k_ids = begin + part * UNIT + lax.broadcasted_iota(jnp.int32, (tile, UNIT), 1)
                q_ids = q_first + lax.broadcasted_iota(jnp.int32, (tile, UNIT), 0)
                parts.append((k_ids <= q_ids) & (k_ids >= begins[...]))
            allowed = parts[0] if len(parts) == 1 else jnp.concatenate(parts, axis=1)
        for kv_head in range(kv_heads):
            keys = k_all[rows, kv_head * HEAD_DIM : (kv_head + 1) * HEAD_DIM]
            values = v_all[rows, kv_head * wide : (kv_head + 1) * wide]
            members = slice(kv_head * share * tile, (kv_head + 1) * share * tile)
            raw = lax.dot_general(
                q_all[members, :], keys, (((1,), (1,)), ((), ())), preferred_element_type=jnp.float32
            )
            weights = jnp.exp2(outer * jnp.tanh(raw * inner))
            if masked:
                weights = weights.reshape(share, tile, size)
                weights = jnp.where(allowed[None], weights, 0.0).reshape(share * tile, size)
            sums[members, :] += jnp.dot(weights.astype(jnp.bfloat16), values, preferred_element_type=jnp.float32)

    def either(begin, size):
        whole = (begin >= last_start) & (begin + size - 1 <= q_first)

        @pl.when(whole)
        def _():
            block_step(begin, size, False)

        @pl.when(jnp.logical_not(whole))
        def _():
            block_step(begin, size, True)

    def long_step(number, carry):
        either(q_first - 4 * UNIT * (number + 1), 4 * UNIT)
        return carry

    block_step(q_first, tile, True)
    lax.fori_loop(0, units // 4, long_step, 0)
    rest = lax.rem(units, 4)

    @pl.when(rest >= 2)
    def _():
        either(lowest + lax.rem(rest, 2) * UNIT, 2 * UNIT)

    @pl.when(lax.rem(rest, 2) == 1)
    def _():
        either(lowest, UNIT)

    for head in range(kv_heads * share):
        rows = slice(head * tile, (head + 1) * tile)
        mixed = sums[rows, :HEAD_DIM] / sums[rows, HEAD_DIM:]
        out_ref[:, head * HEAD_DIM : (head + 1) * HEAD_DIM] = mixed.astype(out_ref.dtype)


def attend(chunk, chunk_rows, query, ends, bounds, halo, kv, kv_heads):
    width = query.shape[1]
    heads = width // HEAD_DIM
    halo_rows = halo.shape[0]
    tiles = chunk_rows // TILE
    first = (chunk * tiles).reshape(1).astype(jnp.int32)
    kernel = functools.partial(attend_kernel, kv_heads, heads // kv_heads, halo_rows, chunk_rows)
    return pl.pallas_call(
        kernel,
        out_shape=jax.ShapeDtypeStruct((chunk_rows, width), jnp.bfloat16),
        grid_spec=pltpu.PrefetchScalarGridSpec(
            num_scalar_prefetch=3,
            grid=(tiles,),
            in_specs=[
                pl.BlockSpec((TILE, width), lambda i, c, s, e: (c[0] + i, 0)),
                pl.BlockSpec(halo.shape, lambda i, c, s, e: (0, 0)),
                pl.BlockSpec(kv.shape, lambda i, c, s, e: (0, 0)),
            ],
            out_specs=pl.BlockSpec((TILE, width), lambda i, c, s, e: (i, 0)),
            scratch_shapes=[
                pltpu.VMEM((halo_rows + kv.shape[0], kv_heads * HEAD_DIM), jnp.bfloat16),
                pltpu.VMEM((halo_rows + kv.shape[0], kv_heads * 2 * HEAD_DIM), jnp.bfloat16),
                pltpu.VMEM((heads * TILE, HEAD_DIM), jnp.bfloat16),
                pltpu.VMEM((heads * TILE, 2 * HEAD_DIM), jnp.float32),
                pltpu.VMEM((TILE, UNIT), jnp.int32),
            ],
        ),
        compiler_params=pltpu.CompilerParams(vmem_limit_bytes=VMEM_BYTES),
        cost_estimate=pl.CostEstimate(
            flops=4 * chunk_rows * width * (halo_rows + chunk_rows) // 2,
            bytes_accessed=4 * chunk_rows * width,
            transcendentals=chunk_rows * heads * (halo_rows + chunk_rows),
        ),
    )(first, bounds, ends, query, halo, kv)


def copied_kernel(block_ref, other_ref, out_ref):
    out_ref[...] = block_ref[...]


def copied_after(block, other):
    return pl.pallas_call(
        copied_kernel,
        out_shape=jax.ShapeDtypeStruct(block.shape, block.dtype),
        in_specs=[pl.BlockSpec(memory_space=pltpu.VMEM), pl.BlockSpec(memory_space=pl.ANY)],
        out_specs=pl.BlockSpec(memory_space=pltpu.VMEM),
        compiler_params=pltpu.CompilerParams(vmem_limit_bytes=PUT_BYTES),
    )(block, other)


def after(block, *others):
    space = pl.BlockSpec(memory_space=pl.ANY)
    return pl.pallas_call(
        lambda *refs: None,
        out_shape=jax.ShapeDtypeStruct(block.shape, block.dtype),
        in_specs=[space] * (1 + len(others)),
        out_specs=space,
        input_output_aliases={0: 0},
    )(block, *others)


def per_device(group, lines, cores, tokens, lengths, w_query, w_key, w_value):
    row_count, depth = tokens.shape
    slice_rows = w_query.shape[0]
    index = lax.axis_index("ca")
    mine, line = index % group, index // group
    core = lax.axis_index("tp")
    q_width = w_query.shape[1] // group
    one_width = w_key.shape[1] // group
    kv_width = 2 * one_width
    kv_heads = one_width // HEAD_DIM
    group_rows = group * row_count
    devices = range(group * lines)

    def slice_for(target):
        return jnp.concatenate(
            [
                lax.dynamic_slice_in_dim(w_query, target * q_width, q_width, 1),
                lax.dynamic_slice_in_dim(w_key, target * one_width, one_width, 1),
                lax.dynamic_slice_in_dim(w_value, target * one_width, one_width, 1),
            ],
            axis=1,
        )

    def to_partner(block, step):
        return lax.ppermute(block, "ca", [(i, i ^ step) for i in devices])

    def along_lines(block):
        lanes = [[place + group * i for i in range(lines)] for place in range(group)]
        return lax.all_gather(block, "ca", axis=0, tiled=True, axis_index_groups=lanes)

    def forwarded(block):
        return lax.ppermute(block, "ca", [(i, (i + group) % (group * lines)) for i in devices])

    def gathered(array, block, column, members):
        if group == 1:
            return (array, block, column, [(0, array.shape[0], lambda s: 0)])
        pieces = []
        for at in range(lines):
            for number, step in enumerate(members):
                source = (at * len(members) + number) * slice_rows
                pieces.append((source, slice_rows, lambda s, at=at, step=step: (at * group + (s[0] ^ step)) * slice_rows))
        return (array, block, column, pieces)

    def from_lines(held, column, members):
        entries = []
        for back, array in enumerate(held):
            pieces = []
            for number, step in enumerate(members):

                def target(s, back=back, step=step):
                    at = lax.rem(s[1] - back + lines, lines)
                    return (at * group + (s[0] ^ step)) * slice_rows

                pieces.append((number * slice_rows, slice_rows, target))
            entries.append((array, (0, array.shape[1]), column, pieces))
        return entries

    half = row_count // 2
    halo_rows = REACH * row_count
    tiles = row_count // TILE

    def tables():
        row_ids = line * group_rows + jnp.arange(group_rows, dtype=jnp.int32)
        starts = doc_starts(lengths, row_ids)
        window_starts = starts - (line * group_rows - halo_rows)
        places = jnp.arange(group * tiles, dtype=jnp.int32) * TILE
        first = window_starts.reshape(group * tiles, TILE)
        bounds = jnp.stack([places, first[:, 0], first[:, -1]])
        cosine, sine = rope_tables(row_ids - starts)
        ends = jnp.cumsum(lengths).astype(jnp.int32) - (line * group_rows - halo_rows)
        return cosine, sine, ends, bounds

    place = jnp.stack([mine, line, core]).astype(jnp.int32)
    if group > 1:
        own_half = lax.dynamic_slice_in_dim(tokens, core * half, half, 0)
        leaving = [slice_for(mine ^ step) for step in range(1, group)]
        leaving[-1] = after(leaving[-1], own_half)
        slices = [slice_for(mine)] + [to_partner(block, step) for step, block in enumerate(leaving, 1)]
        own_slices = along_lines(slices[0])
        rest_q = along_lines(jnp.concatenate([a[:, :q_width] for a in slices[1:]]))
        rest_kv = jnp.concatenate([a[:, q_width:] for a in slices[1:]])
        both = ("ca", "tp")

        def cross(block, steps):
            pairs = [(i * 2 + c, (i ^ steps[c]) * 2 + c) for i in devices for c in range(2)]
            return lax.ppermute(block, both, pairs)

        def swap(block):
            return lax.ppermute(block, both, [(i * 2 + c, i * 2 + 1 - c) for i in devices for c in range(2)])


        def home(step_even, step_odd, mate):
            def target(s):
                step = jnp.where(s[2] == mate, step_even, step_odd)
                return (s[0] ^ step) * row_count + jnp.where(mate == 0, s[2], 1 - s[2]) * half

            return target


        near = cross(own_half, (1, 2))
        other = cross(own_half, (2, 1))

        def prepare(tokens, rest_kv):
            held = [rest_kv]
            for _ in range(1, lines - 1):
                held.append(forwarded(held[-1]))
            return put(place, group_rows, [(tokens, lambda s: s[0] * row_count)]), tables(), tuple(held[1:])

        def share(everything, near, other):
            far = cross(near, (2, 1))
            mates = [swap(block) for block in (near, other)]
            first = [(near, home(1, 2, 0)), (mates[0], home(1, 2, 1)), (other, home(2, 1, 0)), (mates[1], home(2, 1, 1))]
            everything = put(place, group_rows, first, everything)
            far = copied_after(far, everything)
            last = [(far, home(3, 3, 0)), (swap(far), home(3, 3, 1))]
            return put(place, group_rows, last, everything)

        def region(body, flag, *operands):
            def nothing(*operands):
                shapes = jax.eval_shape(body, *operands)
                return jax.tree.map(lambda leaf: jnp.zeros(leaf.shape, leaf.dtype), shapes)

            known = flag.reshape(-1)[0].astype(jnp.float32)
            return lax.cond(known == known, body, nothing, *operands)

        all_tokens, known_tables, held = prepare(tokens, rest_kv)
        held = (*held, forwarded(held[-1]))
        near = after(near, held[1], *known_tables)
        all_tokens = region(share, rest_kv[:1, :1], all_tokens, near, other)
        others = range(1, group)
        kv_weights = [gathered(own_slices, (q_width // kv_width, kv_width), 0, [0])]
        kv_weights += from_lines((rest_kv, *held), 0, others)
        q_weights = [gathered(own_slices, (0, q_width), 0, [0]), gathered(rest_q, (0, q_width), 0, others)]
    else:
        all_tokens, known_tables = tokens, tables()
        own = along_lines(slice_for(mine))
        kv_weights = [gathered(own, (q_width // kv_width, kv_width), 0, [0])]
        q_weights = [gathered(own, (0, q_width), 0, [0])]
    cosine, sine, ends, bounds = known_tables

    kv = project(group, place, all_tokens, kv_weights, kv_width, cosine, sine, kv_heads, (0, group))
    hops = -(-halo_rows // group_rows)
    pieces, moving = [], kv
    for hop in range(hops):
        keep = min(halo_rows - hop * group_rows, group_rows)
        moving = moving[moving.shape[0] - keep :]
        moving = lax.ppermute(moving, "ca", [(i, i + group) for i in devices if i + group in devices])
        pieces.insert(0, moving)
    halo = pieces[0] if len(pieces) == 1 else jnp.concatenate(pieces)

    query = project(group, place, all_tokens, q_weights, q_width, cosine, sine, q_width // HEAD_DIM, (0, group))
    result = jnp.zeros((row_count, w_query.shape[1]), jnp.bfloat16)
    for step in reversed(range(group)):
        part = attend(mine ^ step, row_count, query, ends, bounds, halo, kv, kv_heads)
        if step > 0:
            part = to_partner(part, step)
        elif group == 1:
            return part
        result = lax.dynamic_update_slice_in_dim(result, part, (mine ^ step) * q_width, 1)
    return result


def solution(mesh):
    size, cores = mesh.shape["ca"], mesh.shape["tp"]
    local_kv = KV_HEADS // cores
    group = 4 if cores == 2 and local_kv == 4 and size % 4 == 0 else 1
    placed = (P("ca", None), P(), P("ca", "tp"), P("ca", "tp"), P("ca", "tp"))
    body = functools.partial(per_device, group, size // group, cores)
    return jax.shard_map(body, mesh=mesh, in_specs=placed, out_specs=P("ca", "tp"), check_vma=False)
```

```python
import functools
import math

import jax
import jax.numpy as jnp
from jax import lax
from jax.experimental import pallas as pl
from jax.experimental.pallas import tpu as pltpu
from jax.sharding import PartitionSpec as P

HEADS = 32
KV_HEADS = 8
HEAD_DIM = 128
REACH = 3
ROPE_THETA = 500000.0
LOGIT_CAP = 5.0
TILE = 256
UNIT = 128
PUT_BYTES = 20 * 1024 * 1024
PROJECT_BYTES = 58 * 1024 * 1024
VMEM_BYTES = 58 * 1024 * 1024


def doc_starts(lengths, positions):
    doc_ends = jnp.cumsum(lengths).astype(jnp.int32)
    before = doc_ends[None, :] <= positions[:, None]
    return jnp.max(jnp.where(before, doc_ends[None, :], 0), axis=1).astype(jnp.int32)


def rope_tables(offsets):
    half_dim = HEAD_DIM // 2
    frequency = ROPE_THETA ** (-(jnp.arange(half_dim, dtype=jnp.float32) * 2.0) / HEAD_DIM)
    angles = offsets.astype(jnp.float32)[:, None] * frequency[None, :]
    cosine, sine = jnp.cos(angles), jnp.sin(angles)
    return jnp.concatenate([cosine, cosine], axis=1), jnp.concatenate([-sine, sine], axis=1)


def rotated(values, cosine, sine):
    return values * cosine + pltpu.roll(values, HEAD_DIM // 2, 1) * sine


def project_kernel(rope_heads, layout, given, place, x_ref, *refs):
    w_refs = refs[: len(layout)]
    cos_ref, sin_ref = refs[len(layout) : len(layout) + 2]
    out_ref, w_all = refs[len(layout) + 2 + given :]

    @pl.when(pl.program_id(0) == 0)
    def _():
        for ref, (_, column, pieces) in zip(w_refs, layout):
            columns = slice(column, column + ref.shape[1])
            for source, rows, target in pieces:
                at = pl.multiple_of(target(place), rows)
                w_all[pl.ds(at, rows), columns] = ref[source : source + rows, :]

    total = jnp.dot(x_ref[...], w_all[...], preferred_element_type=jnp.float32)
    cosine, sine = cos_ref[...], sin_ref[...]
    for head in range(out_ref.shape[1] // HEAD_DIM):
        columns = slice(head * HEAD_DIM, (head + 1) * HEAD_DIM)
        part = total[:, columns]
        if head < rope_heads:
            part = rotated(part, cosine, sine)
        out_ref[:, columns] = part.astype(out_ref.dtype)


def project(group, place, tokens, weights, width, cosine, sine, rope_heads, span, into=None):
    rows, depth = tokens.shape
    first, count = span
    tile = rows // group
    arrays, blocks, layout = [], [], []
    for array, (block, columns), column, pieces in weights:
        arrays.append(array)
        blocks.append(pl.BlockSpec((array.shape[0], columns), lambda i, s, block=block: (0, block)))
        layout.append((None, column, pieces))

    def row_block(i, s):
        return (s[0] ^ (first + i), 0)

    given = [] if into is None else [into]
    return pl.pallas_call(
        functools.partial(project_kernel, rope_heads, layout, len(given)),
        out_shape=jax.ShapeDtypeStruct((rows, width), jnp.bfloat16),
        grid_spec=pltpu.PrefetchScalarGridSpec(
            num_scalar_prefetch=1,
            grid=(count,),
            in_specs=[pl.BlockSpec((tile, depth), row_block)]
            + blocks
            + [pl.BlockSpec((tile, HEAD_DIM), row_block)] * 2
            + [pl.BlockSpec(memory_space=pl.ANY)] * len(given),
            out_specs=pl.BlockSpec((tile, width), row_block),
            scratch_shapes=[pltpu.VMEM((depth, width), tokens.dtype)],
        ),
        input_output_aliases={} if into is None else {4 + len(arrays): 0},
        compiler_params=pltpu.CompilerParams(vmem_limit_bytes=PROJECT_BYTES),
        cost_estimate=pl.CostEstimate(
            flops=2 * count * tile * depth * width,
            bytes_accessed=2 * depth * (count * tile + width),
            transcendentals=0,
        ),
    )(place, tokens, *arrays, cosine, sine, *given)


def put_kernel(targets, place, *refs):
    sems, out_ref = refs[-1], refs[-2]
    copies = []
    for number, (ref, target) in enumerate(zip(refs, targets)):
        rows = ref.shape[0]
        at = pl.multiple_of(target(place), rows)
        copies.append(pltpu.make_async_copy(ref, out_ref.at[pl.ds(at, rows), :], sems.at[number]))
        copies[-1].start()
    for copy in copies:
        copy.wait()


def put(place, rows, blocks, into=None):
    arrays, targets = [block for block, _ in blocks], [target for _, target in blocks]
    spaces = [pl.BlockSpec(memory_space=pltpu.SMEM)] + [pl.BlockSpec(memory_space=pltpu.VMEM)] * len(arrays)
    aliases = {}
    if into is not None:
        aliases = {1 + len(arrays): 0}
        arrays.append(into)
        spaces.append(pl.BlockSpec(memory_space=pl.ANY))
    return pl.pallas_call(
        functools.partial(put_kernel, targets),
        out_shape=jax.ShapeDtypeStruct((rows, arrays[0].shape[1]), arrays[0].dtype),
        in_specs=spaces,
        out_specs=pl.BlockSpec(memory_space=pl.ANY),
        scratch_shapes=[pltpu.SemaphoreType.DMA((len(targets),))],
        input_output_aliases=aliases,
        compiler_params=pltpu.CompilerParams(vmem_limit_bytes=PUT_BYTES),
        cost_estimate=pl.CostEstimate(
            flops=0, bytes_accessed=sum(4 * block.size for block, _ in blocks), transcendentals=0
        ),
    )(place, *arrays)


def attend_kernel(kv_heads, share, halo_rows, chunk, first, bounds, ends, q_ref, halo_ref, kv_ref, out_ref, k_all, v_all, q_all, sums, begins):
    tile_index = pl.program_id(0)
    wide = 2 * HEAD_DIM

    @pl.when(tile_index == 0)
    def _():
        for source, start in ((halo_ref, 0), (kv_ref, halo_rows)):
            for number in range(source.shape[0] // chunk):
                here = slice(number * chunk, (number + 1) * chunk)
                rows = slice(start + number * chunk, start + (number + 1) * chunk)
                back = halo_rows + bounds[0, first[0]] - rows.start

                @pl.when((back >= 0) & (back <= halo_rows))
                def _(source=source, here=here, rows=rows):
                    for head in range(kv_heads):
                        columns = slice(head * HEAD_DIM, (head + 1) * HEAD_DIM)
                        at = (kv_heads + head) * HEAD_DIM
                        k_all[rows, columns] = source[here, columns]
                        v_all[rows, head * wide : head * wide + HEAD_DIM] = source[here, at : at + HEAD_DIM]
                        v_all[rows, head * wide + HEAD_DIM : (head + 1) * wide] = jnp.ones(
                            (chunk, HEAD_DIM), v_all.dtype
                        )

    tile = q_ref.shape[0]
    for head in range(kv_heads * share):
        q_all[head * tile : (head + 1) * tile, :] = q_ref[:, head * HEAD_DIM : (head + 1) * HEAD_DIM]
    place = bounds[0, first[0] + tile_index]
    first_start = bounds[1, first[0] + tile_index]
    last_start = bounds[2, first[0] + tile_index]
    q_first = halo_rows + place
    lowest = first_start // UNIT * UNIT
    units = (q_first - lowest) // UNIT
    sums[...] = jnp.zeros_like(sums)
    inner = 1.0 / (math.sqrt(HEAD_DIM) * LOGIT_CAP)
    outer = LOGIT_CAP * math.log2(math.e)
    rows_at = q_first + lax.broadcasted_iota(jnp.int32, (tile, UNIT), 0)
    starts = jnp.zeros((tile, UNIT), jnp.int32)
    for number in range(ends.shape[0]):
        starts = jnp.where(rows_at >= ends[number], jnp.maximum(starts, ends[number]), starts)
    begins[...] = starts

    def block_step(begin, size, masked):
        rows = pl.ds(pl.multiple_of(begin, UNIT), size)
        if masked:
            parts = []
            for part in range(size // UNIT):
                k_ids = begin + part * UNIT + lax.broadcasted_iota(jnp.int32, (tile, UNIT), 1)
                q_ids = q_first + lax.broadcasted_iota(jnp.int32, (tile, UNIT), 0)
                parts.append((k_ids <= q_ids) & (k_ids >= begins[...]))
            allowed = parts[0] if len(parts) == 1 else jnp.concatenate(parts, axis=1)
        for kv_head in range(kv_heads):
            keys = k_all[rows, kv_head * HEAD_DIM : (kv_head + 1) * HEAD_DIM]
            values = v_all[rows, kv_head * wide : (kv_head + 1) * wide]
            pairs = 2 if share % 2 == 0 else 1
            count = share // pairs
            for pair in range(pairs):
                at = (kv_head * share + pair * count) * tile
                members = slice(at, at + count * tile)
                raw = lax.dot_general(
                    q_all[members, :], keys, (((1,), (1,)), ((), ())), preferred_element_type=jnp.float32
                )
                weights = jnp.exp2(outer * jnp.tanh(raw * inner))
                if masked:
                    weights = weights.reshape(count, tile, size)
                    weights = jnp.where(allowed[None], weights, 0.0).reshape(count * tile, size)
                sums[members, :] += jnp.dot(weights.astype(jnp.bfloat16), values, preferred_element_type=jnp.float32)

    def either(begin, size):
        whole = (begin >= last_start) & (begin + size - 1 <= q_first)

        @pl.when(whole)
        def _():
            block_step(begin, size, False)

        @pl.when(jnp.logical_not(whole))
        def _():
            block_step(begin, size, True)

    def long_step(number, carry):
        either(q_first - 4 * UNIT * (number + 1), 4 * UNIT)
        return carry

    block_step(q_first, tile, True)
    lax.fori_loop(0, units // 4, long_step, 0)
    rest = lax.rem(units, 4)

    @pl.when(rest >= 2)
    def _():
        either(lowest + lax.rem(rest, 2) * UNIT, 2 * UNIT)

    @pl.when(lax.rem(rest, 2) == 1)
    def _():
        either(lowest, UNIT)

    for head in range(kv_heads * share):
        rows = slice(head * tile, (head + 1) * tile)
        mixed = sums[rows, :HEAD_DIM] / sums[rows, HEAD_DIM:]
        out_ref[:, head * HEAD_DIM : (head + 1) * HEAD_DIM] = mixed.astype(out_ref.dtype)


def attend(chunk, chunk_rows, query, ends, bounds, halo, kv, kv_heads):
    width = query.shape[1]
    heads = width // HEAD_DIM
    halo_rows = halo.shape[0]
    tiles = chunk_rows // TILE
    first = (chunk * tiles).reshape(1).astype(jnp.int32)
    kernel = functools.partial(attend_kernel, kv_heads, heads // kv_heads, halo_rows, chunk_rows)
    return pl.pallas_call(
        kernel,
        out_shape=jax.ShapeDtypeStruct((chunk_rows, width), jnp.bfloat16),
        grid_spec=pltpu.PrefetchScalarGridSpec(
            num_scalar_prefetch=3,
            grid=(tiles,),
            in_specs=[
                pl.BlockSpec((TILE, width), lambda i, c, s, e: (c[0] + i, 0)),
                pl.BlockSpec(halo.shape, lambda i, c, s, e: (0, 0)),
                pl.BlockSpec(kv.shape, lambda i, c, s, e: (0, 0)),
            ],
            out_specs=pl.BlockSpec((TILE, width), lambda i, c, s, e: (i, 0)),
            scratch_shapes=[
                pltpu.VMEM((halo_rows + kv.shape[0], kv_heads * HEAD_DIM), jnp.bfloat16),
                pltpu.VMEM((halo_rows + kv.shape[0], kv_heads * 2 * HEAD_DIM), jnp.bfloat16),
                pltpu.VMEM((heads * TILE, HEAD_DIM), jnp.bfloat16),
                pltpu.VMEM((heads * TILE, 2 * HEAD_DIM), jnp.float32),
                pltpu.VMEM((TILE, UNIT), jnp.int32),
            ],
        ),
        compiler_params=pltpu.CompilerParams(vmem_limit_bytes=VMEM_BYTES),
        cost_estimate=pl.CostEstimate(
            flops=4 * chunk_rows * width * (halo_rows + chunk_rows) // 2,
            bytes_accessed=4 * chunk_rows * width,
            transcendentals=chunk_rows * heads * (halo_rows + chunk_rows),
        ),
    )(first, bounds, ends, query, halo, kv)


def copied_kernel(block_ref, other_ref, out_ref):
    out_ref[...] = block_ref[...]


def copied_after(block, other):
    return pl.pallas_call(
        copied_kernel,
        out_shape=jax.ShapeDtypeStruct(block.shape, block.dtype),
        in_specs=[pl.BlockSpec(memory_space=pltpu.VMEM), pl.BlockSpec(memory_space=pl.ANY)],
        out_specs=pl.BlockSpec(memory_space=pltpu.VMEM),
        compiler_params=pltpu.CompilerParams(vmem_limit_bytes=PUT_BYTES),
    )(block, other)


def pick_kernel(which, block_ref, out_ref):
    out_ref[...] = block_ref[...]


def pick(which, rows, array):
    return pl.pallas_call(
        pick_kernel,
        out_shape=jax.ShapeDtypeStruct((rows, array.shape[1]), array.dtype),
        grid_spec=pltpu.PrefetchScalarGridSpec(
            num_scalar_prefetch=1,
            grid=(4,),
            in_specs=[pl.BlockSpec((rows // 4, array.shape[1]), lambda i, s: (4 * s[0] + i, 0))],
            out_specs=pl.BlockSpec((rows // 4, array.shape[1]), lambda i, s: (i, 0)),
        ),
    )(which.reshape(1).astype(jnp.int32), array)


def after(block, *others):
    space = pl.BlockSpec(memory_space=pl.ANY)
    return pl.pallas_call(
        lambda *refs: None,
        out_shape=jax.ShapeDtypeStruct(block.shape, block.dtype),
        in_specs=[space] * (1 + len(others)),
        out_specs=space,
        input_output_aliases={0: 0},
    )(block, *others)


def per_device(group, lines, cores, tokens, lengths, w_query, w_key, w_value):
    row_count, depth = tokens.shape
    slice_rows = w_query.shape[0]
    index = lax.axis_index("ca")
    mine, line = index % group, index // group
    core = lax.axis_index("tp")
    q_width = w_query.shape[1] // group
    one_width = w_key.shape[1] // group
    kv_width = 2 * one_width
    kv_heads = one_width // HEAD_DIM
    group_rows = group * row_count
    devices = range(group * lines)

    def slice_for(target):
        return jnp.concatenate(
            [
                lax.dynamic_slice_in_dim(w_query, target * q_width, q_width, 1),
                lax.dynamic_slice_in_dim(w_key, target * one_width, one_width, 1),
                lax.dynamic_slice_in_dim(w_value, target * one_width, one_width, 1),
            ],
            axis=1,
        )

    def to_partner(block, step):
        return lax.ppermute(block, "ca", [(i, i ^ step) for i in devices])

    def along_lines(block):
        lanes = [[place + group * i for i in range(lines)] for place in range(group)]
        return lax.all_gather(block, "ca", axis=0, tiled=True, axis_index_groups=lanes)

    def forwarded(block):
        return lax.ppermute(block, "ca", [(i, (i + group) % (group * lines)) for i in devices])

    def gathered(array, block, column, members):
        if group == 1:
            return (array, block, column, [(0, array.shape[0], lambda s: 0)])
        pieces = []
        for at in range(lines):
            for number, step in enumerate(members):
                source = (at * len(members) + number) * slice_rows
                pieces.append((source, slice_rows, lambda s, at=at, step=step: (at * group + (s[0] ^ step)) * slice_rows))
        return (array, block, column, pieces)

    def from_lines(held, column, members):
        entries = []
        for back, array in enumerate(held):
            pieces = []
            for number, step in enumerate(members):

                def target(s, back=back, step=step):
                    at = lax.rem(s[1] - back + lines, lines)
                    return (at * group + (s[0] ^ step)) * slice_rows

                pieces.append((number * slice_rows, slice_rows, target))
            entries.append((array, (0, array.shape[1]), column, pieces))
        return entries

    half = row_count // 2
    halo_rows = REACH * row_count
    tiles = row_count // TILE

    def tables():
        row_ids = line * group_rows + jnp.arange(group_rows, dtype=jnp.int32)
        starts = doc_starts(lengths, row_ids)
        window_starts = starts - (line * group_rows - halo_rows)
        places = jnp.arange(group * tiles, dtype=jnp.int32) * TILE
        first = window_starts.reshape(group * tiles, TILE)
        bounds = jnp.stack([places, first[:, 0], first[:, -1]])
        cosine, sine = rope_tables(row_ids - starts)
        ends = jnp.cumsum(lengths).astype(jnp.int32) - (line * group_rows - halo_rows)
        return cosine, sine, ends, bounds

    place = jnp.stack([mine, line, core]).astype(jnp.int32)
    if group > 1:
        slices = [slice_for(mine)] + [to_partner(slice_for(mine ^ step), step) for step in range(1, group)]
        own_slices = along_lines(slices[0])
        rest_q = along_lines(jnp.concatenate([a[:, :q_width] for a in slices[1:]]))
        rest_kv = jnp.concatenate([a[:, q_width:] for a in slices[1:]])
        both = ("ca", "tp")

        def cross(block, steps):
            pairs = [(i * 2 + c, (i ^ steps[c]) * 2 + c) for i in devices for c in range(2)]
            return lax.ppermute(block, both, pairs)

        def swap(block):
            return lax.ppermute(block, both, [(i * 2 + c, i * 2 + 1 - c) for i in devices for c in range(2)])


        own_half = pick(core, half, tokens)

        def home(step_even, step_odd, mate):
            def target(s):
                step = jnp.where(s[2] == mate, step_even, step_odd)
                return (s[0] ^ step) * row_count + jnp.where(mate == 0, s[2], 1 - s[2]) * half

            return target


        near = cross(own_half, (1, 2))
        other = cross(own_half, (2, 1))

        def prepare(tokens, rest_kv):
            held = [rest_kv]
            for _ in range(1, lines - 1):
                held.append(forwarded(held[-1]))
            return put(place, group_rows, [(tokens, lambda s: s[0] * row_count)]), tables(), tuple(held[1:])

        def share(everything, near, other):
            far = cross(near, (2, 1))
            mates = [swap(block) for block in (near, other)]
            first = [(near, home(1, 2, 0)), (mates[0], home(1, 2, 1)), (other, home(2, 1, 0)), (mates[1], home(2, 1, 1))]
            everything = put(place, group_rows, first, everything)
            far = copied_after(far, everything)
            last = [(far, home(3, 3, 0)), (swap(far), home(3, 3, 1))]
            return put(place, group_rows, last, everything)

        def region(body, flag, *operands):
            def nothing(*operands):
                shapes = jax.eval_shape(body, *operands)
                return jax.tree.map(lambda leaf: jnp.zeros(leaf.shape, leaf.dtype), shapes)

            known = flag.reshape(-1)[0].astype(jnp.float32)
            return lax.cond(known == known, body, nothing, *operands)

        all_tokens, known_tables, held = prepare(tokens, rest_kv)
        held = (*held, forwarded(held[-1]))
        near = after(near, held[1], *known_tables)
        all_tokens = region(share, rest_kv[:1, :1], all_tokens, near, other)
        others = range(1, group)
        kv_weights = [gathered(own_slices, (q_width // kv_width, kv_width), 0, [0])]
        kv_weights += from_lines((rest_kv, *held), 0, others)
        q_weights = [gathered(own_slices, (0, q_width), 0, [0]), gathered(rest_q, (0, q_width), 0, others)]
    else:
        all_tokens, known_tables = tokens, tables()
        own = along_lines(slice_for(mine))
        kv_weights = [gathered(own, (q_width // kv_width, kv_width), 0, [0])]
        q_weights = [gathered(own, (0, q_width), 0, [0])]
    cosine, sine, ends, bounds = known_tables

    kv = project(group, place, all_tokens, kv_weights, kv_width, cosine, sine, kv_heads, (0, group))
    hops = -(-halo_rows // group_rows)
    pieces, moving = [], kv
    for hop in range(hops):
        keep = min(halo_rows - hop * group_rows, group_rows)
        moving = moving[moving.shape[0] - keep :]
        moving = lax.ppermute(moving, "ca", [(i, i + group) for i in devices if i + group in devices])
        pieces.insert(0, moving)
    halo = pieces[0] if len(pieces) == 1 else jnp.concatenate(pieces)

    query = project(group, place, all_tokens, q_weights, q_width, cosine, sine, q_width // HEAD_DIM, (0, group))
    result = jnp.zeros((row_count, w_query.shape[1]), jnp.bfloat16)
    for step in reversed(range(group)):
        part = attend(mine ^ step, row_count, query, ends, bounds, halo, kv, kv_heads)
        if step > 0:
            part = to_partner(part, step)
        elif group == 1:
            return part
        result = lax.dynamic_update_slice_in_dim(result, part, (mine ^ step) * q_width, 1)
    return result


def solution(mesh):
    size, cores = mesh.shape["ca"], mesh.shape["tp"]
    local_kv = KV_HEADS // cores
    group = 4 if cores == 2 and local_kv == 4 and size % 4 == 0 else 1
    placed = (P("ca", None), P(), P("ca", "tp"), P("ca", "tp"), P("ca", "tp"))
    body = functools.partial(per_device, group, size // group, cores)
    return jax.shard_map(body, mesh=mesh, in_specs=placed, out_specs=P("ca", "tp"), check_vma=False)
```

```python
import functools
import math

import jax
import jax.numpy as jnp
from jax import lax
from jax.experimental import pallas as pl
from jax.experimental.pallas import tpu as pltpu
from jax.sharding import PartitionSpec as P

HEADS = 32
KV_HEADS = 8
HEAD_DIM = 128
REACH = 3
ROPE_THETA = 500000.0
LOGIT_CAP = 5.0
TILE = 256
UNIT = 128
PUT_BYTES = 20 * 1024 * 1024
PROJECT_BYTES = 58 * 1024 * 1024
VMEM_BYTES = 58 * 1024 * 1024


def doc_starts(lengths, positions):
    doc_ends = jnp.cumsum(lengths).astype(jnp.int32)
    before = doc_ends[None, :] <= positions[:, None]
    return jnp.max(jnp.where(before, doc_ends[None, :], 0), axis=1).astype(jnp.int32)


def rope_tables(offsets):
    half_dim = HEAD_DIM // 2
    frequency = ROPE_THETA ** (-(jnp.arange(half_dim, dtype=jnp.float32) * 2.0) / HEAD_DIM)
    angles = offsets.astype(jnp.float32)[:, None] * frequency[None, :]
    cosine, sine = jnp.cos(angles), jnp.sin(angles)
    return jnp.concatenate([cosine, cosine], axis=1), jnp.concatenate([-sine, sine], axis=1)


def rotated(values, cosine, sine):
    return values * cosine + pltpu.roll(values, HEAD_DIM // 2, 1) * sine


def project_kernel(rope_heads, layout, given, place, x_ref, *refs):
    w_refs = refs[: len(layout)]
    cos_ref, sin_ref = refs[len(layout) : len(layout) + 2]
    out_ref, w_all = refs[len(layout) + 2 + given :]

    @pl.when(pl.program_id(0) == 0)
    def _():
        for ref, (_, column, pieces) in zip(w_refs, layout):
            columns = slice(column, column + ref.shape[1])
            for source, rows, target in pieces:
                at = pl.multiple_of(target(place), rows)
                w_all[pl.ds(at, rows), columns] = ref[source : source + rows, :]

    total = jnp.dot(x_ref[...], w_all[...], preferred_element_type=jnp.float32)
    cosine, sine = cos_ref[...], sin_ref[...]
    for head in range(out_ref.shape[1] // HEAD_DIM):
        columns = slice(head * HEAD_DIM, (head + 1) * HEAD_DIM)
        part = total[:, columns]
        if head < rope_heads:
            part = rotated(part, cosine, sine)
        out_ref[:, columns] = part.astype(out_ref.dtype)


def project(group, place, tokens, weights, width, cosine, sine, rope_heads, span, into=None):
    rows, depth = tokens.shape
    first, count = span
    tile = rows // group
    arrays, blocks, layout = [], [], []
    for array, (block, columns), column, pieces in weights:
        arrays.append(array)
        blocks.append(pl.BlockSpec((array.shape[0], columns), lambda i, s, block=block: (0, block)))
        layout.append((None, column, pieces))

    def row_block(i, s):
        return (s[0] ^ (first + i), 0)

    given = [] if into is None else [into]
    return pl.pallas_call(
        functools.partial(project_kernel, rope_heads, layout, len(given)),
        out_shape=jax.ShapeDtypeStruct((rows, width), jnp.bfloat16),
        grid_spec=pltpu.PrefetchScalarGridSpec(
            num_scalar_prefetch=1,
            grid=(count,),
            in_specs=[pl.BlockSpec((tile, depth), row_block)]
            + blocks
            + [pl.BlockSpec((tile, HEAD_DIM), row_block)] * 2
            + [pl.BlockSpec(memory_space=pl.ANY)] * len(given),
            out_specs=pl.BlockSpec((tile, width), row_block),
            scratch_shapes=[pltpu.VMEM((depth, width), tokens.dtype)],
        ),
        input_output_aliases={} if into is None else {4 + len(arrays): 0},
        compiler_params=pltpu.CompilerParams(vmem_limit_bytes=PROJECT_BYTES),
        cost_estimate=pl.CostEstimate(
            flops=2 * count * tile * depth * width,
            bytes_accessed=2 * depth * (count * tile + width),
            transcendentals=0,
        ),
    )(place, tokens, *arrays, cosine, sine, *given)


def put_kernel(targets, place, *refs):
    sems, out_ref = refs[-1], refs[-2]
    copies = []
    for number, (ref, target) in enumerate(zip(refs, targets)):
        rows = ref.shape[0]
        at = pl.multiple_of(target(place), rows)
        copies.append(pltpu.make_async_copy(ref, out_ref.at[pl.ds(at, rows), :], sems.at[number]))
        copies[-1].start()
    for copy in copies:
        copy.wait()


def put(place, rows, blocks, into=None):
    arrays, targets = [block for block, _ in blocks], [target for _, target in blocks]
    spaces = [pl.BlockSpec(memory_space=pltpu.SMEM)] + [pl.BlockSpec(memory_space=pltpu.VMEM)] * len(arrays)
    aliases = {}
    if into is not None:
        aliases = {1 + len(arrays): 0}
        arrays.append(into)
        spaces.append(pl.BlockSpec(memory_space=pl.ANY))
    return pl.pallas_call(
        functools.partial(put_kernel, targets),
        out_shape=jax.ShapeDtypeStruct((rows, arrays[0].shape[1]), arrays[0].dtype),
        in_specs=spaces,
        out_specs=pl.BlockSpec(memory_space=pl.ANY),
        scratch_shapes=[pltpu.SemaphoreType.DMA((len(targets),))],
        input_output_aliases=aliases,
        compiler_params=pltpu.CompilerParams(vmem_limit_bytes=PUT_BYTES),
        cost_estimate=pl.CostEstimate(
            flops=0, bytes_accessed=sum(4 * block.size for block, _ in blocks), transcendentals=0
        ),
    )(place, *arrays)


def attend_kernel(kv_heads, share, halo_rows, chunk, first, bounds, ends, q_ref, halo_ref, kv_ref, out_ref, k_all, v_all, q_all, sums, begins):
    tile_index = pl.program_id(0)
    wide = 2 * HEAD_DIM

    @pl.when(tile_index == 0)
    def _():
        for source, start in ((halo_ref, 0), (kv_ref, halo_rows)):
            for number in range(source.shape[0] // chunk):
                here = slice(number * chunk, (number + 1) * chunk)
                rows = slice(start + number * chunk, start + (number + 1) * chunk)
                back = halo_rows + bounds[0, first[0]] - rows.start

                @pl.when((back >= 0) & (back <= halo_rows))
                def _(source=source, here=here, rows=rows):
                    for head in range(kv_heads):
                        columns = slice(head * HEAD_DIM, (head + 1) * HEAD_DIM)
                        at = (kv_heads + head) * HEAD_DIM
                        k_all[rows, columns] = source[here, columns]
                        v_all[rows, head * wide : head * wide + HEAD_DIM] = source[here, at : at + HEAD_DIM]
                        v_all[rows, head * wide + HEAD_DIM : (head + 1) * wide] = jnp.ones(
                            (chunk, HEAD_DIM), v_all.dtype
                        )

    tile = q_ref.shape[0]
    for head in range(kv_heads * share):
        q_all[head * tile : (head + 1) * tile, :] = q_ref[:, head * HEAD_DIM : (head + 1) * HEAD_DIM]
    place = bounds[0, first[0] + tile_index]
    first_start = bounds[1, first[0] + tile_index]
    last_start = bounds[2, first[0] + tile_index]
    q_first = halo_rows + place
    lowest = first_start // UNIT * UNIT
    units = (q_first - lowest) // UNIT
    sums[...] = jnp.zeros_like(sums)
    inner = 1.0 / (math.sqrt(HEAD_DIM) * LOGIT_CAP)
    outer = LOGIT_CAP * math.log2(math.e)
    rows_at = q_first + lax.broadcasted_iota(jnp.int32, (tile, UNIT), 0)
    starts = jnp.zeros((tile, UNIT), jnp.int32)
    for number in range(ends.shape[0]):
        starts = jnp.where(rows_at >= ends[number], jnp.maximum(starts, ends[number]), starts)
    begins[...] = starts

    def block_step(begin, size, masked):
        rows = pl.ds(pl.multiple_of(begin, UNIT), size)
        if masked:
            parts = []
            for part in range(size // UNIT):
                k_ids = begin + part * UNIT + lax.broadcasted_iota(jnp.int32, (tile, UNIT), 1)
                q_ids = q_first + lax.broadcasted_iota(jnp.int32, (tile, UNIT), 0)
                parts.append((k_ids <= q_ids) & (k_ids >= begins[...]))
            allowed = parts[0] if len(parts) == 1 else jnp.concatenate(parts, axis=1)
        for kv_head in range(kv_heads):
            keys = k_all[rows, kv_head * HEAD_DIM : (kv_head + 1) * HEAD_DIM]
            values = v_all[rows, kv_head * wide : (kv_head + 1) * wide]
            members = slice(kv_head * share * tile, (kv_head + 1) * share * tile)
            raw = lax.dot_general(
                q_all[members, :], keys, (((1,), (1,)), ((), ())), preferred_element_type=jnp.float32
            )
            growth = jnp.exp2(jnp.minimum(raw * (2.0 * inner * math.log2(math.e)), 126.0))
            weights = jnp.exp2(outer - (2.0 * outer) / (1.0 + growth))
            if masked:
                weights = weights.reshape(share, tile, size)
                weights = jnp.where(allowed[None], weights, 0.0).reshape(share * tile, size)
            sums[members, :] += jnp.dot(weights.astype(jnp.bfloat16), values, preferred_element_type=jnp.float32)

    def either(begin, size):
        whole = (begin >= last_start) & (begin + size - 1 <= q_first)

        @pl.when(whole)
        def _():
            block_step(begin, size, False)

        @pl.when(jnp.logical_not(whole))
        def _():
            block_step(begin, size, True)

    def long_step(number, carry):
        either(q_first - 4 * UNIT * (number + 1), 4 * UNIT)
        return carry

    block_step(q_first, tile, True)
    lax.fori_loop(0, units // 4, long_step, 0)
    rest = lax.rem(units, 4)

    @pl.when(rest >= 2)
    def _():
        either(lowest + lax.rem(rest, 2) * UNIT, 2 * UNIT)

    @pl.when(lax.rem(rest, 2) == 1)
    def _():
        either(lowest, UNIT)

    for head in range(kv_heads * share):
        rows = slice(head * tile, (head + 1) * tile)
        mixed = sums[rows, :HEAD_DIM] / sums[rows, HEAD_DIM:]
        out_ref[:, head * HEAD_DIM : (head + 1) * HEAD_DIM] = mixed.astype(out_ref.dtype)


def attend(chunk, chunk_rows, query, ends, bounds, halo, kv, kv_heads):
    width = query.shape[1]
    heads = width // HEAD_DIM
    halo_rows = halo.shape[0]
    tiles = chunk_rows // TILE
    first = (chunk * tiles).reshape(1).astype(jnp.int32)
    kernel = functools.partial(attend_kernel, kv_heads, heads // kv_heads, halo_rows, chunk_rows)
    return pl.pallas_call(
        kernel,
        out_shape=jax.ShapeDtypeStruct((chunk_rows, width), jnp.bfloat16),
        grid_spec=pltpu.PrefetchScalarGridSpec(
            num_scalar_prefetch=3,
            grid=(tiles,),
            in_specs=[
                pl.BlockSpec((TILE, width), lambda i, c, s, e: (c[0] + i, 0)),
                pl.BlockSpec(halo.shape, lambda i, c, s, e: (0, 0)),
                pl.BlockSpec(kv.shape, lambda i, c, s, e: (0, 0)),
            ],
            out_specs=pl.BlockSpec((TILE, width), lambda i, c, s, e: (i, 0)),
            scratch_shapes=[
                pltpu.VMEM((halo_rows + kv.shape[0], kv_heads * HEAD_DIM), jnp.bfloat16),
                pltpu.VMEM((halo_rows + kv.shape[0], kv_heads * 2 * HEAD_DIM), jnp.bfloat16),
                pltpu.VMEM((heads * TILE, HEAD_DIM), jnp.bfloat16),
                pltpu.VMEM((heads * TILE, 2 * HEAD_DIM), jnp.float32),
                pltpu.VMEM((TILE, UNIT), jnp.int32),
            ],
        ),
        compiler_params=pltpu.CompilerParams(vmem_limit_bytes=VMEM_BYTES),
        cost_estimate=pl.CostEstimate(
            flops=4 * chunk_rows * width * (halo_rows + chunk_rows) // 2,
            bytes_accessed=4 * chunk_rows * width,
            transcendentals=chunk_rows * heads * (halo_rows + chunk_rows),
        ),
    )(first, bounds, ends, query, halo, kv)


def copied_kernel(block_ref, other_ref, out_ref):
    out_ref[...] = block_ref[...]


def copied_after(block, other):
    return pl.pallas_call(
        copied_kernel,
        out_shape=jax.ShapeDtypeStruct(block.shape, block.dtype),
        in_specs=[pl.BlockSpec(memory_space=pltpu.VMEM), pl.BlockSpec(memory_space=pl.ANY)],
        out_specs=pl.BlockSpec(memory_space=pltpu.VMEM),
        compiler_params=pltpu.CompilerParams(vmem_limit_bytes=PUT_BYTES),
    )(block, other)


def pick_kernel(which, block_ref, out_ref):
    out_ref[...] = block_ref[...]


def pick(which, rows, array):
    return pl.pallas_call(
        pick_kernel,
        out_shape=jax.ShapeDtypeStruct((rows, array.shape[1]), array.dtype),
        grid_spec=pltpu.PrefetchScalarGridSpec(
            num_scalar_prefetch=1,
            grid=(4,),
            in_specs=[pl.BlockSpec((rows // 4, array.shape[1]), lambda i, s: (4 * s[0] + i, 0))],
            out_specs=pl.BlockSpec((rows // 4, array.shape[1]), lambda i, s: (i, 0)),
        ),
    )(which.reshape(1).astype(jnp.int32), array)


def after(block, *others):
    space = pl.BlockSpec(memory_space=pl.ANY)
    return pl.pallas_call(
        lambda *refs: None,
        out_shape=jax.ShapeDtypeStruct(block.shape, block.dtype),
        in_specs=[space] * (1 + len(others)),
        out_specs=space,
        input_output_aliases={0: 0},
    )(block, *others)


def per_device(group, lines, cores, tokens, lengths, w_query, w_key, w_value):
    row_count, depth = tokens.shape
    slice_rows = w_query.shape[0]
    index = lax.axis_index("ca")
    mine, line = index % group, index // group
    core = lax.axis_index("tp")
    q_width = w_query.shape[1] // group
    one_width = w_key.shape[1] // group
    kv_width = 2 * one_width
    kv_heads = one_width // HEAD_DIM
    group_rows = group * row_count
    devices = range(group * lines)

    def slice_for(target):
        return jnp.concatenate(
            [
                lax.dynamic_slice_in_dim(w_query, target * q_width, q_width, 1),
                lax.dynamic_slice_in_dim(w_key, target * one_width, one_width, 1),
                lax.dynamic_slice_in_dim(w_value, target * one_width, one_width, 1),
            ],
            axis=1,
        )

    def to_partner(block, step):
        return lax.ppermute(block, "ca", [(i, i ^ step) for i in devices])

    def along_lines(block):
        lanes = [[place + group * i for i in range(lines)] for place in range(group)]
        return lax.all_gather(block, "ca", axis=0, tiled=True, axis_index_groups=lanes)

    def forwarded(block):
        return lax.ppermute(block, "ca", [(i, (i + group) % (group * lines)) for i in devices])

    def gathered(array, block, column, members):
        if group == 1:
            return (array, block, column, [(0, array.shape[0], lambda s: 0)])
        pieces = []
        for at in range(lines):
            for number, step in enumerate(members):
                source = (at * len(members) + number) * slice_rows
                pieces.append((source, slice_rows, lambda s, at=at, step=step: (at * group + (s[0] ^ step)) * slice_rows))
        return (array, block, column, pieces)

    def from_lines(held, column, members):
        entries = []
        for back, array in enumerate(held):
            pieces = []
            for number, step in enumerate(members):

                def target(s, back=back, step=step):
                    at = lax.rem(s[1] - back + lines, lines)
                    return (at * group + (s[0] ^ step)) * slice_rows

                pieces.append((number * slice_rows, slice_rows, target))
            entries.append((array, (0, array.shape[1]), column, pieces))
        return entries

    half = row_count // 2
    halo_rows = REACH * row_count
    tiles = row_count // TILE

    def tables():
        row_ids = line * group_rows + jnp.arange(group_rows, dtype=jnp.int32)
        starts = doc_starts(lengths, row_ids)
        window_starts = starts - (line * group_rows - halo_rows)
        places = jnp.arange(group * tiles, dtype=jnp.int32) * TILE
        first = window_starts.reshape(group * tiles, TILE)
        bounds = jnp.stack([places, first[:, 0], first[:, -1]])
        cosine, sine = rope_tables(row_ids - starts)
        ends = jnp.cumsum(lengths).astype(jnp.int32) - (line * group_rows - halo_rows)
        return cosine, sine, ends, bounds

    place = jnp.stack([mine, line, core]).astype(jnp.int32)
    if group > 1:
        slices = [slice_for(mine)] + [to_partner(slice_for(mine ^ step), step) for step in range(1, group)]
        own_slices = along_lines(slices[0])
        rest_q = along_lines(jnp.concatenate([a[:, :q_width] for a in slices[1:]]))
        rest_kv = jnp.concatenate([a[:, q_width:] for a in slices[1:]])
        both = ("ca", "tp")

        def cross(block, steps):
            pairs = [(i * 2 + c, (i ^ steps[c]) * 2 + c) for i in devices for c in range(2)]
            return lax.ppermute(block, both, pairs)

        def swap(block):
            return lax.ppermute(block, both, [(i * 2 + c, i * 2 + 1 - c) for i in devices for c in range(2)])


        own_half = pick(core, half, tokens)

        def home(step_even, step_odd, mate):
            def target(s):
                step = jnp.where(s[2] == mate, step_even, step_odd)
                return (s[0] ^ step) * row_count + jnp.where(mate == 0, s[2], 1 - s[2]) * half

            return target


        near = cross(own_half, (1, 2))
        other = cross(own_half, (2, 1))

        def prepare(tokens, rest_kv):
            held = [rest_kv]
            for _ in range(1, lines - 1):
                held.append(forwarded(held[-1]))
            return put(place, group_rows, [(tokens, lambda s: s[0] * row_count)]), tables(), tuple(held[1:])

        def share(everything, near, other):
            far = cross(near, (2, 1))
            mates = [swap(block) for block in (near, other)]
            first = [(near, home(1, 2, 0)), (mates[0], home(1, 2, 1)), (other, home(2, 1, 0)), (mates[1], home(2, 1, 1))]
            everything = put(place, group_rows, first, everything)
            far = copied_after(far, everything)
            last = [(far, home(3, 3, 0)), (swap(far), home(3, 3, 1))]
            return put(place, group_rows, last, everything)

        def region(body, flag, *operands):
            def nothing(*operands):
                shapes = jax.eval_shape(body, *operands)
                return jax.tree.map(lambda leaf: jnp.zeros(leaf.shape, leaf.dtype), shapes)

            known = flag.reshape(-1)[0].astype(jnp.float32)
            return lax.cond(known == known, body, nothing, *operands)

        all_tokens, known_tables, held = prepare(tokens, rest_kv)
        held = (*held, forwarded(held[-1]))
        near = after(near, held[1], *known_tables)
        all_tokens = region(share, rest_kv[:1, :1], all_tokens, near, other)
        others = range(1, group)
        kv_weights = [gathered(own_slices, (q_width // kv_width, kv_width), 0, [0])]
        kv_weights += from_lines((rest_kv, *held), 0, others)
        q_weights = [gathered(own_slices, (0, q_width), 0, [0]), gathered(rest_q, (0, q_width), 0, others)]
    else:
        all_tokens, known_tables = tokens, tables()
        own = along_lines(slice_for(mine))
        kv_weights = [gathered(own, (q_width // kv_width, kv_width), 0, [0])]
        q_weights = [gathered(own, (0, q_width), 0, [0])]
    cosine, sine, ends, bounds = known_tables

    kv = project(group, place, all_tokens, kv_weights, kv_width, cosine, sine, kv_heads, (0, group))
    hops = -(-halo_rows // group_rows)
    pieces, moving = [], kv
    for hop in range(hops):
        keep = min(halo_rows - hop * group_rows, group_rows)
        moving = moving[moving.shape[0] - keep :]
        moving = lax.ppermute(moving, "ca", [(i, i + group) for i in devices if i + group in devices])
        pieces.insert(0, moving)
    halo = pieces[0] if len(pieces) == 1 else jnp.concatenate(pieces)

    query = project(group, place, all_tokens, q_weights, q_width, cosine, sine, q_width // HEAD_DIM, (0, group))
    result = jnp.zeros((row_count, w_query.shape[1]), jnp.bfloat16)
    for step in reversed(range(group)):
        part = attend(mine ^ step, row_count, query, ends, bounds, halo, kv, kv_heads)
        if step > 0:
            part = to_partner(part, step)
        elif group == 1:
            return part
        result = lax.dynamic_update_slice_in_dim(result, part, (mine ^ step) * q_width, 1)
    return result


def solution(mesh):
    size, cores = mesh.shape["ca"], mesh.shape["tp"]
    local_kv = KV_HEADS // cores
    group = 4 if cores == 2 and local_kv == 4 and size % 4 == 0 else 1
    placed = (P("ca", None), P(), P("ca", "tp"), P("ca", "tp"), P("ca", "tp"))
    body = functools.partial(per_device, group, size // group, cores)
    return jax.shard_map(body, mesh=mesh, in_specs=placed, out_specs=P("ca", "tp"), check_vma=False)
```
